256 devices in a mesh: ctx: 64 (over y, z, core), head: 4 (over x).
Axes of the slice: x: 4, y: 4, z: 8, core: 2. Of those that a mesh axis runs over, the one named last changes fastest.
Arguments:
- queries: bfloat16 [65536, 512], P('ctx', 'head'), may hold values from -18 to 18
- key_states: bfloat16 [65536, 512], P('ctx', 'head'), may hold values from -6 to 6
- value_states: bfloat16 [65536, 512], P('ctx', 'head'), may hold values from -6 to 6
- clip_lengths: int32 [8], replicated, may hold values from 1 to 128, 512 in all
- out_weight: bfloat16 [512, 6144], P(None, 'head'), may hold values from -0.25 to 0.25
Outputs:
- projected: bfloat16 [65536, 6144], P('ctx', 'head')
The draws below stay inside these ranges and needn't reach their ends.
Inputs may be any that keep to these rules, and one draw needn't show every extreme that they name: clip_lengths[c] counts the 128-token blocks of clip c; the clips lie end to end and fill all 512 blocks; the longest has exactly 128 blocks.
All inputs are finite; a program needn't handle non-finite values.
Results may differ from the reference program's by a relative error of at most 0.015.
Values may be sent and summed in bfloat16 or wider, within the bound.
No kernel may reach another device: no remote copies, remote signals or barrier semaphores. Data moves between devices by JAX's collectives and lax.ppermute only.
A program may use at most 128 MiB of HBM per device.

```python
import math
import jax
import jax.numpy as jnp
import numpy as np
from jax import lax

DMODEL = 6144
HEAD_DIM = 128
HEADS = 4
BLOCK = 128
TOK_DEV = 1024
CLIP_DEVS = 16
TOKENS = 65536
BLOCKS_ALL = 512
CLIP_BLOCKS = 128
CLIPS = 8
N_CTX = 64


def draw_queries(key, part):
    key = jax.random.fold_in(key, 1)
    drawn = jnp.clip(jax.random.normal(key, (TOKENS, HEADS * HEAD_DIM), jnp.float32), -6.0, 6.0)
    return drawn.astype(jnp.bfloat16)


def draw_key_states(key, part):
    key = jax.random.fold_in(key, 2)
    drawn = jnp.clip(jax.random.normal(key, (TOKENS, HEADS * HEAD_DIM), jnp.float32), -6.0, 6.0)
    return drawn.astype(jnp.bfloat16)


def block_levels(own_key, extent, cuts, smallest, high):
    level, own = 1.0, jax.random.fold_in(own_key, 6)
    for dim, blocks in cuts:
        heights = jnp.exp(jax.random.uniform(jax.random.fold_in(own, dim), (blocks,), jnp.float32, smallest / len(cuts), high / len(cuts)))
        level = level * jnp.repeat(heights, extent[dim] // blocks).reshape([-1 if axis == dim else 1 for axis in range(len(extent))])
    return level


def profile(amount, total, reach, lean):
    loads = [(1 << 20) // math.isqrt(standing ** lean) + 1 for standing in range(2, amount + 1)]
    spare, holding = total - reach - (amount - 1), [1] * (amount - 1)
    while spare > 0:
        movable = [i for i in range(amount - 1) if holding[i] < reach]
        pool, budget = sum([loads[i] for i in movable]), spare
        for i in movable:
            more = min(reach - holding[i], max(1, budget * loads[i] // pool), spare)
            holding[i] = holding[i] + more
            spare = spare - more
    return np.array([reach] + holding)


def ragged(key, amount, total, most, slope):
    if amount == 2:
        one = jax.random.randint(key, (), max(1, total - most), min(most, total - 1) + 1)
        return jnp.stack([one, total - one])
    tallies = jnp.asarray(profile(amount, total, most, slope), jnp.int32)
    couples = (amount - 1) // 2
    source_of, sink = tallies[1:1 + 2 * couples:2], tallies[2:2 + 2 * couples:2]
    margin = jnp.minimum(source_of - 1, most - sink)
    moved = jax.random.randint(jax.random.fold_in(key, 1), (couples,), 0, 1 << 20) % (margin + 1)
    tallies = tallies.at[1:1 + 2 * couples:2].set(source_of - moved).at[2:2 + 2 * couples:2].set(sink + moved)
    return tallies[jax.random.permutation(jax.random.fold_in(key, 2), amount)]


def gaussian(key, dims, spread, most, split=(), kind=jnp.bfloat16):
    array = jax.random.normal(key, dims, jnp.float32) * spread
    if len(split) > 0:
        array = block_levels(key, dims, split, -0.22, 0.18) * array
    return jnp.clip(array, min=-most, max=most).astype(kind)


def setup_inputs(seed: int = 0) -> dict:
    key_of = jax.random.split(jax.random.key(seed), 6)
    queries = draw_queries(jax.random.fold_in(key_of[5], 71), 0)
    key_states = draw_key_states(jax.random.fold_in(key_of[5], 71), 0)
    value_states = gaussian(key_of[2], (TOKENS, HEADS * HEAD_DIM), 1.0, 6.0, ((0, 64), (1, 4)))
    clip_lengths = ragged(key_of[3], CLIPS, BLOCKS_ALL, CLIP_BLOCKS, 2).astype(jnp.int32)
    out_weight = gaussian(key_of[4], (HEADS * HEAD_DIM, DMODEL), (HEADS * HEAD_DIM) ** -0.5, 0.25, ((1, 4),))
    return dict(queries=queries, key_states=key_states, value_states=value_states, clip_lengths=clip_lengths, out_weight=out_weight)


def clip_index(positions, clip_ends):
    blocks = positions // BLOCK
    return jnp.sum((blocks[:, None] >= clip_ends[None, :]).astype(jnp.int32), axis=1)


def reference(queries, key_states, value_states, clip_lengths, out_weight):
    clip_ends = jnp.cumsum(clip_lengths).astype(jnp.int32)
    feature_width = HEADS * HEAD_DIM
    lead_rows = CLIP_DEVS * TOK_DEV
    window_rows = (CLIP_DEVS + 1) * TOK_DEV
    padded_keys = jnp.concatenate([jnp.zeros((lead_rows, feature_width), jnp.bfloat16), key_states], axis=0)
    padded_values = jnp.concatenate([jnp.zeros((lead_rows, feature_width), jnp.bfloat16), value_states], axis=0)

    def one_shard(own_shard):
        query_rows = lax.dynamic_slice_in_dim(queries, own_shard * TOK_DEV, TOK_DEV, 0)
        key_rows = lax.dynamic_slice_in_dim(padded_keys, own_shard * TOK_DEV, window_rows, 0)
        value_rows = lax.dynamic_slice_in_dim(padded_values, own_shard * TOK_DEV, window_rows, 0)
        query_heads = query_rows.astype(jnp.float32).reshape(TOK_DEV, HEADS, HEAD_DIM)
        key_heads = key_rows.astype(jnp.float32).reshape(window_rows, HEADS, HEAD_DIM)
        value_heads = value_rows.astype(jnp.float32).reshape(window_rows, HEADS, HEAD_DIM)
        query_pos = own_shard * TOK_DEV + jnp.arange(TOK_DEV, dtype=jnp.int32)
        key_pos = (own_shard - CLIP_DEVS) * TOK_DEV + jnp.arange(window_rows, dtype=jnp.int32)
        query_clip = clip_index(query_pos, clip_ends)
        key_clip = clip_index(key_pos, clip_ends)
        allowed = (query_clip[:, None] == key_clip[None, :]) & ((query_pos // BLOCK)[:, None] >= (key_pos // BLOCK)[None, :]) & (key_pos >= 0)[None, :]
        scores = jnp.einsum("qhd,khd->hqk", query_heads, key_heads) * (HEAD_DIM ** -0.5)
        scores = jnp.where(allowed[None], scores, -1e30)
        row_max = jnp.max(scores, axis=-1, keepdims=True)
        weights = jnp.exp(scores - row_max)
        row_sum = jnp.sum(weights, axis=-1)
        probs = lax.optimization_barrier(weights.astype(jnp.bfloat16)).astype(jnp.float32)
        weighted = jnp.einsum("hqk,khd->hqd", probs, value_heads)
        result = weighted / row_sum[..., None]
        return jnp.transpose(result, (1, 0, 2)).reshape(TOK_DEV, feature_width).astype(jnp.bfloat16)

    attended = lax.map(one_shard, jnp.arange(N_CTX, dtype=jnp.int32)).reshape(TOKENS, feature_width)
    return jnp.dot(attended, out_weight, preferred_element_type=jnp.float32).astype(jnp.bfloat16)
```

```python
import functools
import math

import jax
import jax.numpy as jnp
from jax import lax
from jax.experimental import pallas as pl
from jax.experimental.pallas import tpu as pltpu
from jax.sharding import PartitionSpec as P

HEAD_DIM = 128
BLOCK = 128
FAR = -1e30
START = -1e25
TO_LOG2 = math.log2(math.e) * HEAD_DIM**-0.5
VMEM_LIMIT = 48 * 2**20
KEY_TILE = 256


def vmem_spec():
    return pl.BlockSpec(memory_space=pltpu.VMEM)


def smem_spec():
    return pl.BlockSpec(memory_space=pltpu.SMEM)


def fold_kernel(first, info, key_base, q_own, q_sib, kv, *refs):
    if first:
        m_out, a_out, v_wide = refs
        m_in = a_in = None
    else:
        m_in, a_in, m_out, a_out, v_wide = refs
    tok = q_own.shape[0]
    blocks = tok // BLOCK
    k_base = key_base[0]

    def fold_half(half):
        q_ref = (q_own, q_sib)[half]
        rows = slice(half * tok, (half + 1) * tok)
        q_base = info[half]
        begin = [info[2 + half * blocks + i] for i in range(blocks)]
        wanted = (k_base + blocks > begin[0]) & (k_base < q_base + blocks)

        @pl.when(wanted)
        def _():
            v_wide[:, :HEAD_DIM] = kv[1]
            v_wide[:, HEAD_DIM:] = jnp.ones((tok, HEAD_DIM), jnp.bfloat16)
            q = q_ref[...]
            if first:
                m = jnp.full((tok, HEAD_DIM), START, jnp.float32)
                acc = jnp.zeros((tok, 2 * HEAD_DIM), jnp.float32)
            else:
                m = m_in[rows, :]
                acc = a_in[rows, :]
            for t in range(tok // KEY_TILE):
                keys = slice(t * KEY_TILE, (t + 1) * KEY_TILE)
                s = lax.dot_general(
                    q, kv[0, keys, :], (((1,), (1,)), ((), ())), preferred_element_type=jnp.float32
                )
                parts = []
                for j in range(KEY_TILE // BLOCK):
                    k_blk = k_base + t * (KEY_TILE // BLOCK) + j
                    column = []
                    for i in range(blocks):
                        seen = (k_blk >= begin[i]) & (k_blk <= q_base + i)
                        bias = jnp.where(seen, 0.0, FAR).astype(jnp.float32)
                        column.append(
                            s[i * BLOCK : (i + 1) * BLOCK, j * BLOCK : (j + 1) * BLOCK] + bias
                        )
                    parts.append(jnp.concatenate(column, axis=0))
                s = jnp.concatenate(parts, axis=1)
                new_m = jnp.maximum(m, jnp.max(s, axis=1, keepdims=True) * TO_LOG2)
                factor = jnp.exp2(m - new_m)
                p = jnp.exp2(s * TO_LOG2 - jnp.concatenate([new_m] * (KEY_TILE // HEAD_DIM), axis=1))
                added = jnp.dot(
                    p.astype(jnp.bfloat16), v_wide[keys, :], preferred_element_type=jnp.float32
                )
                acc = acc * jnp.concatenate([factor] * 2, axis=1) + added
                m = new_m
            m_out[rows, :] = m
            a_out[rows, :] = acc

        if first:

            @pl.when(jnp.logical_not(wanted))
            def _():
                m_out[rows, :] = jnp.full((tok, HEAD_DIM), START, jnp.float32)
                a_out[rows, :] = jnp.zeros((tok, 2 * HEAD_DIM), jnp.float32)

    fold_half(0)
    fold_half(1)


def fold(info, key_base, q_own, q_sib, kv, state):
    tok = q_own.shape[0]
    first = state is None
    shapes = [
        jax.ShapeDtypeStruct((2 * tok, HEAD_DIM), jnp.float32),
        jax.ShapeDtypeStruct((2 * tok, 2 * HEAD_DIM), jnp.float32),
    ]
    return pl.pallas_call(
        functools.partial(fold_kernel, first),
        out_shape=shapes,
        in_specs=[smem_spec()] * 2 + [vmem_spec()] * (3 if first else 5),
        out_specs=[vmem_spec()] * 2,
        scratch_shapes=[pltpu.VMEM((tok, 2 * HEAD_DIM), jnp.bfloat16)],
        input_output_aliases={} if first else {5: 0, 6: 1},
        compiler_params=pltpu.CompilerParams(vmem_limit_bytes=VMEM_LIMIT),
        cost_estimate=pl.CostEstimate(
            flops=8 * tok * tok * HEAD_DIM, bytes_accessed=10**6, transcendentals=2 * tok * tok
        ),
        name="fold",
    )(info, key_base, q_own, q_sib, kv, *(() if first else state))


def leave_kernel(m_ref, a_ref, out_ref):
    tok = out_ref.shape[0]
    total = a_ref[tok:, HEAD_DIM:]
    some = total > 0.0
    out = a_ref[tok:, :HEAD_DIM] / jnp.where(some, total, 1.0)
    log_sum = jnp.where(some, m_ref[tok:, :] + jnp.log2(jnp.where(some, total, 1.0)), START)
    high = log_sum.astype(jnp.bfloat16).astype(jnp.float32)
    middle = (log_sum - high).astype(jnp.bfloat16).astype(jnp.float32)
    low = log_sum - high - middle
    lane = lax.broadcasted_iota(jnp.int32, (tok, HEAD_DIM), 1)
    parts = jnp.where(lane == 0, high, jnp.where(lane == 1, middle, jnp.where(lane == 2, low, 0.0)))
    out_ref[:, :HEAD_DIM] = out.astype(jnp.bfloat16)
    out_ref[:, HEAD_DIM:] = parts.astype(jnp.bfloat16)


def leave(state):
    tok = state[0].shape[0] // 2
    return pl.pallas_call(
        leave_kernel,
        out_shape=jax.ShapeDtypeStruct((tok, 2 * HEAD_DIM), jnp.bfloat16),
        in_specs=[vmem_spec()] * 2,
        out_specs=vmem_spec(),
        compiler_params=pltpu.CompilerParams(vmem_limit_bytes=VMEM_LIMIT),
        name="leave",
    )(*state)


def join_kernel(m_ref, a_ref, other_ref, out_ref):
    tok = out_ref.shape[0]
    m = m_ref[:tok, :]
    log_sum = jnp.sum(other_ref[:, HEAD_DIM:].astype(jnp.float32), axis=1, keepdims=True)
    top = jnp.maximum(m, log_sum)
    own = jnp.exp2(m - top)
    sib = jnp.exp2(log_sum - top)
    mixed = a_ref[:tok, :HEAD_DIM] * own + other_ref[:, :HEAD_DIM].astype(jnp.float32) * sib
    out_ref[...] = (mixed / (a_ref[:tok, HEAD_DIM:] * own + sib)).astype(jnp.bfloat16)


def join(state, other):
    tok = other.shape[0]
    return pl.pallas_call(
        join_kernel,
        out_shape=jax.ShapeDtypeStruct((tok, HEAD_DIM), jnp.bfloat16),
        in_specs=[vmem_spec()] * 3,
        out_specs=vmem_spec(),
        compiler_params=pltpu.CompilerParams(vmem_limit_bytes=VMEM_LIMIT),
        name="join",
    )(*state, other)


def project_kernel(heads, own, left, right, far_a, far_b, weight, out_ref, w_turned):
    step = pl.program_id(0)
    h = heads[0]
    count = weight.shape[0] // HEAD_DIM

    @pl.when(step == 0)
    def _():
        for slot, by in enumerate((0, count - 1, 1, 2)):
            row = pl.multiple_of(lax.rem(h + by, count) * HEAD_DIM, HEAD_DIM)
            w_turned[slot * HEAD_DIM : (slot + 1) * HEAD_DIM, :] = weight[pl.ds(row, HEAD_DIM), :]

    height = out_ref.shape[0]
    rows = pl.ds(pl.multiple_of(step * height, height), height)
    half = pl.num_programs(0) // 2

    def run(far, far_rows):
        lhs = jnp.concatenate([own[rows, :], left[rows, :], right[rows, :], far[far_rows, :]], axis=1)
        out_ref[...] = jnp.dot(
            lhs, w_turned[...], preferred_element_type=jnp.float32
        ).astype(jnp.bfloat16)

    @pl.when(step < half)
    def _():
        run(far_a, rows)

    @pl.when(step >= half)
    def _():
        run(far_b, pl.ds(pl.multiple_of((step - half) * height, height), height))


def project(heads, pieces, weight):
    tok = pieces[0].shape[0]
    width = weight.shape[1]
    height = tok // 4
    return pl.pallas_call(
        project_kernel,
        grid=(4,),
        out_shape=jax.ShapeDtypeStruct((tok, width), jnp.bfloat16),
        in_specs=[smem_spec()] + [vmem_spec()] * 6,
        out_specs=pl.BlockSpec((height, width), lambda i: (i, 0)),
        scratch_shapes=[pltpu.VMEM(weight.shape, jnp.bfloat16)],
        compiler_params=pltpu.CompilerParams(vmem_limit_bytes=VMEM_LIMIT),
        name="project",
    )(heads, *pieces, weight)


def shards(queries, key_states, value_states, clip_lengths, out_weight):
    tok = queries.shape[0]
    blocks = tok // BLOCK
    ctx_count = lax.axis_size("ctx")
    head_count = lax.axis_size("head")
    chips = ctx_count // 2
    me = lax.axis_index("ctx")
    chip, core = me // 2, me % 2
    head = lax.axis_index("head")
    reach = 8

    def to(by_even, by_odd, cross=False):
        pairs = []
        for n in range(chips):
            pairs.append((2 * n + (1 if cross else 0), 2 * ((n + by_even) % chips)))
            pairs.append((2 * n + (0 if cross else 1), 2 * ((n + by_odd) % chips) + 1))
        return pairs

    def send(value, pairs):
        return lax.ppermute(value, "ctx", pairs)

    def turn(value, by):
        pairs = [(i, (i + by) % head_count) for i in range(head_count)]
        return lax.ppermute(value, "head", pairs)

    swap = [(i, i ^ 1) for i in range(ctx_count)]
    kv = jnp.stack([key_states, value_states])
    near = send(kv, to(1, reach))
    cross = send(kv, to(1, reach, cross=True))
    q_sib = send(queries, swap)

    ends = jnp.cumsum(clip_lengths).astype(jnp.int32)
    bases = jnp.stack([me, me ^ 1]) * blocks
    q_blocks = bases[:, None] + jnp.arange(blocks, dtype=jnp.int32)[None, :]
    begin = jnp.max(
        jnp.where(ends[None, None, :] <= q_blocks[:, :, None], ends[None, None, :], 0), axis=-1
    )
    info = jnp.concatenate([bases, begin.reshape(-1)]).astype(jnp.int32)

    state = fold(info, (me * blocks).reshape(1).astype(jnp.int32), queries, q_sib, kv, None)
    for step in range(reach // 2):
        from_chip = jnp.where(core == 0, chip - 1 - step, chip - reach + step)
        base = (2 * from_chip + core) * blocks
        other = (2 * from_chip + 1 - core) * blocks
        if step:
            near = send(near, to(1, -1))
            cross = send(cross, to(1, -1))
        state = fold(info, base.reshape(1).astype(jnp.int32), queries, q_sib, near, state)
        state = fold(info, other.reshape(1).astype(jnp.int32), queries, q_sib, cross, state)
    attended = join(state, send(leave(state), swap))
    half = tok // 2
    left = turn(attended, 1)
    right = turn(attended, -1)
    far_a = turn(attended[:half], 2)
    far_b = turn(attended[half:], -2)
    return project(
        head.reshape(1).astype(jnp.int32), (attended, left, right, far_a, far_b), out_weight
    )


def solution(mesh):
    placed = (P("ctx", "head"), P("ctx", "head"), P("ctx", "head"), P(), P(None, "head"))
    return jax.shard_map(
        shards, mesh=mesh, in_specs=placed, out_specs=P("ctx", "head"), check_vma=False
    )
```

```python
import functools
import math

import jax
import jax.numpy as jnp
from jax import lax
from jax.experimental import pallas as pl
from jax.experimental.pallas import tpu as pltpu
from jax.sharding import PartitionSpec as P

HEAD_DIM = 128
BLOCK = 128
FAR = -1e30
START = -1e25
TO_LOG2 = math.log2(math.e) * HEAD_DIM**-0.5
VMEM_LIMIT = 48 * 2**20
KEY_TILE = 256


def vmem_spec():
    return pl.BlockSpec(memory_space=pltpu.VMEM)


def smem_spec():
    return pl.BlockSpec(memory_space=pltpu.SMEM)


def fold_kernel(first, info, key_base, q_own, q_sib, kv, *refs):
    if first:
        m_out, a_out, v_wide = refs
        m_in = a_in = None
    else:
        m_in, a_in, m_out, a_out, v_wide = refs
    tok = q_own.shape[0]
    blocks = tok // BLOCK
    k_base = key_base[0]

    def fold_half(half):
        q_ref = (q_own, q_sib)[half]
        rows = slice(half * tok, (half + 1) * tok)
        q_base = info[half]
        begin = [info[2 + half * blocks + i] for i in range(blocks)]
        wanted = (k_base + blocks > begin[0]) & (k_base < q_base + blocks)

        @pl.when(wanted)
        def _():
            v_wide[:, :HEAD_DIM] = kv[1]
            v_wide[:, HEAD_DIM:] = jnp.ones((tok, HEAD_DIM), jnp.bfloat16)
            q = q_ref[...]
            if first:
                m = jnp.full((tok, HEAD_DIM), START, jnp.float32)
                acc = jnp.zeros((tok, 2 * HEAD_DIM), jnp.float32)
            else:
                m = m_in[rows, :]
                acc = a_in[rows, :]
            for t in range(tok // KEY_TILE):
                keys = slice(t * KEY_TILE, (t + 1) * KEY_TILE)
                s = lax.dot_general(
                    q, kv[0, keys, :], (((1,), (1,)), ((), ())), preferred_element_type=jnp.float32
                )
                parts = []
                for j in range(KEY_TILE // BLOCK):
                    k_blk = k_base + t * (KEY_TILE // BLOCK) + j
                    column = []
                    for i in range(blocks):
                        seen = (k_blk >= begin[i]) & (k_blk <= q_base + i)
                        bias = jnp.where(seen, 0.0, FAR).astype(jnp.float32)
                        column.append(
                            s[i * BLOCK : (i + 1) * BLOCK, j * BLOCK : (j + 1) * BLOCK] + bias
                        )
                    parts.append(jnp.concatenate(column, axis=0))
                s = jnp.concatenate(parts, axis=1)
                new_m = jnp.maximum(m, jnp.max(s, axis=1, keepdims=True) * TO_LOG2)
                factor = jnp.exp2(m - new_m)
                p = jnp.exp2(s * TO_LOG2 - jnp.concatenate([new_m] * (KEY_TILE // HEAD_DIM), axis=1))
                added = jnp.dot(
                    p.astype(jnp.bfloat16), v_wide[keys, :], preferred_element_type=jnp.float32
                )
                acc = acc * jnp.concatenate([factor] * 2, axis=1) + added
                m = new_m
            m_out[rows, :] = m
            a_out[rows, :] = acc

        if first:

            @pl.when(jnp.logical_not(wanted))
            def _():
                m_out[rows, :] = jnp.full((tok, HEAD_DIM), START, jnp.float32)
                a_out[rows, :] = jnp.zeros((tok, 2 * HEAD_DIM), jnp.float32)

    fold_half(0)
    fold_half(1)


def fold(info, key_base, q_own, q_sib, kv, state):
    tok = q_own.shape[0]
    first = state is None
    shapes = [
        jax.ShapeDtypeStruct((2 * tok, HEAD_DIM), jnp.float32),
        jax.ShapeDtypeStruct((2 * tok, 2 * HEAD_DIM), jnp.float32),
    ]
    return pl.pallas_call(
        functools.partial(fold_kernel, first),
        out_shape=shapes,
        in_specs=[smem_spec()] * 2 + [vmem_spec()] * (3 if first else 5),
        out_specs=[vmem_spec()] * 2,
        scratch_shapes=[pltpu.VMEM((tok, 2 * HEAD_DIM), jnp.bfloat16)],
        input_output_aliases={} if first else {5: 0, 6: 1},
        compiler_params=pltpu.CompilerParams(vmem_limit_bytes=VMEM_LIMIT),
        cost_estimate=pl.CostEstimate(
            flops=52 * tok * tok * HEAD_DIM, bytes_accessed=10**6, transcendentals=2 * tok * tok
        ),
        name="fold",
    )(info, key_base, q_own, q_sib, kv, *(() if first else state))


def leave_kernel(m_ref, a_ref, out_ref):
    tok = out_ref.shape[0]
    total = a_ref[tok:, HEAD_DIM:]
    some = total > 0.0
    out = a_ref[tok:, :HEAD_DIM] / jnp.where(some, total, 1.0)
    log_sum = jnp.where(some, m_ref[tok:, :] + jnp.log2(jnp.where(some, total, 1.0)), START)
    high = log_sum.astype(jnp.bfloat16).astype(jnp.float32)
    middle = (log_sum - high).astype(jnp.bfloat16).astype(jnp.float32)
    low = log_sum - high - middle
    lane = lax.broadcasted_iota(jnp.int32, (tok, HEAD_DIM), 1)
    parts = jnp.where(lane == 0, high, jnp.where(lane == 1, middle, jnp.where(lane == 2, low, 0.0)))
    out_ref[:, :HEAD_DIM] = out.astype(jnp.bfloat16)
    out_ref[:, HEAD_DIM:] = parts.astype(jnp.bfloat16)


def leave(state):
    tok = state[0].shape[0] // 2
    return pl.pallas_call(
        leave_kernel,
        out_shape=jax.ShapeDtypeStruct((tok, 2 * HEAD_DIM), jnp.bfloat16),
        in_specs=[vmem_spec()] * 2,
        out_specs=vmem_spec(),
        compiler_params=pltpu.CompilerParams(vmem_limit_bytes=VMEM_LIMIT),
        name="leave",
    )(*state)


def join_kernel(m_ref, a_ref, other_ref, out_ref):
    tok = out_ref.shape[0]
    m = m_ref[:tok, :]
    log_sum = jnp.sum(other_ref[:, HEAD_DIM:].astype(jnp.float32), axis=1, keepdims=True)
    top = jnp.maximum(m, log_sum)
    own = jnp.exp2(m - top)
    sib = jnp.exp2(log_sum - top)
    mixed = a_ref[:tok, :HEAD_DIM] * own + other_ref[:, :HEAD_DIM].astype(jnp.float32) * sib
    out_ref[...] = (mixed / (a_ref[:tok, HEAD_DIM:] * own + sib)).astype(jnp.bfloat16)


def join(state, other):
    tok = other.shape[0]
    return pl.pallas_call(
        join_kernel,
        out_shape=jax.ShapeDtypeStruct((tok, HEAD_DIM), jnp.bfloat16),
        in_specs=[vmem_spec()] * 3,
        out_specs=vmem_spec(),
        compiler_params=pltpu.CompilerParams(vmem_limit_bytes=VMEM_LIMIT),
        name="join",
    )(*state, other)


def project_kernel(heads, own, left, right, far_a, far_b, weight, out_ref, w_turned):
    step = pl.program_id(0)
    h = heads[0]
    count = weight.shape[0] // HEAD_DIM

    @pl.when(step == 0)
    def _():
        for slot, by in enumerate((0, count - 1, 1, 2)):
            row = pl.multiple_of(lax.rem(h + by, count) * HEAD_DIM, HEAD_DIM)
            w_turned[slot * HEAD_DIM : (slot + 1) * HEAD_DIM, :] = weight[pl.ds(row, HEAD_DIM), :]

    height = out_ref.shape[0]
    rows = pl.ds(pl.multiple_of(step * height, height), height)
    half = pl.num_programs(0) // 2

    def run(far, far_rows):
        lhs = jnp.concatenate([own[rows, :], left[rows, :], right[rows, :], far[far_rows, :]], axis=1)
        out_ref[...] = jnp.dot(
            lhs, w_turned[...], preferred_element_type=jnp.float32
        ).astype(jnp.bfloat16)

    @pl.when(step < half)
    def _():
        run(far_a, rows)

    @pl.when(step >= half)
    def _():
        run(far_b, pl.ds(pl.multiple_of((step - half) * height, height), height))


def project(heads, pieces, weight):
    tok = pieces[0].shape[0]
    width = weight.shape[1]
    height = tok // 4
    return pl.pallas_call(
        project_kernel,
        grid=(4,),
        out_shape=jax.ShapeDtypeStruct((tok, width), jnp.bfloat16),
        in_specs=[smem_spec()] + [vmem_spec()] * 6,
        out_specs=pl.BlockSpec((height, width), lambda i: (i, 0)),
        scratch_shapes=[pltpu.VMEM(weight.shape, jnp.bfloat16)],
        compiler_params=pltpu.CompilerParams(vmem_limit_bytes=VMEM_LIMIT),
        name="project",
    )(heads, *pieces, weight)


def shards(queries, key_states, value_states, clip_lengths, out_weight):
    tok = queries.shape[0]
    blocks = tok // BLOCK
    ctx_count = lax.axis_size("ctx")
    head_count = lax.axis_size("head")
    chips = ctx_count // 2
    me = lax.axis_index("ctx")
    chip, core = me // 2, me % 2
    head = lax.axis_index("head")
    reach = 8

    def to(by_even, by_odd, cross=False):
        pairs = []
        for n in range(chips):
            pairs.append((2 * n + (1 if cross else 0), 2 * ((n + by_even) % chips)))
            pairs.append((2 * n + (0 if cross else 1), 2 * ((n + by_odd) % chips) + 1))
        return pairs

    def send(value, pairs):
        return lax.ppermute(value, "ctx", pairs)

    def turn(value, by):
        pairs = [(i, (i + by) % head_count) for i in range(head_count)]
        return lax.ppermute(value, "head", pairs)

    swap = [(i, i ^ 1) for i in range(ctx_count)]
    kv = jnp.stack([key_states, value_states])
    near = send(kv, to(1, reach))
    cross = send(kv, to(1, reach, cross=True))
    q_sib = send(queries, swap)

    upto = jnp.arange(clip_lengths.shape[0])
    ends = jnp.sum(jnp.where(upto[None, :] <= upto[:, None], clip_lengths[None, :], 0), axis=1)
    bases = jnp.stack([me, me ^ 1]) * blocks
    q_blocks = bases[:, None] + jnp.arange(blocks, dtype=jnp.int32)[None, :]
    begin = jnp.max(
        jnp.where(ends[None, None, :] <= q_blocks[:, :, None], ends[None, None, :], 0), axis=-1
    )
    info = jnp.concatenate([bases, begin.reshape(-1)]).astype(jnp.int32)

    state = fold(info, (me * blocks).reshape(1).astype(jnp.int32), queries, q_sib, kv, None)
    for step in range(reach // 2):
        from_chip = jnp.where(core == 0, chip - 1 - step, chip - reach + step)
        base = (2 * from_chip + core) * blocks
        other = (2 * from_chip + 1 - core) * blocks
        if step:
            near = send(near, to(1, -1))
            cross = send(cross, to(1, -1))
        state = fold(info, base.reshape(1).astype(jnp.int32), queries, q_sib, near, state)
        state = fold(info, other.reshape(1).astype(jnp.int32), queries, q_sib, cross, state)
    attended = join(state, send(leave(state), swap))
    half = tok // 2
    left = turn(attended, 1)
    right = turn(attended, -1)
    far_a = turn(attended[:half], 2)
    far_b = turn(attended[half:], -2)
    return project(
        head.reshape(1).astype(jnp.int32), (attended, left, right, far_a, far_b), out_weight
    )


def solution(mesh):
    placed = (P("ctx", "head"), P("ctx", "head"), P("ctx", "head"), P(), P(None, "head"))
    return jax.shard_map(
        shards, mesh=mesh, in_specs=placed, out_specs=P("ctx", "head"), check_vma=False
    )
```

```python
import functools
import math

import jax
import jax.numpy as jnp
from jax import lax
from jax.experimental import pallas as pl
from jax.experimental.pallas import tpu as pltpu
from jax.sharding import PartitionSpec as P

HEAD_DIM = 128
BLOCK = 128
FAR = -1e30
START = -1e25
TO_LOG2 = math.log2(math.e) * HEAD_DIM**-0.5
VMEM_LIMIT = 48 * 2**20
KEY_TILE = 256


def vmem_spec():
    return pl.BlockSpec(memory_space=pltpu.VMEM)


def smem_spec():
    return pl.BlockSpec(memory_space=pltpu.SMEM)


def fold_kernel(first, info, key_base, q_own, q_sib, kv, *refs):
    if first:
        m_out, a_out, v_wide = refs
        m_in = a_in = None
    else:
        m_in, a_in, m_out, a_out, v_wide = refs
    tok = q_own.shape[0]
    blocks = tok // BLOCK
    k_base = key_base[0]

    def fold_half(half):
        q_ref = (q_own, q_sib)[half]
        rows = slice(half * tok, (half + 1) * tok)
        q_base = info[half]
        begin = [info[2 + half * blocks + i] for i in range(blocks)]
        wanted = (k_base + blocks > begin[0]) & (k_base < q_base + blocks)

        @pl.when(wanted)
        def _():
            v_wide[:, :HEAD_DIM] = kv[1]
            v_wide[:, HEAD_DIM:] = jnp.ones((tok, HEAD_DIM), jnp.bfloat16)
            q = q_ref[...]
            if first:
                m = jnp.full((tok, HEAD_DIM), START, jnp.float32)
                acc = jnp.zeros((tok, 2 * HEAD_DIM), jnp.float32)
            else:
                m = m_in[rows, :]
                acc = a_in[rows, :]
            for t in range(tok // KEY_TILE):
                keys = slice(t * KEY_TILE, (t + 1) * KEY_TILE)
                s = lax.dot_general(
                    q, kv[0, keys, :], (((1,), (1,)), ((), ())), preferred_element_type=jnp.float32
                )
                parts = []
                for j in range(KEY_TILE // BLOCK):
                    k_blk = k_base + t * (KEY_TILE // BLOCK) + j
                    column = []
                    for i in range(blocks):
                        seen = (k_blk >= begin[i]) & (k_blk <= q_base + i)
                        bias = jnp.where(seen, 0.0, FAR).astype(jnp.float32)
                        column.append(
                            s[i * BLOCK : (i + 1) * BLOCK, j * BLOCK : (j + 1) * BLOCK] + bias
                        )
                    parts.append(jnp.concatenate(column, axis=0))
                s = jnp.concatenate(parts, axis=1)
                new_m = jnp.maximum(m, jnp.max(s, axis=1, keepdims=True) * TO_LOG2)
                factor = jnp.exp2(m - new_m)
                p = jnp.exp2(s * TO_LOG2 - jnp.concatenate([new_m] * (KEY_TILE // HEAD_DIM), axis=1))
                added = jnp.dot(
                    p.astype(jnp.bfloat16), v_wide[keys, :], preferred_element_type=jnp.float32
                )
                acc = acc * jnp.concatenate([factor] * 2, axis=1) + added
                m = new_m
            m_out[rows, :] = m
            a_out[rows, :] = acc

        if first:

            @pl.when(jnp.logical_not(wanted))
            def _():
                m_out[rows, :] = jnp.full((tok, HEAD_DIM), START, jnp.float32)
                a_out[rows, :] = jnp.zeros((tok, 2 * HEAD_DIM), jnp.float32)

    fold_half(0)
    fold_half(1)


def fold(info, key_base, q_own, q_sib, kv, state):
    tok = q_own.shape[0]
    first = state is None
    shapes = [
        jax.ShapeDtypeStruct((2 * tok, HEAD_DIM), jnp.float32),
        jax.ShapeDtypeStruct((2 * tok, 2 * HEAD_DIM), jnp.float32),
    ]
    return pl.pallas_call(
        functools.partial(fold_kernel, first),
        out_shape=shapes,
        in_specs=[smem_spec()] * 2 + [vmem_spec()] * (3 if first else 5),
        out_specs=[vmem_spec()] * 2,
        scratch_shapes=[pltpu.VMEM((tok, 2 * HEAD_DIM), jnp.bfloat16)],
        input_output_aliases={} if first else {5: 0, 6: 1},
        compiler_params=pltpu.CompilerParams(vmem_limit_bytes=VMEM_LIMIT),
        cost_estimate=pl.CostEstimate(
            flops=52 * tok * tok * HEAD_DIM, bytes_accessed=10**6, transcendentals=2 * tok * tok
        ),
        name="fold",
    )(info, key_base, q_own, q_sib, kv, *(() if first else state))


def leave_kernel(m_ref, a_ref, out_ref):
    tok = out_ref.shape[0]
    total = a_ref[tok:, HEAD_DIM:]
    some = total > 0.0
    out = a_ref[tok:, :HEAD_DIM] / jnp.where(some, total, 1.0)
    log_sum = jnp.where(some, m_ref[tok:, :] + jnp.log2(jnp.where(some, total, 1.0)), START)
    high = log_sum.astype(jnp.bfloat16).astype(jnp.float32)
    middle = (log_sum - high).astype(jnp.bfloat16).astype(jnp.float32)
    low = log_sum - high - middle
    lane = lax.broadcasted_iota(jnp.int32, (tok, HEAD_DIM), 1)
    parts = jnp.where(lane == 0, high, jnp.where(lane == 1, middle, jnp.where(lane == 2, low, 0.0)))
    out_ref[:, :HEAD_DIM] = out.astype(jnp.bfloat16)
    out_ref[:, HEAD_DIM:] = parts.astype(jnp.bfloat16)


def leave(state):
    tok = state[0].shape[0] // 2
    return pl.pallas_call(
        leave_kernel,
        out_shape=jax.ShapeDtypeStruct((tok, 2 * HEAD_DIM), jnp.bfloat16),
        in_specs=[vmem_spec()] * 2,
        out_specs=vmem_spec(),
        compiler_params=pltpu.CompilerParams(vmem_limit_bytes=VMEM_LIMIT),
        name="leave",
    )(*state)


def join_kernel(m_ref, a_ref, other_ref, out_ref):
    tok = out_ref.shape[0]
    m = m_ref[:tok, :]
    log_sum = jnp.sum(other_ref[:, HEAD_DIM:].astype(jnp.float32), axis=1, keepdims=True)
    top = jnp.maximum(m, log_sum)
    own = jnp.exp2(m - top)
    sib = jnp.exp2(log_sum - top)
    mixed = a_ref[:tok, :HEAD_DIM] * own + other_ref[:, :HEAD_DIM].astype(jnp.float32) * sib
    out_ref[...] = (mixed / (a_ref[:tok, HEAD_DIM:] * own + sib)).astype(jnp.bfloat16)


def join(state, other):
    tok = other.shape[0]
    return pl.pallas_call(
        join_kernel,
        out_shape=jax.ShapeDtypeStruct((tok, HEAD_DIM), jnp.bfloat16),
        in_specs=[vmem_spec()] * 3,
        out_specs=vmem_spec(),
        compiler_params=pltpu.CompilerParams(vmem_limit_bytes=VMEM_LIMIT),
        name="join",
    )(*state, other)


def project_kernel(heads, own, left, right, far_a, far_b, weight, out_ref, lhs):
    step = pl.program_id(0)
    h = heads[0]
    count = weight.shape[0] // HEAD_DIM
    height = out_ref.shape[0]
    rows = pl.ds(pl.multiple_of(step * height, height), height)
    half = pl.num_programs(0) // 2

    def put(by, piece):
        column = pl.multiple_of(lax.rem(h + by, count) * HEAD_DIM, HEAD_DIM)
        lhs[:, pl.ds(column, HEAD_DIM)] = piece

    put(0, own[rows, :])
    put(count - 1, left[rows, :])
    put(1, right[rows, :])

    @pl.when(step < half)
    def _():
        put(2, far_a[rows, :])

    @pl.when(step >= half)
    def _():
        put(2, far_b[pl.ds(pl.multiple_of((step - half) * height, height), height), :])

    out_ref[...] = jnp.dot(
        lhs[...], weight[...], preferred_element_type=jnp.float32
    ).astype(jnp.bfloat16)


def project(heads, pieces, weight):
    tok = pieces[0].shape[0]
    width = weight.shape[1]
    height = tok // 4
    return pl.pallas_call(
        project_kernel,
        grid=(4,),
        out_shape=jax.ShapeDtypeStruct((tok, width), jnp.bfloat16),
        in_specs=[smem_spec()] + [vmem_spec()] * 6,
        out_specs=pl.BlockSpec((height, width), lambda i: (i, 0)),
        scratch_shapes=[pltpu.VMEM((height, weight.shape[0]), jnp.bfloat16)],
        compiler_params=pltpu.CompilerParams(vmem_limit_bytes=VMEM_LIMIT),
        name="project",
    )(heads, *pieces, weight)


def shards(queries, key_states, value_states, clip_lengths, out_weight):
    tok = queries.shape[0]
    blocks = tok // BLOCK
    ctx_count = lax.axis_size("ctx")
    head_count = lax.axis_size("head")
    chips = ctx_count // 2
    me = lax.axis_index("ctx")
    chip, core = me // 2, me % 2
    head = lax.axis_index("head")
    reach = 8

    def to(by_even, by_odd, cross=False):
        pairs = []
        for n in range(chips):
            pairs.append((2 * n + (1 if cross else 0), 2 * ((n + by_even) % chips)))
            pairs.append((2 * n + (0 if cross else 1), 2 * ((n + by_odd) % chips) + 1))
        return pairs

    def send(value, pairs):
        return lax.ppermute(value, "ctx", pairs)

    def turn(value, by):
        pairs = [(i, (i + by) % head_count) for i in range(head_count)]
        return lax.ppermute(value, "head", pairs)

    swap = [(i, i ^ 1) for i in range(ctx_count)]
    kv = jnp.stack([key_states, value_states])
    near = send(kv, to(1, reach))
    cross = send(kv, to(1, reach, cross=True))
    q_sib = send(queries, swap)

    upto = jnp.arange(clip_lengths.shape[0])
    ends = jnp.sum(jnp.where(upto[None, :] <= upto[:, None], clip_lengths[None, :], 0), axis=1)
    bases = jnp.stack([me, me ^ 1]) * blocks
    q_blocks = bases[:, None] + jnp.arange(blocks, dtype=jnp.int32)[None, :]
    begin = jnp.max(
        jnp.where(ends[None, None, :] <= q_blocks[:, :, None], ends[None, None, :], 0), axis=-1
    )
    info = jnp.concatenate([bases, begin.reshape(-1)]).astype(jnp.int32)

    state = fold(info, (me * blocks).reshape(1).astype(jnp.int32), queries, q_sib, kv, None)
    left_only = [(2 * n + 1, 2 * ((n - 1) % chips) + 1) for n in range(chips)]
    last = reach // 2
    nothing = -4 * blocks
    for step in range(last + 1):
        from_chip = jnp.where(core == 0, chip - 1 - step, chip - reach + step)
        base = (2 * from_chip + core) * blocks
        other = (2 * from_chip + 1 - core) * blocks
        if step == last:
            near = send(near, left_only)
            base = jnp.where(core == 0, nothing, base)
        elif step:
            near = send(near, to(1, -1))
            cross = send(cross, to(1, -1) if step < last - 1 else left_only)
        state = fold(info, base.reshape(1).astype(jnp.int32), queries, q_sib, near, state)
        if step < last:
            if step == last - 1:
                other = jnp.where(core == 0, nothing, other)
            state = fold(info, other.reshape(1).astype(jnp.int32), queries, q_sib, cross, state)
    attended = join(state, send(leave(state), swap))
    half = tok // 2
    left = turn(attended, 1)
    right = turn(attended, -1)
    far_a = turn(attended[:half], 2)
    far_b = turn(attended[half:], -2)
    return project(
        head.reshape(1).astype(jnp.int32), (attended, left, right, far_a, far_b), out_weight
    )


def solution(mesh):
    placed = (P("ctx", "head"), P("ctx", "head"), P("ctx", "head"), P(), P(None, "head"))
    return jax.shard_map(
        shards, mesh=mesh, in_specs=placed, out_specs=P("ctx", "head"), check_vma=False
    )
```

```python
import functools
import math

import jax
import jax.numpy as jnp
from jax import lax
from jax.experimental import pallas as pl
from jax.experimental.pallas import tpu as pltpu
from jax.sharding import PartitionSpec as P

HEAD_DIM = 128
BLOCK = 128
FAR = -1e30
START = -1e25
TO_LOG2 = math.log2(math.e) * HEAD_DIM**-0.5
VMEM_LIMIT = 24 * 2**20
KEY_TILE = 256
RING_CHIPS = 8


def vmem_spec():
    return pl.BlockSpec(memory_space=pltpu.VMEM)


def smem_spec():
    return pl.BlockSpec(memory_space=pltpu.SMEM)


def fold_kernel(first, info, key_base, q_0, q_1, q_2, q_3, kv, *refs):
    if first:
        m_out, a_out, v_wide = refs
        m_in = a_in = None
    else:
        m_in, a_in, m_out, a_out, v_wide = refs
    tok = q_0.shape[0]
    blocks = tok // BLOCK
    k_base = key_base[0]
    v_wide[:, :HEAD_DIM] = kv[1]
    v_wide[:, HEAD_DIM:] = jnp.ones((tok, HEAD_DIM), jnp.bfloat16)

    for part, q_ref in enumerate((q_0, q_1, q_2, q_3)):
        rows = slice(part * tok, (part + 1) * tok)
        q_base = info[part]
        begin = [info[4 + part * blocks + i] for i in range(blocks)]
        wanted = (k_base + blocks > begin[0]) & (k_base < q_base + blocks)

        @pl.when(wanted)
        def _(q_ref=q_ref, rows=rows, q_base=q_base, begin=begin):
            q = q_ref[...]
            if first:
                m = jnp.full((tok, HEAD_DIM), START, jnp.float32)
                acc = jnp.zeros((tok, 2 * HEAD_DIM), jnp.float32)
            else:
                m = m_in[rows, :]
                acc = a_in[rows, :]
            for t in range(tok // KEY_TILE):
                keys = slice(t * KEY_TILE, (t + 1) * KEY_TILE)
                s = lax.dot_general(
                    q, kv[0, keys, :], (((1,), (1,)), ((), ())), preferred_element_type=jnp.float32
                )
                parts = []
                for j in range(KEY_TILE // BLOCK):
                    k_blk = k_base + t * (KEY_TILE // BLOCK) + j
                    column = []
                    for i in range(blocks):
                        seen = (k_blk >= begin[i]) & (k_blk <= q_base + i)
                        bias = jnp.where(seen, 0.0, FAR).astype(jnp.float32)
                        column.append(
                            s[i * BLOCK : (i + 1) * BLOCK, j * BLOCK : (j + 1) * BLOCK] + bias
                        )
                    parts.append(jnp.concatenate(column, axis=0))
                s = jnp.concatenate(parts, axis=1)
                new_m = jnp.maximum(m, jnp.max(s, axis=1, keepdims=True) * TO_LOG2)
                factor = jnp.exp2(m - new_m)
                p = jnp.exp2(s * TO_LOG2 - jnp.concatenate([new_m] * (KEY_TILE // HEAD_DIM), axis=1))
                added = jnp.dot(
                    p.astype(jnp.bfloat16), v_wide[keys, :], preferred_element_type=jnp.float32
                )
                acc = acc * jnp.concatenate([factor] * 2, axis=1) + added
                m = new_m
            m_out[rows, :] = m
            a_out[rows, :] = acc

        if first:

            @pl.when(jnp.logical_not(wanted))
            def _(rows=rows):
                m_out[rows, :] = jnp.full((tok, HEAD_DIM), START, jnp.float32)
                a_out[rows, :] = jnp.zeros((tok, 2 * HEAD_DIM), jnp.float32)


def fold(info, key_base, q_parts, kv, state):
    tok = q_parts[0].shape[0]
    first = state is None
    shapes = [
        pltpu.VMEM((4 * tok, HEAD_DIM), jnp.float32),
        pltpu.VMEM((4 * tok, 2 * HEAD_DIM), jnp.float32),
    ]
    return pl.pallas_call(
        functools.partial(fold_kernel, first),
        out_shape=shapes,
        in_specs=[smem_spec()] * 2 + [vmem_spec()] * (5 if first else 7),
        out_specs=[vmem_spec()] * 2,
        scratch_shapes=[pltpu.VMEM((tok, 2 * HEAD_DIM), jnp.bfloat16)],
        input_output_aliases={} if first else {7: 0, 8: 1},
        compiler_params=pltpu.CompilerParams(vmem_limit_bytes=VMEM_LIMIT),
        cost_estimate=pl.CostEstimate(
            flops=52 * tok * tok * HEAD_DIM, bytes_accessed=10**6, transcendentals=2 * tok * tok
        ),
        name="fold",
    )(info, key_base, *q_parts, kv, *(() if first else state))


def diagonal():
    row = lax.broadcasted_iota(jnp.int32, (BLOCK, BLOCK), 0)
    return row == lax.broadcasted_iota(jnp.int32, (BLOCK, BLOCK), 1)


def pack(out_ref, out, log_sum):
    tok = out.shape[0]
    blocks = tok // BLOCK
    on = diagonal()
    rows = [
        jnp.sum(jnp.where(on, log_sum[i * BLOCK : (i + 1) * BLOCK, :], 0.0), axis=0, keepdims=True)
        for i in range(blocks)
    ]
    rest = jnp.concatenate(rows, axis=0)
    out_ref[:tok, :] = out.astype(jnp.bfloat16)
    for k in range(3):
        piece = rest.astype(jnp.bfloat16)
        rest = rest - piece.astype(jnp.float32)
        both = jnp.concatenate([piece.astype(jnp.float32), jnp.zeros((blocks, BLOCK), jnp.float32)])
        out_ref[tok + 2 * blocks * k : tok + 2 * blocks * (k + 1), :] = both.astype(jnp.bfloat16)


def unpack(ref, tok):
    blocks = tok // BLOCK
    on = diagonal()
    tail = ref[tok:, :].astype(jnp.float32)
    log_rows = sum(tail[2 * blocks * k : 2 * blocks * k + blocks, :] for k in range(3))
    columns = [
        jnp.sum(jnp.where(on, log_rows[i : i + 1, :], 0.0), axis=1, keepdims=True)
        for i in range(blocks)
    ]
    return ref[:tok, :].astype(jnp.float32), jnp.concatenate(columns, axis=0)


def packed_shape(tok):
    return jax.ShapeDtypeStruct((tok + 6 * (tok // BLOCK), HEAD_DIM), jnp.bfloat16)


def own_part(m_ref, a_ref, rows):
    return m_ref[rows, :], a_ref[rows, :HEAD_DIM], a_ref[rows, HEAD_DIM:]


def pack_state(out_ref, m, num, den):
    some = den > 0.0
    safe = jnp.where(some, den, 1.0)
    pack(out_ref, num / safe, jnp.where(some, m + jnp.log2(safe), START))


def mix(m, num, den, out, log_sum):
    top = jnp.maximum(m, log_sum)
    here = jnp.exp2(m - top)
    there = jnp.exp2(log_sum - top)
    return top, num * here + out * there, den * here + there * (log_sum > 0.5 * START)


def leave_kernel(tok, part, m_ref, a_ref, out_ref):
    pack_state(out_ref, *own_part(m_ref, a_ref, slice(part * tok, (part + 1) * tok)))


def pass_on_kernel(tok, part, m_ref, a_ref, other, out_ref):
    state = own_part(m_ref, a_ref, slice(part * tok, (part + 1) * tok))
    pack_state(out_ref, *mix(*state, *unpack(other, tok)))


def join_kernel(tok, m_ref, a_ref, other, back, out_ref):
    state = mix(*own_part(m_ref, a_ref, slice(0, tok)), *unpack(other, tok))
    _, num, den = mix(*state, *unpack(back, tok))
    out_ref[...] = (num / den).astype(jnp.bfloat16)


def small_call(kernel, name, out_shape, *args):
    return pl.pallas_call(
        kernel,
        out_shape=out_shape,
        in_specs=[vmem_spec()] * len(args),
        out_specs=vmem_spec(),
        compiler_params=pltpu.CompilerParams(vmem_limit_bytes=VMEM_LIMIT),
        name=name,
    )(*args)


def project_kernel(heads, own, left, right, far_a, far_b, weight, out_ref, lhs):
    step = pl.program_id(0)
    h = heads[0]
    count = weight.shape[0] // HEAD_DIM
    height = out_ref.shape[0]
    rows = pl.ds(pl.multiple_of(step * height, height), height)
    half = pl.num_programs(0) // 2

    def put(by, piece):
        column = pl.multiple_of(lax.rem(h + by, count) * HEAD_DIM, HEAD_DIM)
        lhs[:, pl.ds(column, HEAD_DIM)] = piece

    put(0, own[rows, :])
    put(count - 1, left[rows, :])
    put(1, right[rows, :])

    @pl.when(step < half)
    def _():
        put(2, far_a[rows, :])

    @pl.when(step >= half)
    def _():
        put(2, far_b[pl.ds(pl.multiple_of((step - half) * height, height), height), :])

    out_ref[...] = jnp.dot(
        lhs[...], weight[...], preferred_element_type=jnp.float32
    ).astype(jnp.bfloat16)


def project(heads, pieces, weight):
    tok = pieces[0].shape[0]
    width = weight.shape[1]
    height = tok // 4
    return pl.pallas_call(
        project_kernel,
        grid=(4,),
        out_shape=jax.ShapeDtypeStruct((tok, width), jnp.bfloat16),
        in_specs=[smem_spec()] + [vmem_spec()] * 6,
        out_specs=pl.BlockSpec((height, width), lambda i: (i, 0)),
        scratch_shapes=[pltpu.VMEM((height, weight.shape[0]), jnp.bfloat16)],
        compiler_params=pltpu.CompilerParams(vmem_limit_bytes=VMEM_LIMIT),
        name="project",
    )(heads, *pieces, weight)


def shards(queries, key_states, value_states, clip_lengths, out_weight):
    tok = queries.shape[0]
    blocks = tok // BLOCK
    ctx_count = lax.axis_size("ctx")
    head_count = lax.axis_size("head")
    ring = 2 * RING_CHIPS
    me = lax.axis_index("ctx")
    core = me % 2
    first_of_ring = me // ring * ring
    place = (me % ring) // 2
    head = lax.axis_index("head")

    def send(value, target):
        return lax.ppermute(value, "ctx", [(i, target(i)) for i in range(ctx_count)])

    def sibling(i):
        return i ^ 1

    def along(i):
        at = i % ring
        by = 2 if i % 2 == 0 else -2
        return i - at + (at + by) % ring

    def up(i):
        return (i + ring) % ctx_count

    def down(i):
        return (i - ring) % ctx_count

    def turn(value, by):
        pairs = [(i, (i + by) % head_count) for i in range(head_count)]
        return lax.ppermute(value, "head", pairs)

    kv = jnp.stack([key_states, value_states])
    cross = send(kv, sibling)
    near = send(kv, along)
    q_parts = (
        queries,
        send(queries, sibling),
        send(queries, down),
        send(queries, lambda i: sibling(down(i))),
    )

    upto = jnp.arange(clip_lengths.shape[0])
    ends = jnp.sum(jnp.where(upto[None, :] <= upto[:, None], clip_lengths[None, :], 0), axis=1)
    owners = jnp.stack([me, me ^ 1, (me + ring) % ctx_count, ((me + ring) % ctx_count) ^ 1])
    bases = owners * blocks
    q_blocks = bases[:, None] + jnp.arange(blocks, dtype=jnp.int32)[None, :]
    begin = jnp.max(
        jnp.where(ends[None, None, :] <= q_blocks[:, :, None], ends[None, None, :], 0), axis=-1
    )
    info = jnp.concatenate([bases, begin.reshape(-1)]).astype(jnp.int32)

    def base_of(step, of_core):
        chip = (place + jnp.where(core == 0, -step, step)) % RING_CHIPS
        return ((first_of_ring + 2 * chip + of_core) * blocks).reshape(1).astype(jnp.int32)

    state = fold(info, base_of(0, core), q_parts, kv, None)
    last = RING_CHIPS // 2
    for step in range(1, last + 1):
        if step > 1:
            near = send(near, along)
        state = fold(info, base_of(step, core), q_parts, near, state)
        if step < last:
            cross = send(cross, along)
            state = fold(info, base_of(step, 1 - core), q_parts, cross, state)

    packed = packed_shape(tok)
    leave = functools.partial(leave_kernel, tok)
    next_there = send(small_call(functools.partial(leave, 3), "leave_next", packed, *state), sibling)
    own_there = send(small_call(functools.partial(leave, 1), "leave_own", packed, *state), sibling)
    passed = small_call(
        functools.partial(pass_on_kernel, tok, 2), "pass_on", packed, *state, next_there
    )
    back = send(passed, up)
    attended = small_call(
        functools.partial(join_kernel, tok),
        "join",
        jax.ShapeDtypeStruct((tok, HEAD_DIM), jnp.bfloat16),
        *state,
        own_there,
        back,
    )
    half = tok // 2
    left = turn(attended, 1)
    right = turn(attended, -1)
    far_a = turn(attended[:half], 2)
    far_b = turn(attended[half:], -2)
    return project(
        head.reshape(1).astype(jnp.int32), (attended, left, right, far_a, far_b), out_weight
    )


def solution(mesh):
    placed = (P("ctx", "head"), P("ctx", "head"), P("ctx", "head"), P(), P(None, "head"))
    return jax.shard_map(
        shards, mesh=mesh, in_specs=placed, out_specs=P("ctx", "head"), check_vma=False
    )
```

```python
import functools
import math

import jax
import jax.numpy as jnp
from jax import lax
from jax.experimental import pallas as pl
from jax.experimental.pallas import tpu as pltpu
from jax.sharding import PartitionSpec as P

HEAD_DIM = 128
BLOCK = 128
FAR = -1e30
START = -1e25
TO_LOG2 = math.log2(math.e) * HEAD_DIM**-0.5
VMEM_LIMIT = 24 * 2**20
KEY_TILE = 256
RING_CHIPS = 8


def vmem_spec():
    return pl.BlockSpec(memory_space=pltpu.VMEM)


def smem_spec():
    return pl.BlockSpec(memory_space=pltpu.SMEM)


def fold_kernel(first, info, key_base, q_0, q_1, q_2, q_3, kv, *refs):
    if first:
        m_out, a_out, v_wide, q_all = refs
        m_in, a_in = m_out, a_out
        m_out[...] = jnp.full(m_out.shape, START, jnp.float32)
        a_out[...] = jnp.zeros(a_out.shape, jnp.float32)
    else:
        m_in, a_in, m_out, a_out, v_wide, q_all = refs
    tok = q_0.shape[0]
    blocks = tok // BLOCK
    k_base = key_base[0]

    def wants(part):
        return (k_base + blocks > info[4 + part * blocks]) & (k_base < info[part] + blocks)

    any_wants = False
    for part, q_ref in enumerate((q_0, q_1, q_2, q_3)):
        any_wants = any_wants | wants(part)

        @pl.when(wants(part))
        def _(part=part, q_ref=q_ref):
            q_all[part] = q_ref[...]

    @pl.when(any_wants)
    def _():
        v_wide[:, :HEAD_DIM] = kv[1]
        v_wide[:, HEAD_DIM:] = jnp.ones((tok, HEAD_DIM), jnp.bfloat16)

    @pl.loop(0, 4)
    def _(part):
        rows = pl.ds(pl.multiple_of(part * tok, tok), tok)
        q_base = info[part]
        begin = [info[4 + part * blocks + i] for i in range(blocks)]

        @pl.when(wants(part))
        def _():
            q = q_all[part]
            m = m_in[rows, :]
            acc = a_in[rows, :]
            for t in range(tok // KEY_TILE):
                keys = slice(t * KEY_TILE, (t + 1) * KEY_TILE)
                s = lax.dot_general(
                    q, kv[0, keys, :], (((1,), (1,)), ((), ())), preferred_element_type=jnp.float32
                )
                columns = []
                for j in range(KEY_TILE // BLOCK):
                    k_blk = k_base + t * (KEY_TILE // BLOCK) + j
                    column = []
                    for i in range(blocks):
                        seen = (k_blk >= begin[i]) & (k_blk <= q_base + i)
                        bias = jnp.where(seen, 0.0, FAR).astype(jnp.float32)
                        column.append(
                            s[i * BLOCK : (i + 1) * BLOCK, j * BLOCK : (j + 1) * BLOCK] + bias
                        )
                    columns.append(jnp.concatenate(column, axis=0))
                s = jnp.concatenate(columns, axis=1)
                new_m = jnp.maximum(m, jnp.max(s, axis=1, keepdims=True) * TO_LOG2)
                factor = jnp.exp2(m - new_m)
                p = jnp.exp2(s * TO_LOG2 - jnp.concatenate([new_m] * (KEY_TILE // HEAD_DIM), axis=1))
                added = jnp.dot(
                    p.astype(jnp.bfloat16), v_wide[keys, :], preferred_element_type=jnp.float32
                )
                acc = acc * jnp.concatenate([factor] * 2, axis=1) + added
                m = new_m
            m_out[rows, :] = m
            a_out[rows, :] = acc


def fold(info, key_base, q_parts, kv, state):
    tok = q_parts[0].shape[0]
    first = state is None
    shapes = [
        pltpu.VMEM((4 * tok, HEAD_DIM), jnp.float32),
        pltpu.VMEM((4 * tok, 2 * HEAD_DIM), jnp.float32),
    ]
    return pl.pallas_call(
        functools.partial(fold_kernel, first),
        out_shape=shapes,
        in_specs=[smem_spec()] * 2 + [vmem_spec()] * (5 if first else 7),
        out_specs=[vmem_spec()] * 2,
        scratch_shapes=[
            pltpu.VMEM((tok, 2 * HEAD_DIM), jnp.bfloat16),
            pltpu.VMEM((4, tok, HEAD_DIM), jnp.bfloat16),
        ],
        input_output_aliases={} if first else {7: 0, 8: 1},
        compiler_params=pltpu.CompilerParams(vmem_limit_bytes=VMEM_LIMIT),
        cost_estimate=pl.CostEstimate(
            flops=46 * tok * tok * HEAD_DIM, bytes_accessed=10**6, transcendentals=2 * tok * tok
        ),
        name="fold",
    )(info, key_base, *q_parts, kv, *(() if first else state))


def diagonal():
    row = lax.broadcasted_iota(jnp.int32, (BLOCK, BLOCK), 0)
    return row == lax.broadcasted_iota(jnp.int32, (BLOCK, BLOCK), 1)


def pack(out_ref, out, log_sum):
    tok = out.shape[0]
    blocks = tok // BLOCK
    on = diagonal()
    rows = [
        jnp.sum(jnp.where(on, log_sum[i * BLOCK : (i + 1) * BLOCK, :], 0.0), axis=0, keepdims=True)
        for i in range(blocks)
    ]
    rest = jnp.concatenate(rows, axis=0)
    out_ref[:tok, :] = out.astype(jnp.bfloat16)
    for k in range(3):
        piece = rest.astype(jnp.bfloat16)
        rest = rest - piece.astype(jnp.float32)
        both = jnp.concatenate([piece.astype(jnp.float32), jnp.zeros((blocks, BLOCK), jnp.float32)])
        out_ref[tok + 2 * blocks * k : tok + 2 * blocks * (k + 1), :] = both.astype(jnp.bfloat16)


def unpack(ref, tok):
    blocks = tok // BLOCK
    on = diagonal()
    tail = ref[tok:, :].astype(jnp.float32)
    log_rows = sum(tail[2 * blocks * k : 2 * blocks * k + blocks, :] for k in range(3))
    columns = [
        jnp.sum(jnp.where(on, log_rows[i : i + 1, :], 0.0), axis=1, keepdims=True)
        for i in range(blocks)
    ]
    return ref[:tok, :].astype(jnp.float32), jnp.concatenate(columns, axis=0)


def packed_shape(tok):
    return jax.ShapeDtypeStruct((tok + 6 * (tok // BLOCK), HEAD_DIM), jnp.bfloat16)


def own_part(m_ref, a_ref, rows):
    return m_ref[rows, :], a_ref[rows, :HEAD_DIM], a_ref[rows, HEAD_DIM:]


def pack_state(out_ref, m, num, den):
    some = den > 0.0
    safe = jnp.where(some, den, 1.0)
    pack(out_ref, num / safe, jnp.where(some, m + jnp.log2(safe), START))


def mix(m, num, den, out, log_sum):
    top = jnp.maximum(m, log_sum)
    here = jnp.exp2(m - top)
    there = jnp.exp2(log_sum - top)
    return top, num * here + out * there, den * here + there * (log_sum > 0.5 * START)


def leave_kernel(tok, part, m_ref, a_ref, out_ref):
    pack_state(out_ref, *own_part(m_ref, a_ref, slice(part * tok, (part + 1) * tok)))


def pass_on_kernel(tok, part, m_ref, a_ref, other, out_ref):
    state = own_part(m_ref, a_ref, slice(part * tok, (part + 1) * tok))
    pack_state(out_ref, *mix(*state, *unpack(other, tok)))


def join_kernel(tok, m_ref, a_ref, other, back, out_ref):
    state = mix(*own_part(m_ref, a_ref, slice(0, tok)), *unpack(other, tok))
    _, num, den = mix(*state, *unpack(back, tok))
    out_ref[...] = (num / den).astype(jnp.bfloat16)


def small_call(kernel, name, out_shape, *args):
    return pl.pallas_call(
        kernel,
        out_shape=out_shape,
        in_specs=[vmem_spec()] * len(args),
        out_specs=vmem_spec(),
        compiler_params=pltpu.CompilerParams(vmem_limit_bytes=VMEM_LIMIT),
        name=name,
    )(*args)


def project_kernel(heads, own, left, right, far_a, far_b, weight, out_ref, lhs):
    step = pl.program_id(0)
    h = heads[0]
    count = weight.shape[0] // HEAD_DIM
    height = out_ref.shape[0]
    rows = pl.ds(pl.multiple_of(step * height, height), height)
    half = pl.num_programs(0) // 2

    def put(by, piece):
        column = pl.multiple_of(lax.rem(h + by, count) * HEAD_DIM, HEAD_DIM)
        lhs[:, pl.ds(column, HEAD_DIM)] = piece

    put(0, own[rows, :])
    put(count - 1, left[rows, :])
    put(1, right[rows, :])

    @pl.when(step < half)
    def _():
        put(2, far_a[rows, :])

    @pl.when(step >= half)
    def _():
        put(2, far_b[pl.ds(pl.multiple_of((step - half) * height, height), height), :])

    out_ref[...] = jnp.dot(
        lhs[...], weight[...], preferred_element_type=jnp.float32
    ).astype(jnp.bfloat16)


def project(heads, pieces, weight):
    tok = pieces[0].shape[0]
    width = weight.shape[1]
    height = tok // 4
    return pl.pallas_call(
        project_kernel,
        grid=(4,),
        out_shape=jax.ShapeDtypeStruct((tok, width), jnp.bfloat16),
        in_specs=[smem_spec()] + [vmem_spec()] * 6,
        out_specs=pl.BlockSpec((height, width), lambda i: (i, 0)),
        scratch_shapes=[pltpu.VMEM((height, weight.shape[0]), jnp.bfloat16)],
        compiler_params=pltpu.CompilerParams(vmem_limit_bytes=VMEM_LIMIT),
        name="project",
    )(heads, *pieces, weight)


def shards(queries, key_states, value_states, clip_lengths, out_weight):
    tok = queries.shape[0]
    blocks = tok // BLOCK
    ctx_count = lax.axis_size("ctx")
    head_count = lax.axis_size("head")
    ring = 2 * RING_CHIPS
    me = lax.axis_index("ctx")
    core = me % 2
    first_of_ring = me // ring * ring
    place = (me % ring) // 2
    head = lax.axis_index("head")

    def send(value, target):
        return lax.ppermute(value, "ctx", [(i, target(i)) for i in range(ctx_count)])

    def sibling(i):
        return i ^ 1

    def along(i):
        at = i % ring
        by = 2 if i % 2 == 0 else -2
        return i - at + (at + by) % ring

    def after(value, state):
        value, m = lax.optimization_barrier((value, state[0]))
        return value, (m, state[1])

    def up(i):
        return (i + ring) % ctx_count

    def down(i):
        return (i - ring) % ctx_count

    def turn(value, by):
        pairs = [(i, (i + by) % head_count) for i in range(head_count)]
        return lax.ppermute(value, "head", pairs)

    kv = jnp.stack([key_states, value_states])
    near = send(kv, along)
    cross = send(kv, sibling)
    queries, cross = lax.optimization_barrier((queries, cross))
    q_parts = (
        queries,
        send(queries, sibling),
        send(queries, down),
        send(queries, lambda i: sibling(down(i))),
    )

    upto = jnp.arange(clip_lengths.shape[0])
    ends = jnp.sum(jnp.where(upto[None, :] <= upto[:, None], clip_lengths[None, :], 0), axis=1)
    owners = jnp.stack([me, me ^ 1, (me + ring) % ctx_count, ((me + ring) % ctx_count) ^ 1])
    bases = owners * blocks
    q_blocks = bases[:, None] + jnp.arange(blocks, dtype=jnp.int32)[None, :]
    begin = jnp.max(
        jnp.where(ends[None, None, :] <= q_blocks[:, :, None], ends[None, None, :], 0), axis=-1
    )
    info = jnp.concatenate([bases, begin.reshape(-1)]).astype(jnp.int32)

    def base_of(step, of_core):
        chip = (place + jnp.where(core == 0, -step, step)) % RING_CHIPS
        return ((first_of_ring + 2 * chip + of_core) * blocks).reshape(1).astype(jnp.int32)

    last = RING_CHIPS // 2
    cross = send(cross, along)
    state = fold(info, base_of(0, core), q_parts, kv, None)
    for step in range(1, last + 1):
        near, state = after(near, state)
        near_on = send(near, along) if step < last else None
        state = fold(info, base_of(step, core), q_parts, near, state)
        near = near_on
        if step < last:
            cross, state = after(cross, state)
            cross_on = send(cross, along) if step < last - 1 else None
            state = fold(info, base_of(step, 1 - core), q_parts, cross, state)
            cross = cross_on

    packed = packed_shape(tok)
    leave = functools.partial(leave_kernel, tok)
    next_there = send(small_call(functools.partial(leave, 3), "leave_next", packed, *state), sibling)
    own_there = send(small_call(functools.partial(leave, 1), "leave_own", packed, *state), sibling)
    passed = small_call(
        functools.partial(pass_on_kernel, tok, 2), "pass_on", packed, *state, next_there
    )
    back = send(passed, up)
    attended = small_call(
        functools.partial(join_kernel, tok),
        "join",
        jax.ShapeDtypeStruct((tok, HEAD_DIM), jnp.bfloat16),
        *state,
        own_there,
        back,
    )
    half = tok // 2
    left = turn(attended, 1)
    right = turn(attended, -1)
    far_a = turn(attended[:half], 2)
    far_b = turn(attended[half:], -2)
    return project(
        head.reshape(1).astype(jnp.int32), (attended, left, right, far_a, far_b), out_weight
    )


def solution(mesh):
    placed = (P("ctx", "head"), P("ctx", "head"), P("ctx", "head"), P(), P(None, "head"))
    return jax.shard_map(
        shards, mesh=mesh, in_specs=placed, out_specs=P("ctx", "head"), check_vma=False
    )
```

```python
import functools
import math

import jax
import jax.numpy as jnp
from jax import lax
from jax.experimental import pallas as pl
from jax.experimental.pallas import tpu as pltpu
from jax.sharding import PartitionSpec as P

HEAD_DIM = 128
BLOCK = 128
FAR = -1e30
START = -1e25
TO_LOG2 = math.log2(math.e) * HEAD_DIM**-0.5
VMEM_LIMIT = 24 * 2**20
KEY_TILE = 256
RING_CHIPS = 8


def vmem_spec():
    return pl.BlockSpec(memory_space=pltpu.VMEM)


def smem_spec():
    return pl.BlockSpec(memory_space=pltpu.SMEM)


def fold_kernel(first, info, key_base, q_0, q_1, q_2, q_3, kv, *refs):
    if first:
        m_out, a_out, v_wide, q_all = refs
        m_in, a_in = m_out, a_out
        m_out[...] = jnp.full(m_out.shape, START, jnp.float32)
        a_out[...] = jnp.zeros(a_out.shape, jnp.float32)
    else:
        m_in, a_in, m_out, a_out, v_wide, q_all = refs
    tok = q_0.shape[0]
    blocks = tok // BLOCK
    k_base = key_base[0]

    def wants(part):
        return (k_base + blocks > info[4 + part * blocks]) & (k_base < info[part] + blocks)

    any_wants = False
    for part, q_ref in enumerate((q_0, q_1, q_2, q_3)):
        any_wants = any_wants | wants(part)

        @pl.when(wants(part))
        def _(part=part, q_ref=q_ref):
            q_all[part] = q_ref[...]

    @pl.when(any_wants)
    def _():
        v_wide[:, :HEAD_DIM] = kv[1]
        v_wide[:, HEAD_DIM:] = jnp.ones((tok, HEAD_DIM), jnp.bfloat16)

    @pl.loop(0, 4)
    def _(part):
        rows = pl.ds(pl.multiple_of(part * tok, tok), tok)
        q_base = info[part]
        begin = [info[4 + part * blocks + i] for i in range(blocks)]

        @pl.when(wants(part))
        def _():
            q = q_all[part]
            m = m_in[rows, :]
            acc = a_in[rows, :]
            for t in range(tok // KEY_TILE):
                keys = slice(t * KEY_TILE, (t + 1) * KEY_TILE)
                s = lax.dot_general(
                    q, kv[0, keys, :], (((1,), (1,)), ((), ())), preferred_element_type=jnp.float32
                )
                columns = []
                for j in range(KEY_TILE // BLOCK):
                    k_blk = k_base + t * (KEY_TILE // BLOCK) + j
                    column = []
                    for i in range(blocks):
                        seen = (k_blk >= begin[i]) & (k_blk <= q_base + i)
                        bias = jnp.where(seen, 0.0, FAR).astype(jnp.float32)
                        column.append(
                            s[i * BLOCK : (i + 1) * BLOCK, j * BLOCK : (j + 1) * BLOCK] + bias
                        )
                    columns.append(jnp.concatenate(column, axis=0))
                s = jnp.concatenate(columns, axis=1)
                new_m = jnp.maximum(m, jnp.max(s, axis=1, keepdims=True) * TO_LOG2)
                factor = jnp.exp2(m - new_m)
                p = jnp.exp2(s * TO_LOG2 - jnp.concatenate([new_m] * (KEY_TILE // HEAD_DIM), axis=1))
                added = jnp.dot(
                    p.astype(jnp.bfloat16), v_wide[keys, :], preferred_element_type=jnp.float32
                )
                acc = acc * jnp.concatenate([factor] * 2, axis=1) + added
                m = new_m
            m_out[rows, :] = m
            a_out[rows, :] = acc


def fold(info, key_base, q_parts, kv, state):
    tok = q_parts[0].shape[0]
    first = state is None
    shapes = [
        pltpu.VMEM((4 * tok, HEAD_DIM), jnp.float32),
        pltpu.VMEM((4 * tok, 2 * HEAD_DIM), jnp.float32),
    ]
    return pl.pallas_call(
        functools.partial(fold_kernel, first),
        out_shape=shapes,
        in_specs=[smem_spec()] * 2 + [vmem_spec()] * (5 if first else 7),
        out_specs=[vmem_spec()] * 2,
        scratch_shapes=[
            pltpu.VMEM((tok, 2 * HEAD_DIM), jnp.bfloat16),
            pltpu.VMEM((4, tok, HEAD_DIM), jnp.bfloat16),
        ],
        input_output_aliases={} if first else {7: 0, 8: 1},
        compiler_params=pltpu.CompilerParams(vmem_limit_bytes=VMEM_LIMIT),
        cost_estimate=pl.CostEstimate(
            flops=12 * tok * tok * HEAD_DIM, bytes_accessed=10**6, transcendentals=2 * tok * tok
        ),
        name="fold",
    )(info, key_base, *q_parts, kv, *(() if first else state))


def diagonal():
    row = lax.broadcasted_iota(jnp.int32, (BLOCK, BLOCK), 0)
    return row == lax.broadcasted_iota(jnp.int32, (BLOCK, BLOCK), 1)


def pack(out_ref, out, log_sum):
    tok = out.shape[0]
    blocks = tok // BLOCK
    on = diagonal()
    rows = [
        jnp.sum(jnp.where(on, log_sum[i * BLOCK : (i + 1) * BLOCK, :], 0.0), axis=0, keepdims=True)
        for i in range(blocks)
    ]
    rest = jnp.concatenate(rows, axis=0)
    out_ref[:tok, :] = out.astype(jnp.bfloat16)
    for k in range(3):
        piece = rest.astype(jnp.bfloat16)
        rest = rest - piece.astype(jnp.float32)
        both = jnp.concatenate([piece.astype(jnp.float32), jnp.zeros((blocks, BLOCK), jnp.float32)])
        out_ref[tok + 2 * blocks * k : tok + 2 * blocks * (k + 1), :] = both.astype(jnp.bfloat16)


def unpack(ref, tok):
    blocks = tok // BLOCK
    on = diagonal()
    tail = ref[tok:, :].astype(jnp.float32)
    log_rows = sum(tail[2 * blocks * k : 2 * blocks * k + blocks, :] for k in range(3))
    columns = [
        jnp.sum(jnp.where(on, log_rows[i : i + 1, :], 0.0), axis=1, keepdims=True)
        for i in range(blocks)
    ]
    return ref[:tok, :].astype(jnp.float32), jnp.concatenate(columns, axis=0)


def packed_shape(tok):
    return jax.ShapeDtypeStruct((tok + 6 * (tok // BLOCK), HEAD_DIM), jnp.bfloat16)


def own_part(m_ref, a_ref, rows):
    return m_ref[rows, :], a_ref[rows, :HEAD_DIM], a_ref[rows, HEAD_DIM:]


def pack_state(out_ref, m, num, den):
    some = den > 0.0
    safe = jnp.where(some, den, 1.0)
    pack(out_ref, num / safe, jnp.where(some, m + jnp.log2(safe), START))


def mix(m, num, den, out, log_sum):
    top = jnp.maximum(m, log_sum)
    here = jnp.exp2(m - top)
    there = jnp.exp2(log_sum - top)
    return top, num * here + out * there, den * here + there * (log_sum > 0.5 * START)


def leave_kernel(tok, part, m_ref, a_ref, out_ref):
    pack_state(out_ref, *own_part(m_ref, a_ref, slice(part * tok, (part + 1) * tok)))


def pass_on_kernel(tok, part, m_ref, a_ref, other, out_ref):
    state = own_part(m_ref, a_ref, slice(part * tok, (part + 1) * tok))
    pack_state(out_ref, *mix(*state, *unpack(other, tok)))


def join_kernel(tok, m_ref, a_ref, other, back, out_ref):
    state = mix(*own_part(m_ref, a_ref, slice(0, tok)), *unpack(other, tok))
    _, num, den = mix(*state, *unpack(back, tok))
    out_ref[...] = (num / den).astype(jnp.bfloat16)


def small_call(kernel, name, out_shape, *args):
    return pl.pallas_call(
        kernel,
        out_shape=out_shape,
        in_specs=[vmem_spec()] * len(args),
        out_specs=vmem_spec(),
        compiler_params=pltpu.CompilerParams(vmem_limit_bytes=VMEM_LIMIT),
        name=name,
    )(*args)


def project_kernel(heads, own, left, right, far_a, far_b, weight, out_ref, lhs):
    step = pl.program_id(0)
    h = heads[0]
    count = weight.shape[0] // HEAD_DIM
    height = out_ref.shape[0]
    rows = pl.ds(pl.multiple_of(step * height, height), height)
    half = pl.num_programs(0) // 2

    def put(by, piece):
        column = pl.multiple_of(lax.rem(h + by, count) * HEAD_DIM, HEAD_DIM)
        lhs[:, pl.ds(column, HEAD_DIM)] = piece

    put(0, own[rows, :])
    put(count - 1, left[rows, :])
    put(1, right[rows, :])

    @pl.when(step < half)
    def _():
        put(2, far_a[rows, :])

    @pl.when(step >= half)
    def _():
        put(2, far_b[pl.ds(pl.multiple_of((step - half) * height, height), height), :])

    out_ref[...] = jnp.dot(
        lhs[...], weight[...], preferred_element_type=jnp.float32
    ).astype(jnp.bfloat16)


def project(heads, pieces, weight):
    tok = pieces[0].shape[0]
    width = weight.shape[1]
    height = tok // 4
    return pl.pallas_call(
        project_kernel,
        grid=(4,),
        out_shape=jax.ShapeDtypeStruct((tok, width), jnp.bfloat16),
        in_specs=[smem_spec()] + [vmem_spec()] * 6,
        out_specs=pl.BlockSpec((height, width), lambda i: (i, 0)),
        scratch_shapes=[pltpu.VMEM((height, weight.shape[0]), jnp.bfloat16)],
        compiler_params=pltpu.CompilerParams(vmem_limit_bytes=VMEM_LIMIT),
        name="project",
    )(heads, *pieces, weight)


def shards(queries, key_states, value_states, clip_lengths, out_weight):
    tok = queries.shape[0]
    blocks = tok // BLOCK
    ctx_count = lax.axis_size("ctx")
    head_count = lax.axis_size("head")
    ring = 2 * RING_CHIPS
    me = lax.axis_index("ctx")
    core = me % 2
    first_of_ring = me // ring * ring
    place = (me % ring) // 2
    head = lax.axis_index("head")

    def send(value, target):
        return lax.ppermute(value, "ctx", [(i, target(i)) for i in range(ctx_count)])

    def sibling(i):
        return i ^ 1

    def along(i):
        at = i % ring
        by = 2 if i % 2 == 0 else -2
        return i - at + (at + by) % ring

    def after(value, state):
        value, m = lax.optimization_barrier((value, state[0]))
        return value, (m, state[1])

    def up(i):
        return (i + ring) % ctx_count

    def down(i):
        return (i - ring) % ctx_count

    def turn(value, by):
        pairs = [(i, (i + by) % head_count) for i in range(head_count)]
        return lax.ppermute(value, "head", pairs)

    kv = jnp.stack([key_states, value_states])
    near = send(kv, along)
    cross = send(kv, sibling)
    next_own = send(queries, down)
    queries, cross = lax.optimization_barrier((queries, cross))
    q_parts = (queries, send(queries, sibling), next_own, send(next_own, sibling))

    upto = jnp.arange(clip_lengths.shape[0])
    ends = jnp.sum(jnp.where(upto[None, :] <= upto[:, None], clip_lengths[None, :], 0), axis=1)
    owners = jnp.stack([me, me ^ 1, (me + ring) % ctx_count, ((me + ring) % ctx_count) ^ 1])
    bases = owners * blocks
    q_blocks = bases[:, None] + jnp.arange(blocks, dtype=jnp.int32)[None, :]
    begin = jnp.max(
        jnp.where(ends[None, None, :] <= q_blocks[:, :, None], ends[None, None, :], 0), axis=-1
    )
    info = jnp.concatenate([bases, begin.reshape(-1)]).astype(jnp.int32)

    def base_of(step, of_core):
        chip = (place + jnp.where(core == 0, -step, step)) % RING_CHIPS
        return ((first_of_ring + 2 * chip + of_core) * blocks).reshape(1).astype(jnp.int32)

    order = []
    for step in range(1, RING_CHIPS // 2 + 1):
        order += [(step, core), (step, 1 - core)]
    order = order[:-1]
    arrived = [near, send(cross, along)]
    state = fold(info, base_of(0, core), q_parts, kv, None)
    for n, (step, of_core) in enumerate(order):
        if n + 2 < len(order):
            value = arrived[n]
            if n >= 2:
                value, state = after(value, state)
            arrived.append(send(value, along))
        state = fold(info, base_of(step, of_core), q_parts, arrived[n], state)

    packed = packed_shape(tok)
    leave = functools.partial(leave_kernel, tok)
    next_there = send(small_call(functools.partial(leave, 3), "leave_next", packed, *state), sibling)
    own_there = send(small_call(functools.partial(leave, 1), "leave_own", packed, *state), sibling)
    passed = small_call(
        functools.partial(pass_on_kernel, tok, 2), "pass_on", packed, *state, next_there
    )
    back = send(passed, up)
    attended = small_call(
        functools.partial(join_kernel, tok),
        "join",
        jax.ShapeDtypeStruct((tok, HEAD_DIM), jnp.bfloat16),
        *state,
        own_there,
        back,
    )
    half = tok // 2
    left = turn(attended, 1)
    right = turn(attended, -1)
    far_a = turn(attended[:half], 2)
    far_b = turn(attended[half:], -2)
    return project(
        head.reshape(1).astype(jnp.int32), (attended, left, right, far_a, far_b), out_weight
    )


def solution(mesh):
    placed = (P("ctx", "head"), P("ctx", "head"), P("ctx", "head"), P(), P(None, "head"))
    return jax.shard_map(
        shards, mesh=mesh, in_specs=placed, out_specs=P("ctx", "head"), check_vma=False
    )
```

```python
import functools
import math

import jax
import jax.numpy as jnp
from jax import lax
from jax.experimental import pallas as pl
from jax.experimental.pallas import tpu as pltpu
from jax.sharding import PartitionSpec as P

HEAD_DIM = 128
BLOCK = 128
FAR = -1e30
START = -1e25
TO_LOG2 = math.log2(math.e) * HEAD_DIM**-0.5
VMEM_LIMIT = 16 * 2**20
KEY_TILE = 256
RING_CHIPS = 8


def vmem_spec():
    return pl.BlockSpec(memory_space=pltpu.VMEM)


def smem_spec():
    return pl.BlockSpec(memory_space=pltpu.SMEM)


def fold_kernel(first, parts, info, key_base, *refs):
    count = len(parts)
    q_refs, kv, refs = refs[:count], refs[count], refs[count + 1 :]
    if first:
        m_out, a_out, v_wide, q_all = refs
        m_in, a_in = m_out, a_out
        m_out[...] = jnp.full(m_out.shape, START, jnp.float32)
        a_out[...] = jnp.zeros(a_out.shape, jnp.float32)
    else:
        m_in, a_in, m_out, a_out, v_wide, q_all = refs
    tok = q_refs[0].shape[0]
    blocks = tok // BLOCK
    k_base = key_base[0]

    def wants(part):
        return (k_base + blocks > info[4 + part * blocks]) & (k_base < info[part] + blocks)

    any_wants = False
    for part, q_ref in zip(parts, q_refs):
        any_wants = any_wants | wants(part)

        @pl.when(wants(part))
        def _(part=part, q_ref=q_ref):
            q_all[part - parts[0]] = q_ref[...]

    @pl.when(any_wants)
    def _():
        v_wide[:, :HEAD_DIM] = kv[1]
        v_wide[:, HEAD_DIM:] = jnp.ones((tok, HEAD_DIM), jnp.bfloat16)

    @pl.loop(parts[0], parts[0] + count)
    def _(part):
        rows = pl.ds(pl.multiple_of(part * tok, tok), tok)
        q_base = info[part]
        begin = [info[4 + part * blocks + i] for i in range(blocks)]

        @pl.when(wants(part))
        def _():
            q = q_all[part - parts[0]]
            m = m_in[rows, :]
            acc = a_in[rows, :]
            for t in range(tok // KEY_TILE):
                keys = slice(t * KEY_TILE, (t + 1) * KEY_TILE)
                s = lax.dot_general(
                    q, kv[0, keys, :], (((1,), (1,)), ((), ())), preferred_element_type=jnp.float32
                )
                columns = []
                for j in range(KEY_TILE // BLOCK):
                    k_blk = k_base + t * (KEY_TILE // BLOCK) + j
                    column = []
                    for i in range(blocks):
                        seen = (k_blk >= begin[i]) & (k_blk <= q_base + i)
                        bias = jnp.where(seen, 0.0, FAR).astype(jnp.float32)
                        column.append(
                            s[i * BLOCK : (i + 1) * BLOCK, j * BLOCK : (j + 1) * BLOCK] + bias
                        )
                    columns.append(jnp.concatenate(column, axis=0))
                s = jnp.concatenate(columns, axis=1)
                new_m = jnp.maximum(m, jnp.max(s, axis=1, keepdims=True) * TO_LOG2)
                factor = jnp.exp2(m - new_m)
                p = jnp.exp2(s * TO_LOG2 - jnp.concatenate([new_m] * (KEY_TILE // HEAD_DIM), axis=1))
                added = jnp.dot(
                    p.astype(jnp.bfloat16), v_wide[keys, :], preferred_element_type=jnp.float32
                )
                acc = acc * jnp.concatenate([factor] * 2, axis=1) + added
                m = new_m
            m_out[rows, :] = m
            a_out[rows, :] = acc


def fold(info, key_base, q_parts, parts, kv, state):
    tok = q_parts[0].shape[0]
    first = state is None
    count = len(parts)
    shapes = [
        pltpu.VMEM((4 * tok, HEAD_DIM), jnp.float32),
        pltpu.VMEM((4 * tok, 2 * HEAD_DIM), jnp.float32),
    ]
    return pl.pallas_call(
        functools.partial(fold_kernel, first, parts),
        out_shape=shapes,
        in_specs=[smem_spec()] * 2 + [vmem_spec()] * (count + (1 if first else 3)),
        out_specs=[vmem_spec()] * 2,
        scratch_shapes=[
            pltpu.VMEM((tok, 2 * HEAD_DIM), jnp.bfloat16),
            pltpu.VMEM((count, tok, HEAD_DIM), jnp.bfloat16),
        ],
        input_output_aliases={} if first else {count + 3: 0, count + 4: 1},
        compiler_params=pltpu.CompilerParams(vmem_limit_bytes=VMEM_LIMIT),
        cost_estimate=pl.CostEstimate(
            flops=46 * tok * tok * HEAD_DIM, bytes_accessed=10**6, transcendentals=2 * tok * tok
        ),
        name="fold",
    )(info, key_base, *[q_parts[p] for p in parts], kv, *(() if first else state))


def diagonal():
    row = lax.broadcasted_iota(jnp.int32, (BLOCK, BLOCK), 0)
    return row == lax.broadcasted_iota(jnp.int32, (BLOCK, BLOCK), 1)


def pack(out_ref, out, log_sum):
    tok = out.shape[0]
    blocks = tok // BLOCK
    on = diagonal()
    rows = [
        jnp.sum(jnp.where(on, log_sum[i * BLOCK : (i + 1) * BLOCK, :], 0.0), axis=0, keepdims=True)
        for i in range(blocks)
    ]
    rest = jnp.concatenate(rows, axis=0)
    out_ref[:tok, :] = out.astype(jnp.bfloat16)
    for k in range(3):
        piece = rest.astype(jnp.bfloat16)
        rest = rest - piece.astype(jnp.float32)
        both = jnp.concatenate([piece.astype(jnp.float32), jnp.zeros((blocks, BLOCK), jnp.float32)])
        out_ref[tok + 2 * blocks * k : tok + 2 * blocks * (k + 1), :] = both.astype(jnp.bfloat16)


def unpack(ref, tok):
    blocks = tok // BLOCK
    on = diagonal()
    tail = ref[tok:, :].astype(jnp.float32)
    log_rows = sum(tail[2 * blocks * k : 2 * blocks * k + blocks, :] for k in range(3))
    columns = [
        jnp.sum(jnp.where(on, log_rows[i : i + 1, :], 0.0), axis=1, keepdims=True)
        for i in range(blocks)
    ]
    return ref[:tok, :].astype(jnp.float32), jnp.concatenate(columns, axis=0)


def packed_shape(tok):
    return jax.ShapeDtypeStruct((tok + 6 * (tok // BLOCK), HEAD_DIM), jnp.bfloat16)


def own_part(m_ref, a_ref, rows):
    return m_ref[rows, :], a_ref[rows, :HEAD_DIM], a_ref[rows, HEAD_DIM:]


def pack_state(out_ref, m, num, den):
    some = den > 0.0
    safe = jnp.where(some, den, 1.0)
    pack(out_ref, num / safe, jnp.where(some, m + jnp.log2(safe), START))


def mix(m, num, den, out, log_sum):
    top = jnp.maximum(m, log_sum)
    here = jnp.exp2(m - top)
    there = jnp.exp2(log_sum - top)
    return top, num * here + out * there, den * here + there * (log_sum > 0.5 * START)


def leave_kernel(tok, part, m_ref, a_ref, out_ref):
    pack_state(out_ref, *own_part(m_ref, a_ref, slice(part * tok, (part + 1) * tok)))


def pass_on_kernel(tok, part, m_ref, a_ref, other, out_ref):
    state = own_part(m_ref, a_ref, slice(part * tok, (part + 1) * tok))
    pack_state(out_ref, *mix(*state, *unpack(other, tok)))


def join_kernel(tok, m_ref, a_ref, other, back, out_ref):
    state = mix(*own_part(m_ref, a_ref, slice(0, tok)), *unpack(other, tok))
    _, num, den = mix(*state, *unpack(back, tok))
    out_ref[...] = (num / den).astype(jnp.bfloat16)


def small_call(kernel, name, out_shape, *args):
    return pl.pallas_call(
        kernel,
        out_shape=out_shape,
        in_specs=[vmem_spec()] * len(args),
        out_specs=vmem_spec(),
        compiler_params=pltpu.CompilerParams(vmem_limit_bytes=VMEM_LIMIT),
        name=name,
    )(*args)


def project_kernel(heads, own, left, right, far_a, far_b, weight, out_ref, lhs):
    step = pl.program_id(0)
    h = heads[0]
    count = weight.shape[0] // HEAD_DIM
    height = out_ref.shape[0]
    rows = pl.ds(pl.multiple_of(step * height, height), height)
    half = pl.num_programs(0) // 2

    def put(by, piece):
        column = pl.multiple_of(lax.rem(h + by, count) * HEAD_DIM, HEAD_DIM)
        lhs[:, pl.ds(column, HEAD_DIM)] = piece

    put(0, own[rows, :])
    put(count - 1, left[rows, :])
    put(1, right[rows, :])

    @pl.when(step < half)
    def _():
        put(2, far_a[rows, :])

    @pl.when(step >= half)
    def _():
        put(2, far_b[pl.ds(pl.multiple_of((step - half) * height, height), height), :])

    out_ref[...] = jnp.dot(
        lhs[...], weight[...], preferred_element_type=jnp.float32
    ).astype(jnp.bfloat16)


def project(heads, pieces, weight):
    tok = pieces[0].shape[0]
    width = weight.shape[1]
    height = tok // 4
    return pl.pallas_call(
        project_kernel,
        grid=(4,),
        out_shape=jax.ShapeDtypeStruct((tok, width), jnp.bfloat16),
        in_specs=[smem_spec()] + [vmem_spec()] * 6,
        out_specs=pl.BlockSpec((height, width), lambda i: (i, 0)),
        scratch_shapes=[pltpu.VMEM((height, weight.shape[0]), jnp.bfloat16)],
        compiler_params=pltpu.CompilerParams(vmem_limit_bytes=VMEM_LIMIT),
        name="project",
    )(heads, *pieces, weight)


def shards(queries, key_states, value_states, clip_lengths, out_weight):
    tok = queries.shape[0]
    blocks = tok // BLOCK
    ctx_count = lax.axis_size("ctx")
    head_count = lax.axis_size("head")
    ring = 2 * RING_CHIPS
    me = lax.axis_index("ctx")
    core = me % 2
    first_of_ring = me // ring * ring
    place = (me % ring) // 2
    head = lax.axis_index("head")

    def send(value, target):
        return lax.ppermute(value, "ctx", [(i, target(i)) for i in range(ctx_count)])

    def sibling(i):
        return i ^ 1

    def along(i):
        at = i % ring
        by = 2 if i % 2 == 0 else -2
        return i - at + (at + by) % ring

    def after(value, state):
        value, m = lax.optimization_barrier((value, state[0]))
        return value, (m, state[1])

    def up(i):
        return (i + ring) % ctx_count

    def down(i):
        return (i - ring) % ctx_count

    def turn(value, by):
        pairs = [(i, (i + by) % head_count) for i in range(head_count)]
        return lax.ppermute(value, "head", pairs)

    kv = jnp.stack([key_states, value_states])
    near = send(kv, along)
    cross = send(kv, sibling)
    next_own = send(queries, down)
    queries, cross = lax.optimization_barrier((queries, cross))
    q_parts = (queries, send(queries, sibling), next_own, send(next_own, sibling))

    upto = jnp.arange(clip_lengths.shape[0])
    ends = jnp.sum(jnp.where(upto[None, :] <= upto[:, None], clip_lengths[None, :], 0), axis=1)
    owners = jnp.stack([me, me ^ 1, (me + ring) % ctx_count, ((me + ring) % ctx_count) ^ 1])
    bases = owners * blocks
    q_blocks = bases[:, None] + jnp.arange(blocks, dtype=jnp.int32)[None, :]
    begin = jnp.max(
        jnp.where(ends[None, None, :] <= q_blocks[:, :, None], ends[None, None, :], 0), axis=-1
    )
    info = jnp.concatenate([bases, begin.reshape(-1)]).astype(jnp.int32)

    def base_of(step, of_core):
        chip = (place + jnp.where(core == 0, -step, step)) % RING_CHIPS
        return ((first_of_ring + 2 * chip + of_core) * blocks).reshape(1).astype(jnp.int32)

    order = []
    for step in range(1, RING_CHIPS // 2 + 1):
        order += [(step, core), (step, 1 - core)]
    order = order[:-1]
    arrived = [near, send(cross, along)]
    everyone = (0, 1, 2, 3)
    state = fold(info, base_of(0, core), q_parts, (0, 1), kv, None)
    for n, (step, of_core) in enumerate(order):
        value = arrived[n]
        if n + 2 < len(order):
            value, state = after(value, state)
            arrived.append(send(value, along))
        if n == len(order) - 1:
            state = fold(info, base_of(0, core), q_parts, (2, 3), kv, state)
        state = fold(info, base_of(step, of_core), q_parts, everyone, value, state)

    packed = packed_shape(tok)
    leave = functools.partial(leave_kernel, tok)
    next_there = send(small_call(functools.partial(leave, 3), "leave_next", packed, *state), sibling)
    own_there = send(small_call(functools.partial(leave, 1), "leave_own", packed, *state), sibling)
    passed = small_call(
        functools.partial(pass_on_kernel, tok, 2), "pass_on", packed, *state, next_there
    )
    back = send(passed, up)
    attended = small_call(
        functools.partial(join_kernel, tok),
        "join",
        jax.ShapeDtypeStruct((tok, HEAD_DIM), jnp.bfloat16),
        *state,
        own_there,
        back,
    )
    half = tok // 2
    left = turn(attended, 1)
    right = turn(attended, -1)
    far_a = turn(attended[:half], 2)
    far_b = turn(attended[half:], -2)
    return project(
        head.reshape(1).astype(jnp.int32), (attended, left, right, far_a, far_b), out_weight
    )


def solution(mesh):
    placed = (P("ctx", "head"), P("ctx", "head"), P("ctx", "head"), P(), P(None, "head"))
    return jax.shard_map(
        shards, mesh=mesh, in_specs=placed, out_specs=P("ctx", "head"), check_vma=False
    )
```

```python
import functools
import math

import jax
import jax.numpy as jnp
from jax import lax
from jax.experimental import pallas as pl
from jax.experimental.pallas import tpu as pltpu
from jax.sharding import PartitionSpec as P

HEAD_DIM = 128
BLOCK = 128
FAR = -1e30
START = -1e25
TO_LOG2 = math.log2(math.e) * HEAD_DIM**-0.5
VMEM_LIMIT = 16 * 2**20
KEY_TILE = 256
RING_CHIPS = 8


def vmem_spec():
    return pl.BlockSpec(memory_space=pltpu.VMEM)


def smem_spec():
    return pl.BlockSpec(memory_space=pltpu.SMEM)


def fold_kernel(first, parts, info, key_base, *refs):
    count = len(parts)
    q_refs, kv, refs = refs[:count], refs[count], refs[count + 1 :]
    if first:
        m_out, a_out, v_wide, q_all = refs
        m_in, a_in = m_out, a_out
        m_out[...] = jnp.full(m_out.shape, START, jnp.float32)
        a_out[...] = jnp.zeros(a_out.shape, jnp.float32)
    else:
        m_in, a_in, m_out, a_out, v_wide, q_all = refs
    tok = q_refs[0].shape[0]
    blocks = tok // BLOCK
    k_base = key_base[0]

    def wants(part):
        return (k_base + blocks > info[4 + part * blocks]) & (k_base < info[part] + blocks)

    any_wants = False
    for part, q_ref in zip(parts, q_refs):
        any_wants = any_wants | wants(part)

        @pl.when(wants(part))
        def _(part=part, q_ref=q_ref):
            q_all[part - parts[0]] = q_ref[...]

    @pl.when(any_wants)
    def _():
        v_wide[:, :HEAD_DIM] = kv[1]
        v_wide[:, HEAD_DIM:] = jnp.ones((tok, HEAD_DIM), jnp.bfloat16)

    @pl.loop(parts[0], parts[0] + count)
    def _(part):
        rows = pl.ds(pl.multiple_of(part * tok, tok), tok)
        q_base = info[part]
        begin = [info[4 + part * blocks + i] for i in range(blocks)]

        @pl.when(wants(part))
        def _():
            q = q_all[part - parts[0]]
            m = m_in[rows, :]
            acc = a_in[rows, :]
            for t in range(tok // KEY_TILE):
                keys = slice(t * KEY_TILE, (t + 1) * KEY_TILE)
                s = lax.dot_general(
                    q, kv[0, keys, :], (((1,), (1,)), ((), ())), preferred_element_type=jnp.float32
                )
                columns = []
                for j in range(KEY_TILE // BLOCK):
                    k_blk = k_base + t * (KEY_TILE // BLOCK) + j
                    column = []
                    for i in range(blocks):
                        seen = (k_blk >= begin[i]) & (k_blk <= q_base + i)
                        bias = jnp.where(seen, 0.0, FAR).astype(jnp.float32)
                        column.append(
                            s[i * BLOCK : (i + 1) * BLOCK, j * BLOCK : (j + 1) * BLOCK] + bias
                        )
                    columns.append(jnp.concatenate(column, axis=0))
                s = jnp.concatenate(columns, axis=1)
                new_m = jnp.maximum(m, jnp.max(s, axis=1, keepdims=True) * TO_LOG2)
                factor = jnp.exp2(m - new_m)
                p = jnp.exp2(s * TO_LOG2 - jnp.concatenate([new_m] * (KEY_TILE // HEAD_DIM), axis=1))
                added = jnp.dot(
                    p.astype(jnp.bfloat16), v_wide[keys, :], preferred_element_type=jnp.float32
                )
                acc = acc * jnp.concatenate([factor] * 2, axis=1) + added
                m = new_m
            m_out[rows, :] = m
            a_out[rows, :] = acc


def fold(info, key_base, q_parts, parts, kv, state, weight=46):
    tok = q_parts[0].shape[0]
    first = state is None
    count = len(parts)
    shapes = [
        pltpu.VMEM((4 * tok, HEAD_DIM), jnp.float32),
        pltpu.VMEM((4 * tok, 2 * HEAD_DIM), jnp.float32),
    ]
    return pl.pallas_call(
        functools.partial(fold_kernel, first, parts),
        out_shape=shapes,
        in_specs=[smem_spec()] * 2 + [vmem_spec()] * (count + (1 if first else 3)),
        out_specs=[vmem_spec()] * 2,
        scratch_shapes=[
            pltpu.VMEM((tok, 2 * HEAD_DIM), jnp.bfloat16),
            pltpu.VMEM((count, tok, HEAD_DIM), jnp.bfloat16),
        ],
        input_output_aliases={} if first else {count + 3: 0, count + 4: 1},
        compiler_params=pltpu.CompilerParams(vmem_limit_bytes=VMEM_LIMIT),
        cost_estimate=pl.CostEstimate(
            flops=weight * tok * tok * HEAD_DIM, bytes_accessed=10**6, transcendentals=2 * tok * tok
        ),
        name="fold",
    )(info, key_base, *[q_parts[p] for p in parts], kv, *(() if first else state))


def diagonal():
    row = lax.broadcasted_iota(jnp.int32, (BLOCK, BLOCK), 0)
    return row == lax.broadcasted_iota(jnp.int32, (BLOCK, BLOCK), 1)


def pack(out_ref, out, log_sum):
    tok = out.shape[0]
    blocks = tok // BLOCK
    on = diagonal()
    rows = [
        jnp.sum(jnp.where(on, log_sum[i * BLOCK : (i + 1) * BLOCK, :], 0.0), axis=0, keepdims=True)
        for i in range(blocks)
    ]
    rest = jnp.concatenate(rows, axis=0)
    out_ref[:tok, :] = out.astype(jnp.bfloat16)
    for k in range(3):
        piece = rest.astype(jnp.bfloat16)
        rest = rest - piece.astype(jnp.float32)
        both = jnp.concatenate([piece.astype(jnp.float32), jnp.zeros((blocks, BLOCK), jnp.float32)])
        out_ref[tok + 2 * blocks * k : tok + 2 * blocks * (k + 1), :] = both.astype(jnp.bfloat16)


def unpack(ref, tok):
    blocks = tok // BLOCK
    on = diagonal()
    tail = ref[tok:, :].astype(jnp.float32)
    log_rows = sum(tail[2 * blocks * k : 2 * blocks * k + blocks, :] for k in range(3))
    columns = [
        jnp.sum(jnp.where(on, log_rows[i : i + 1, :], 0.0), axis=1, keepdims=True)
        for i in range(blocks)
    ]
    return ref[:tok, :].astype(jnp.float32), jnp.concatenate(columns, axis=0)


def packed_shape(tok):
    return jax.ShapeDtypeStruct((tok + 6 * (tok // BLOCK), HEAD_DIM), jnp.bfloat16)


def own_part(m_ref, a_ref, rows):
    return m_ref[rows, :], a_ref[rows, :HEAD_DIM], a_ref[rows, HEAD_DIM:]


def pack_state(out_ref, m, num, den):
    some = den > 0.0
    safe = jnp.where(some, den, 1.0)
    pack(out_ref, num / safe, jnp.where(some, m + jnp.log2(safe), START))


def mix(m, num, den, out, log_sum):
    top = jnp.maximum(m, log_sum)
    here = jnp.exp2(m - top)
    there = jnp.exp2(log_sum - top)
    return top, num * here + out * there, den * here + there * (log_sum > 0.5 * START)


def leave_kernel(tok, part, m_ref, a_ref, out_ref):
    pack_state(out_ref, *own_part(m_ref, a_ref, slice(part * tok, (part + 1) * tok)))


def pass_on_kernel(tok, part, m_ref, a_ref, other, out_ref):
    state = own_part(m_ref, a_ref, slice(part * tok, (part + 1) * tok))
    pack_state(out_ref, *mix(*state, *unpack(other, tok)))


def join_kernel(tok, m_ref, a_ref, other, back, out_ref):
    state = mix(*own_part(m_ref, a_ref, slice(0, tok)), *unpack(other, tok))
    _, num, den = mix(*state, *unpack(back, tok))
    out_ref[...] = (num / den).astype(jnp.bfloat16)


def small_call(kernel, name, out_shape, *args):
    return pl.pallas_call(
        kernel,
        out_shape=out_shape,
        in_specs=[vmem_spec()] * len(args),
        out_specs=vmem_spec(),
        compiler_params=pltpu.CompilerParams(vmem_limit_bytes=VMEM_LIMIT),
        name=name,
    )(*args)


def project_kernel(heads, own, left, right, far_a, far_b, weight, out_ref, lhs):
    step = pl.program_id(0)
    h = heads[0]
    count = weight.shape[0] // HEAD_DIM
    height = out_ref.shape[0]
    rows = pl.ds(pl.multiple_of(step * height, height), height)
    half = pl.num_programs(0) // 2

    def put(by, piece):
        column = pl.multiple_of(lax.rem(h + by, count) * HEAD_DIM, HEAD_DIM)
        lhs[:, pl.ds(column, HEAD_DIM)] = piece

    put(0, own[rows, :])
    put(count - 1, left[rows, :])
    put(1, right[rows, :])

    @pl.when(step < half)
    def _():
        put(2, far_a[rows, :])

    @pl.when(step >= half)
    def _():
        put(2, far_b[pl.ds(pl.multiple_of((step - half) * height, height), height), :])

    out_ref[...] = jnp.dot(
        lhs[...], weight[...], preferred_element_type=jnp.float32
    ).astype(jnp.bfloat16)


def project(heads, pieces, weight):
    tok = pieces[0].shape[0]
    width = weight.shape[1]
    height = tok // 4
    return pl.pallas_call(
        project_kernel,
        grid=(4,),
        out_shape=jax.ShapeDtypeStruct((tok, width), jnp.bfloat16),
        in_specs=[smem_spec()] + [vmem_spec()] * 6,
        out_specs=pl.BlockSpec((height, width), lambda i: (i, 0)),
        scratch_shapes=[pltpu.VMEM((height, weight.shape[0]), jnp.bfloat16)],
        compiler_params=pltpu.CompilerParams(vmem_limit_bytes=VMEM_LIMIT),
        name="project",
    )(heads, *pieces, weight)


def shards(queries, key_states, value_states, clip_lengths, out_weight):
    tok = queries.shape[0]
    blocks = tok // BLOCK
    ctx_count = lax.axis_size("ctx")
    head_count = lax.axis_size("head")
    ring = 2 * RING_CHIPS
    me = lax.axis_index("ctx")
    core = me % 2
    first_of_ring = me // ring * ring
    place = (me % ring) // 2
    head = lax.axis_index("head")

    def send(value, target):
        return lax.ppermute(value, "ctx", [(i, target(i)) for i in range(ctx_count)])

    def sibling(i):
        return i ^ 1

    def along(i):
        at = i % ring
        by = 2 if i % 2 == 0 else -2
        return i - at + (at + by) % ring

    def after(value, state):
        value, m = lax.optimization_barrier((value, state[0]))
        return value, (m, state[1])

    def up(i):
        return (i + ring) % ctx_count

    def down(i):
        return (i - ring) % ctx_count

    def turn(value, by):
        pairs = [(i, (i + by) % head_count) for i in range(head_count)]
        return lax.ppermute(value, "head", pairs)

    kv = jnp.stack([key_states, value_states])
    near = send(kv, along)
    cross = send(kv, lambda i: along(sibling(i)))
    next_own = send(queries, down)
    q_sibling = send(queries, sibling)

    upto = jnp.arange(clip_lengths.shape[0])
    ends = jnp.sum(jnp.where(upto[None, :] <= upto[:, None], clip_lengths[None, :], 0), axis=1)
    owners = jnp.stack([me, me ^ 1, (me + ring) % ctx_count, ((me + ring) % ctx_count) ^ 1])
    bases = owners * blocks
    q_blocks = bases[:, None] + jnp.arange(blocks, dtype=jnp.int32)[None, :]
    begin = jnp.max(
        jnp.where(ends[None, None, :] <= q_blocks[:, :, None], ends[None, None, :], 0), axis=-1
    )
    info = jnp.concatenate([bases, begin.reshape(-1)]).astype(jnp.int32)

    def base_of(step, of_core):
        chip = (place + jnp.where(core == 0, -step, step)) % RING_CHIPS
        return ((first_of_ring + 2 * chip + of_core) * blocks).reshape(1).astype(jnp.int32)

    order = []
    for step in range(1, RING_CHIPS // 2 + 1):
        order += [(step, core), (step, 1 - core)]
    order = order[:-1]
    arrived = [near, cross]
    everyone = (0, 1, 2, 3)
    own_base = base_of(0, core)
    state = fold(info, own_base, (queries,), (0,), kv, None, 4)
    state = fold(info, own_base, (queries, q_sibling), (1,), kv, state, 4)
    next_own, state = after(next_own, state)
    q_parts = (queries, q_sibling, next_own, send(next_own, sibling))
    for n, (step, of_core) in enumerate(order):
        value = arrived[n]
        if n + 2 < len(order):
            value, state = after(value, state)
            arrived.append(send(value, along))
        if n == len(order) - 1:
            state = fold(info, own_base, q_parts, (2, 3), kv, state)
        state = fold(
            info, base_of(step, of_core), q_parts, everyone, value, state, 46 if n else 8
        )

    packed = packed_shape(tok)
    leave = functools.partial(leave_kernel, tok)
    next_there = send(small_call(functools.partial(leave, 3), "leave_next", packed, *state), sibling)
    own_there = send(small_call(functools.partial(leave, 1), "leave_own", packed, *state), sibling)
    passed = small_call(
        functools.partial(pass_on_kernel, tok, 2), "pass_on", packed, *state, next_there
    )
    back = send(passed, up)
    attended = small_call(
        functools.partial(join_kernel, tok),
        "join",
        jax.ShapeDtypeStruct((tok, HEAD_DIM), jnp.bfloat16),
        *state,
        own_there,
        back,
    )
    half = tok // 2
    left = turn(attended, 1)
    right = turn(attended, -1)
    far_a = turn(attended[:half], 2)
    far_b = turn(attended[half:], -2)
    return project(
        head.reshape(1).astype(jnp.int32), (attended, left, right, far_a, far_b), out_weight
    )


def solution(mesh):
    placed = (P("ctx", "head"), P("ctx", "head"), P("ctx", "head"), P(), P(None, "head"))
    return jax.shard_map(
        shards, mesh=mesh, in_specs=placed, out_specs=P("ctx", "head"), check_vma=False
    )
```

```python
import functools
import math

import jax
import jax.numpy as jnp
from jax import lax
from jax.experimental import pallas as pl
from jax.experimental.pallas import tpu as pltpu
from jax.sharding import PartitionSpec as P

HEAD_DIM = 128
BLOCK = 128
FAR = -1e30
START = -1e25
TO_LOG2 = math.log2(math.e) * HEAD_DIM**-0.5
VMEM_LIMIT = 16 * 2**20
KEY_TILE = 256
RING_CHIPS = 8


def vmem_spec():
    return pl.BlockSpec(memory_space=pltpu.VMEM)


def smem_spec():
    return pl.BlockSpec(memory_space=pltpu.SMEM)


def fold_kernel(first, parts, info, key_base, *refs):
    count = len(parts)
    q_refs, kv, refs = refs[:count], refs[count], refs[count + 1 :]
    if first:
        m_out, a_out, v_wide, q_all = refs
        m_in, a_in = m_out, a_out
        m_out[...] = jnp.full(m_out.shape, START, jnp.float32)
        a_out[...] = jnp.zeros(a_out.shape, jnp.float32)
    else:
        m_in, a_in, m_out, a_out, v_wide, q_all = refs
    tok = q_refs[0].shape[0]
    blocks = tok // BLOCK
    k_base = key_base[0]

    def wants(part):
        return (k_base + blocks > info[4 + part * blocks]) & (k_base < info[part] + blocks)

    any_wants = False
    for part, q_ref in zip(parts, q_refs):
        any_wants = any_wants | wants(part)

        @pl.when(wants(part))
        def _(part=part, q_ref=q_ref):
            q_all[part - parts[0]] = q_ref[...]

    @pl.when(any_wants)
    def _():
        v_wide[:, :HEAD_DIM] = kv[1]
        v_wide[:, HEAD_DIM:] = jnp.ones((tok, HEAD_DIM), jnp.bfloat16)

    @pl.loop(parts[0], parts[0] + count)
    def _(part):
        rows = pl.ds(pl.multiple_of(part * tok, tok), tok)
        q_base = info[part]
        begin = [info[4 + part * blocks + i] for i in range(blocks)]

        @pl.when(wants(part))
        def _():
            q = q_all[part - parts[0]]
            m = m_in[rows, :]
            acc = a_in[rows, :]
            for t in range(tok // KEY_TILE):
                keys = slice(t * KEY_TILE, (t + 1) * KEY_TILE)
                s = lax.dot_general(
                    q, kv[0, keys, :], (((1,), (1,)), ((), ())), preferred_element_type=jnp.float32
                )
                columns = []
                for j in range(KEY_TILE // BLOCK):
                    k_blk = k_base + t * (KEY_TILE // BLOCK) + j
                    column = []
                    for i in range(blocks):
                        seen = (k_blk >= begin[i]) & (k_blk <= q_base + i)
                        bias = jnp.where(seen, 0.0, FAR).astype(jnp.float32)
                        column.append(
                            s[i * BLOCK : (i + 1) * BLOCK, j * BLOCK : (j + 1) * BLOCK] + bias
                        )
                    columns.append(jnp.concatenate(column, axis=0))
                s = jnp.concatenate(columns, axis=1)
                new_m = jnp.maximum(m, jnp.max(s, axis=1, keepdims=True) * TO_LOG2)
                factor = jnp.exp2(m - new_m)
                p = jnp.exp2(s * TO_LOG2 - jnp.concatenate([new_m] * (KEY_TILE // HEAD_DIM), axis=1))
                added = jnp.dot(
                    p.astype(jnp.bfloat16), v_wide[keys, :], preferred_element_type=jnp.float32
                )
                acc = acc * jnp.concatenate([factor] * 2, axis=1) + added
                m = new_m
            m_out[rows, :] = m
            a_out[rows, :] = acc


def fold(info, key_base, q_parts, parts, kv, state, weight=46):
    tok = q_parts[0].shape[0]
    first = state is None
    count = len(parts)
    shapes = [
        pltpu.VMEM((4 * tok, HEAD_DIM), jnp.float32),
        pltpu.VMEM((4 * tok, 2 * HEAD_DIM), jnp.float32),
    ]
    return pl.pallas_call(
        functools.partial(fold_kernel, first, parts),
        out_shape=shapes,
        in_specs=[smem_spec()] * 2 + [vmem_spec()] * (count + (1 if first else 3)),
        out_specs=[vmem_spec()] * 2,
        scratch_shapes=[
            pltpu.VMEM((tok, 2 * HEAD_DIM), jnp.bfloat16),
            pltpu.VMEM((count, tok, HEAD_DIM), jnp.bfloat16),
        ],
        input_output_aliases={} if first else {count + 3: 0, count + 4: 1},
        compiler_params=pltpu.CompilerParams(vmem_limit_bytes=VMEM_LIMIT),
        cost_estimate=pl.CostEstimate(
            flops=weight * tok * tok * HEAD_DIM, bytes_accessed=10**6, transcendentals=2 * tok * tok
        ),
        name="fold",
    )(info, key_base, *[q_parts[p] for p in parts], kv, *(() if first else state))


def diagonal():
    row = lax.broadcasted_iota(jnp.int32, (BLOCK, BLOCK), 0)
    return row == lax.broadcasted_iota(jnp.int32, (BLOCK, BLOCK), 1)


def pack(out_ref, out, log_sum):
    tok = out.shape[0]
    blocks = tok // BLOCK
    on = diagonal()
    rows = [
        jnp.sum(jnp.where(on, log_sum[i * BLOCK : (i + 1) * BLOCK, :], 0.0), axis=0, keepdims=True)
        for i in range(blocks)
    ]
    rest = jnp.concatenate(rows, axis=0)
    out_ref[:tok, :] = out.astype(jnp.bfloat16)
    for k in range(3):
        piece = rest.astype(jnp.bfloat16)
        rest = rest - piece.astype(jnp.float32)
        both = jnp.concatenate([piece.astype(jnp.float32), jnp.zeros((blocks, BLOCK), jnp.float32)])
        out_ref[tok + 2 * blocks * k : tok + 2 * blocks * (k + 1), :] = both.astype(jnp.bfloat16)


def unpack(ref, tok):
    blocks = tok // BLOCK
    on = diagonal()
    tail = ref[tok:, :].astype(jnp.float32)
    log_rows = sum(tail[2 * blocks * k : 2 * blocks * k + blocks, :] for k in range(3))
    columns = [
        jnp.sum(jnp.where(on, log_rows[i : i + 1, :], 0.0), axis=1, keepdims=True)
        for i in range(blocks)
    ]
    return ref[:tok, :].astype(jnp.float32), jnp.concatenate(columns, axis=0)


def packed_shape(tok):
    return jax.ShapeDtypeStruct((tok + 6 * (tok // BLOCK), HEAD_DIM), jnp.bfloat16)


def own_part(m_ref, a_ref, rows):
    return m_ref[rows, :], a_ref[rows, :HEAD_DIM], a_ref[rows, HEAD_DIM:]


def pack_state(out_ref, m, num, den):
    some = den > 0.0
    safe = jnp.where(some, den, 1.0)
    pack(out_ref, num / safe, jnp.where(some, m + jnp.log2(safe), START))


def mix(m, num, den, out, log_sum):
    top = jnp.maximum(m, log_sum)
    here = jnp.exp2(m - top)
    there = jnp.exp2(log_sum - top)
    return top, num * here + out * there, den * here + there * (log_sum > 0.5 * START)


def leave_kernel(tok, part, m_ref, a_ref, out_ref):
    pack_state(out_ref, *own_part(m_ref, a_ref, slice(part * tok, (part + 1) * tok)))


def pass_on_kernel(tok, part, m_ref, a_ref, other, out_ref):
    state = own_part(m_ref, a_ref, slice(part * tok, (part + 1) * tok))
    pack_state(out_ref, *mix(*state, *unpack(other, tok)))


def join_kernel(tok, m_ref, a_ref, other, back, out_ref):
    state = mix(*own_part(m_ref, a_ref, slice(0, tok)), *unpack(other, tok))
    _, num, den = mix(*state, *unpack(back, tok))
    out_ref[...] = (num / den).astype(jnp.bfloat16)


def small_call(kernel, name, out_shape, *args):
    return pl.pallas_call(
        kernel,
        out_shape=out_shape,
        in_specs=[vmem_spec()] * len(args),
        out_specs=vmem_spec(),
        compiler_params=pltpu.CompilerParams(vmem_limit_bytes=VMEM_LIMIT),
        name=name,
    )(*args)


def project_kernel(heads, own, left, right, far_a, far_b, weight, out_ref, lhs):
    step = pl.program_id(0)
    h = heads[0]
    count = weight.shape[0] // HEAD_DIM
    height = out_ref.shape[0]
    rows = pl.ds(pl.multiple_of(step * height, height), height)
    half = pl.num_programs(0) // 2

    def put(by, piece):
        column = pl.multiple_of(lax.rem(h + by, count) * HEAD_DIM, HEAD_DIM)
        lhs[:, pl.ds(column, HEAD_DIM)] = piece

    put(0, own[rows, :])
    put(count - 1, left[rows, :])
    put(1, right[rows, :])

    @pl.when(step < half)
    def _():
        put(2, far_a[rows, :])

    @pl.when(step >= half)
    def _():
        put(2, far_b[pl.ds(pl.multiple_of((step - half) * height, height), height), :])

    out_ref[...] = jnp.dot(
        lhs[...], weight[...], preferred_element_type=jnp.float32
    ).astype(jnp.bfloat16)


def project(heads, pieces, weight):
    tok = pieces[0].shape[0]
    width = weight.shape[1]
    height = tok // 4
    return pl.pallas_call(
        project_kernel,
        grid=(4,),
        out_shape=jax.ShapeDtypeStruct((tok, width), jnp.bfloat16),
        in_specs=[smem_spec()] + [vmem_spec()] * 6,
        out_specs=pl.BlockSpec((height, width), lambda i: (i, 0)),
        scratch_shapes=[pltpu.VMEM((height, weight.shape[0]), jnp.bfloat16)],
        compiler_params=pltpu.CompilerParams(vmem_limit_bytes=VMEM_LIMIT),
        name="project",
    )(heads, *pieces, weight)


def shards(queries, key_states, value_states, clip_lengths, out_weight):
    tok = queries.shape[0]
    blocks = tok // BLOCK
    ctx_count = lax.axis_size("ctx")
    head_count = lax.axis_size("head")
    ring = 2 * RING_CHIPS
    me = lax.axis_index("ctx")
    core = me % 2
    first_of_ring = me // ring * ring
    place = (me % ring) // 2
    head = lax.axis_index("head")

    def send(value, target):
        return lax.ppermute(value, "ctx", [(i, target(i)) for i in range(ctx_count)])

    def sibling(i):
        return i ^ 1

    def along(i):
        at = i % ring
        by = 2 if i % 2 == 0 else -2
        return i - at + (at + by) % ring

    def after(value, state):
        value, m = lax.optimization_barrier((value, state[0]))
        return value, (m, state[1])

    def up(i):
        return (i + ring) % ctx_count

    def down(i):
        return (i - ring) % ctx_count

    def turn(value, by):
        pairs = [(i, (i + by) % head_count) for i in range(head_count)]
        return lax.ppermute(value, "head", pairs)

    kv = jnp.stack([key_states, value_states])
    near = send(kv, along)
    cross = send(kv, lambda i: along(sibling(i)))
    next_own = send(queries, down)
    q_sibling = send(queries, sibling)

    upto = jnp.arange(clip_lengths.shape[0])
    ends = jnp.sum(jnp.where(upto[None, :] <= upto[:, None], clip_lengths[None, :], 0), axis=1)
    owners = jnp.stack([me, me ^ 1, (me + ring) % ctx_count, ((me + ring) % ctx_count) ^ 1])
    bases = owners * blocks
    q_blocks = bases[:, None] + jnp.arange(blocks, dtype=jnp.int32)[None, :]
    begin = jnp.max(
        jnp.where(ends[None, None, :] <= q_blocks[:, :, None], ends[None, None, :], 0), axis=-1
    )
    info = jnp.concatenate([bases, begin.reshape(-1)]).astype(jnp.int32)

    def base_of(step, of_core):
        chip = (place + jnp.where(core == 0, -step, step)) % RING_CHIPS
        return ((first_of_ring + 2 * chip + of_core) * blocks).reshape(1).astype(jnp.int32)

    order = []
    for step in range(1, RING_CHIPS // 2 + 1):
        order += [(step, core), (step, 1 - core)]
    order = order[:-1]
    arrived = [near, cross]
    everyone = (0, 1, 2, 3)
    own_base = base_of(0, core)
    state = fold(info, own_base, (queries,), (0,), kv, None, 4)
    state = fold(info, own_base, (queries, q_sibling), (1,), kv, state, 4)
    q_parts = (queries, q_sibling, next_own, send(queries, lambda i: sibling(down(i))))
    for n, (step, of_core) in enumerate(order):
        value = arrived[n]
        if n + 2 < len(order):
            value, state = after(value, state)
            arrived.append(send(value, along))
        if n == len(order) - 1:
            state = fold(info, own_base, q_parts, (2, 3), kv, state)
        state = fold(
            info, base_of(step, of_core), q_parts, everyone, value, state, 46 if n else 8
        )

    packed = packed_shape(tok)
    leave = functools.partial(leave_kernel, tok)
    next_there = send(small_call(functools.partial(leave, 3), "leave_next", packed, *state), sibling)
    own_there = send(small_call(functools.partial(leave, 1), "leave_own", packed, *state), sibling)
    passed = small_call(
        functools.partial(pass_on_kernel, tok, 2), "pass_on", packed, *state, next_there
    )
    back = send(passed, up)
    attended = small_call(
        functools.partial(join_kernel, tok),
        "join",
        jax.ShapeDtypeStruct((tok, HEAD_DIM), jnp.bfloat16),
        *state,
        own_there,
        back,
    )
    half = tok // 2
    left = turn(attended, 1)
    right = turn(attended, -1)
    far_a = turn(attended[:half], 2)
    far_b = turn(attended[half:], -2)
    return project(
        head.reshape(1).astype(jnp.int32), (attended, left, right, far_a, far_b), out_weight
    )


def solution(mesh):
    placed = (P("ctx", "head"), P("ctx", "head"), P("ctx", "head"), P(), P(None, "head"))
    return jax.shard_map(
        shards, mesh=mesh, in_specs=placed, out_specs=P("ctx", "head"), check_vma=False
    )
```

```python
import functools
import math

import jax
import jax.numpy as jnp
from jax import lax
from jax.experimental import pallas as pl
from jax.experimental.pallas import tpu as pltpu
from jax.sharding import PartitionSpec as P

HEAD_DIM = 128
BLOCK = 128
FAR = -1e30
START = -1e25
TO_LOG2 = math.log2(math.e) * HEAD_DIM**-0.5
VMEM_LIMIT = 16 * 2**20
KEY_TILE = 256
RING_CHIPS = 8


def vmem_spec():
    return pl.BlockSpec(memory_space=pltpu.VMEM)


def smem_spec():
    return pl.BlockSpec(memory_space=pltpu.SMEM)


def fold_kernel(first, parts, info, key_base, *refs):
    count = len(parts)
    q_refs, kv, refs = refs[:count], refs[count], refs[count + 1 :]
    if first:
        m_out, a_out, v_wide, q_all = refs
        m_in, a_in = m_out, a_out
        m_out[...] = jnp.full(m_out.shape, START, jnp.float32)
        a_out[...] = jnp.zeros(a_out.shape, jnp.float32)
    else:
        m_in, a_in, m_out, a_out, v_wide, q_all = refs
    tok = q_refs[0].shape[0]
    blocks = tok // BLOCK
    k_base = key_base[0]

    def wants(part):
        return (k_base + blocks > info[4 + part * blocks]) & (k_base < info[part] + blocks)

    any_wants = False
    for part, q_ref in zip(parts, q_refs):
        any_wants = any_wants | wants(part)

        @pl.when(wants(part))
        def _(part=part, q_ref=q_ref):
            q_all[part - parts[0]] = q_ref[...]

    @pl.when(any_wants)
    def _():
        v_wide[:, :HEAD_DIM] = kv[1]
        v_wide[:, HEAD_DIM:] = jnp.ones((tok, HEAD_DIM), jnp.bfloat16)

    @pl.loop(parts[0], parts[0] + count)
    def _(part):
        rows = pl.ds(pl.multiple_of(part * tok, tok), tok)
        q_base = info[part]
        begin = [info[4 + part * blocks + i] for i in range(blocks)]

        @pl.when(wants(part))
        def _():
            q = q_all[part - parts[0]]
            m = m_in[rows, :]
            acc = a_in[rows, :]
            for t in range(tok // KEY_TILE):
                keys = slice(t * KEY_TILE, (t + 1) * KEY_TILE)
                s = lax.dot_general(
                    q, kv[0, keys, :], (((1,), (1,)), ((), ())), preferred_element_type=jnp.float32
                )
                columns = []
                for j in range(KEY_TILE // BLOCK):
                    k_blk = k_base + t * (KEY_TILE // BLOCK) + j
                    column = []
                    for i in range(blocks):
                        seen = (k_blk >= begin[i]) & (k_blk <= q_base + i)
                        bias = jnp.where(seen, 0.0, FAR).astype(jnp.float32)
                        column.append(
                            s[i * BLOCK : (i + 1) * BLOCK, j * BLOCK : (j + 1) * BLOCK] + bias
                        )
                    columns.append(jnp.concatenate(column, axis=0))
                s = jnp.concatenate(columns, axis=1)
                new_m = jnp.maximum(m, jnp.max(s, axis=1, keepdims=True) * TO_LOG2)
                factor = jnp.exp2(m - new_m)
                p = jnp.exp2(s * TO_LOG2 - jnp.concatenate([new_m] * (KEY_TILE // HEAD_DIM), axis=1))
                added = jnp.dot(
                    p.astype(jnp.bfloat16), v_wide[keys, :], preferred_element_type=jnp.float32
                )
                acc = acc * jnp.concatenate([factor] * 2, axis=1) + added
                m = new_m
            m_out[rows, :] = m
            a_out[rows, :] = acc


def fold(info, key_base, q_parts, parts, kv, state, weight=46):
    tok = q_parts[0].shape[0]
    first = state is None
    count = len(parts)
    shapes = [
        pltpu.VMEM((4 * tok, HEAD_DIM), jnp.float32),
        pltpu.VMEM((4 * tok, 2 * HEAD_DIM), jnp.float32),
    ]
    return pl.pallas_call(
        functools.partial(fold_kernel, first, parts),
        out_shape=shapes,
        in_specs=[smem_spec()] * 2 + [vmem_spec()] * (count + (1 if first else 3)),
        out_specs=[vmem_spec()] * 2,
        scratch_shapes=[
            pltpu.VMEM((tok, 2 * HEAD_DIM), jnp.bfloat16),
            pltpu.VMEM((count, tok, HEAD_DIM), jnp.bfloat16),
        ],
        input_output_aliases={} if first else {count + 3: 0, count + 4: 1},
        compiler_params=pltpu.CompilerParams(vmem_limit_bytes=VMEM_LIMIT),
        cost_estimate=pl.CostEstimate(
            flops=weight * tok * tok * HEAD_DIM, bytes_accessed=10**6, transcendentals=2 * tok * tok
        ),
        name="fold",
    )(info, key_base, *[q_parts[p] for p in parts], kv, *(() if first else state))


def diagonal():
    row = lax.broadcasted_iota(jnp.int32, (BLOCK, BLOCK), 0)
    return row == lax.broadcasted_iota(jnp.int32, (BLOCK, BLOCK), 1)


def pack(out_ref, out, log_sum):
    tok = out.shape[0]
    blocks = tok // BLOCK
    on = diagonal()
    rows = [
        jnp.sum(jnp.where(on, log_sum[i * BLOCK : (i + 1) * BLOCK, :], 0.0), axis=0, keepdims=True)
        for i in range(blocks)
    ]
    rest = jnp.concatenate(rows, axis=0)
    out_ref[:tok, :] = out.astype(jnp.bfloat16)
    for k in range(3):
        piece = rest.astype(jnp.bfloat16)
        rest = rest - piece.astype(jnp.float32)
        both = jnp.concatenate([piece.astype(jnp.float32), jnp.zeros((blocks, BLOCK), jnp.float32)])
        out_ref[tok + 2 * blocks * k : tok + 2 * blocks * (k + 1), :] = both.astype(jnp.bfloat16)


def unpack(ref, tok):
    blocks = tok // BLOCK
    on = diagonal()
    tail = ref[tok:, :].astype(jnp.float32)
    log_rows = sum(tail[2 * blocks * k : 2 * blocks * k + blocks, :] for k in range(3))
    columns = [
        jnp.sum(jnp.where(on, log_rows[i : i + 1, :], 0.0), axis=1, keepdims=True)
        for i in range(blocks)
    ]
    return ref[:tok, :].astype(jnp.float32), jnp.concatenate(columns, axis=0)


def packed_shape(tok):
    return jax.ShapeDtypeStruct((tok + 6 * (tok // BLOCK), HEAD_DIM), jnp.bfloat16)


def own_part(m_ref, a_ref, rows):
    return m_ref[rows, :], a_ref[rows, :HEAD_DIM], a_ref[rows, HEAD_DIM:]


def pack_state(out_ref, m, num, den):
    some = den > 0.0
    safe = jnp.where(some, den, 1.0)
    pack(out_ref, num / safe, jnp.where(some, m + jnp.log2(safe), START))


def mix(m, num, den, out, log_sum):
    top = jnp.maximum(m, log_sum)
    here = jnp.exp2(m - top)
    there = jnp.exp2(log_sum - top)
    return top, num * here + out * there, den * here + there * (log_sum > 0.5 * START)


def leave_kernel(tok, part, m_ref, a_ref, out_ref):
    pack_state(out_ref, *own_part(m_ref, a_ref, slice(part * tok, (part + 1) * tok)))


def pass_on_kernel(tok, part, m_ref, a_ref, other, out_ref):
    state = own_part(m_ref, a_ref, slice(part * tok, (part + 1) * tok))
    pack_state(out_ref, *mix(*state, *unpack(other, tok)))


def join_kernel(tok, m_ref, a_ref, other, back, out_ref):
    state = mix(*own_part(m_ref, a_ref, slice(0, tok)), *unpack(other, tok))
    _, num, den = mix(*state, *unpack(back, tok))
    out_ref[...] = (num / den).astype(jnp.bfloat16)


def small_call(kernel, name, out_shape, *args):
    return pl.pallas_call(
        kernel,
        out_shape=out_shape,
        in_specs=[vmem_spec()] * len(args),
        out_specs=vmem_spec(),
        compiler_params=pltpu.CompilerParams(vmem_limit_bytes=VMEM_LIMIT),
        name=name,
    )(*args)


def project_kernel(heads, own, left, right, far, weight, out_ref, lhs):
    step = pl.program_id(0)
    h = heads[0]
    count = weight.shape[0] // HEAD_DIM
    width = out_ref.shape[1]

    @pl.when(step == 0)
    def _():
        for by, piece in ((0, own), (count - 1, left), (1, right), (2, far)):
            column = pl.multiple_of(lax.rem(h + by, count) * HEAD_DIM, HEAD_DIM)
            lhs[:, pl.ds(column, HEAD_DIM)] = piece[...]

    columns = pl.ds(pl.multiple_of(step * width, width), width)
    out_ref[...] = jnp.dot(
        lhs[...], weight[:, columns], preferred_element_type=jnp.float32
    ).astype(jnp.bfloat16)


def project(heads, pieces, weight):
    tok = pieces[0].shape[0]
    steps = 3
    width = weight.shape[1] // steps
    return pl.pallas_call(
        project_kernel,
        grid=(steps,),
        out_shape=jax.ShapeDtypeStruct((tok, weight.shape[1]), jnp.bfloat16),
        in_specs=[smem_spec()] + [vmem_spec()] * 5,
        out_specs=pl.BlockSpec((tok, width), lambda i: (0, i)),
        scratch_shapes=[pltpu.VMEM((tok, weight.shape[0]), jnp.bfloat16)],
        compiler_params=pltpu.CompilerParams(vmem_limit_bytes=VMEM_LIMIT),
        name="project",
    )(heads, *pieces, weight)


def shards(queries, key_states, value_states, clip_lengths, out_weight):
    tok = queries.shape[0]
    blocks = tok // BLOCK
    ctx_count = lax.axis_size("ctx")
    head_count = lax.axis_size("head")
    ring = 2 * RING_CHIPS
    me = lax.axis_index("ctx")
    core = me % 2
    first_of_ring = me // ring * ring
    place = (me % ring) // 2
    head = lax.axis_index("head")

    def send(value, target):
        return lax.ppermute(value, "ctx", [(i, target(i)) for i in range(ctx_count)])

    def sibling(i):
        return i ^ 1

    def along(i):
        at = i % ring
        by = 2 if i % 2 == 0 else -2
        return i - at + (at + by) % ring

    def after(value, state):
        value, m = lax.optimization_barrier((value, state[0]))
        return value, (m, state[1])

    def up(i):
        return (i + ring) % ctx_count

    def down(i):
        return (i - ring) % ctx_count

    def turn(value, by):
        pairs = [(i, (i + by) % head_count) for i in range(head_count)]
        return lax.ppermute(value, "head", pairs)

    kv = jnp.stack([key_states, value_states])
    near = send(kv, along)
    cross = send(kv, lambda i: along(sibling(i)))
    next_own = send(queries, down)
    q_sibling = send(queries, sibling)

    upto = jnp.arange(clip_lengths.shape[0])
    ends = jnp.sum(jnp.where(upto[None, :] <= upto[:, None], clip_lengths[None, :], 0), axis=1)
    owners = jnp.stack([me, me ^ 1, (me + ring) % ctx_count, ((me + ring) % ctx_count) ^ 1])
    bases = owners * blocks
    q_blocks = bases[:, None] + jnp.arange(blocks, dtype=jnp.int32)[None, :]
    begin = jnp.max(
        jnp.where(ends[None, None, :] <= q_blocks[:, :, None], ends[None, None, :], 0), axis=-1
    )
    info = jnp.concatenate([bases, begin.reshape(-1)]).astype(jnp.int32)

    def base_of(step, of_core):
        chip = (place + jnp.where(core == 0, -step, step)) % RING_CHIPS
        return ((first_of_ring + 2 * chip + of_core) * blocks).reshape(1).astype(jnp.int32)

    order = []
    for step in range(1, RING_CHIPS // 2 + 1):
        order += [(step, core), (step, 1 - core)]
    order = order[:-1]
    arrived = [near, cross]
    everyone = (0, 1, 2, 3)
    own_base = base_of(0, core)
    state = fold(info, own_base, (queries,), (0,), kv, None, 4)
    state = fold(info, own_base, (queries, q_sibling), (1,), kv, state, 4)
    q_parts = (queries, q_sibling, next_own, send(queries, lambda i: sibling(down(i))))
    for n, (step, of_core) in enumerate(order):
        value = arrived[n]
        if n + 2 < len(order):
            value, state = after(value, state)
            arrived.append(send(value, along))
        if n == len(order) - 1:
            state = fold(info, own_base, q_parts, (2, 3), kv, state)
        state = fold(
            info, base_of(step, of_core), q_parts, everyone, value, state, 46 if n else 8
        )

    packed = packed_shape(tok)
    leave = functools.partial(leave_kernel, tok)
    next_there = send(small_call(functools.partial(leave, 3), "leave_next", packed, *state), sibling)
    own_there = send(small_call(functools.partial(leave, 1), "leave_own", packed, *state), sibling)
    passed = small_call(
        functools.partial(pass_on_kernel, tok, 2), "pass_on", packed, *state, next_there
    )
    back = send(passed, up)
    attended = small_call(
        functools.partial(join_kernel, tok),
        "join",
        jax.ShapeDtypeStruct((tok, HEAD_DIM), jnp.bfloat16),
        *state,
        own_there,
        back,
    )
    pieces = (attended, turn(attended, 1), turn(attended, -1), turn(attended, 2))
    return project(head.reshape(1).astype(jnp.int32), pieces, out_weight)


def solution(mesh):
    placed = (P("ctx", "head"), P("ctx", "head"), P("ctx", "head"), P(), P(None, "head"))
    return jax.shard_map(
        shards, mesh=mesh, in_specs=placed, out_specs=P("ctx", "head"), check_vma=False
    )
```

```python
import functools
import math

import jax
import jax.numpy as jnp
from jax import lax
from jax.experimental import pallas as pl
from jax.experimental.pallas import tpu as pltpu
from jax.sharding import PartitionSpec as P

HEAD_DIM = 128
BLOCK = 128
FAR = -1e30
START = -1e25
TO_LOG2 = math.log2(math.e) * HEAD_DIM**-0.5
VMEM_LIMIT = 16 * 2**20
RING_CHIPS = 8


def vmem_spec():
    return pl.BlockSpec(memory_space=pltpu.VMEM)


def smem_spec():
    return pl.BlockSpec(memory_space=pltpu.SMEM)


def fold_kernel(first, parts, info, key_base, *refs):
    count = len(parts)
    q_refs, kv, refs = refs[:count], refs[count], refs[count + 1 :]
    if first:
        m_out, a_out, v_wide, q_all = refs
        m_in, a_in = m_out, a_out
        m_out[...] = jnp.full(m_out.shape, START, jnp.float32)
        a_out[...] = jnp.zeros(a_out.shape, jnp.float32)
    else:
        m_in, a_in, m_out, a_out, v_wide, q_all = refs
    tok = q_refs[0].shape[0]
    blocks = tok // BLOCK
    k_base = key_base[0]

    def wants(part):
        return (k_base + blocks > info[4 + part * blocks]) & (k_base < info[part] + blocks)

    any_wants = False
    for part, q_ref in zip(parts, q_refs):
        any_wants = any_wants | wants(part)

        @pl.when(wants(part))
        def _(part=part, q_ref=q_ref):
            q_all[part - parts[0]] = q_ref[...]

    @pl.when(any_wants)
    def _():
        v_wide[:, :HEAD_DIM] = kv[1]
        v_wide[:, HEAD_DIM:] = jnp.ones((tok, HEAD_DIM), jnp.bfloat16)

    @pl.loop(parts[0], parts[0] + count)
    def _(part):
        q_base = info[part]
        begin = [info[4 + part * blocks + i] for i in range(blocks)]

        @pl.when(wants(part))
        def _():
            half = tok // 2
            both = (slice(0, half), slice(half, tok))

            def score(rows_in):
                return lax.dot_general(
                    q_all[part - parts[0], rows_in, :],
                    kv[0],
                    (((1,), (1,)), ((), ())),
                    preferred_element_type=jnp.float32,
                )

            scores = [score(rows_in) for rows_in in both]
            for n, s in enumerate(scores):
                rows_here = pl.ds(pl.multiple_of(part * tok + n * half, half), half)
                columns = []
                for j in range(blocks):
                    column = []
                    for i in range(blocks // 2):
                        i_all = n * (blocks // 2) + i
                        seen = (k_base + j >= begin[i_all]) & (k_base + j <= q_base + i_all)
                        bias = jnp.where(seen, 0.0, FAR).astype(jnp.float32)
                        column.append(
                            s[i * BLOCK : (i + 1) * BLOCK, j * BLOCK : (j + 1) * BLOCK] + bias
                        )
                    columns.append(jnp.concatenate(column, axis=0))
                s = jnp.concatenate(columns, axis=1)
                m = m_in[rows_here, :]
                new_m = jnp.maximum(m, jnp.max(s, axis=1, keepdims=True) * TO_LOG2)
                factor = jnp.exp2(m - new_m)
                p = jnp.exp2(s * TO_LOG2 - jnp.concatenate([new_m] * blocks, axis=1))
                added = jnp.dot(
                    p.astype(jnp.bfloat16), v_wide[...], preferred_element_type=jnp.float32
                )
                a_out[rows_here, :] = (
                    a_in[rows_here, :] * jnp.concatenate([factor] * 2, axis=1) + added
                )
                m_out[rows_here, :] = new_m


def fold(info, key_base, q_parts, parts, kv, state, weight=46):
    tok = q_parts[0].shape[0]
    first = state is None
    count = len(parts)
    shapes = [
        pltpu.VMEM((4 * tok, HEAD_DIM), jnp.float32),
        pltpu.VMEM((4 * tok, 2 * HEAD_DIM), jnp.float32),
    ]
    return pl.pallas_call(
        functools.partial(fold_kernel, first, parts),
        out_shape=shapes,
        in_specs=[smem_spec()] * 2 + [vmem_spec()] * (count + (1 if first else 3)),
        out_specs=[vmem_spec()] * 2,
        scratch_shapes=[
            pltpu.VMEM((tok, 2 * HEAD_DIM), jnp.bfloat16),
            pltpu.VMEM((count, tok, HEAD_DIM), jnp.bfloat16),
        ],
        input_output_aliases={} if first else {count + 3: 0, count + 4: 1},
        compiler_params=pltpu.CompilerParams(vmem_limit_bytes=VMEM_LIMIT),
        cost_estimate=pl.CostEstimate(
            flops=weight * tok * tok * HEAD_DIM, bytes_accessed=10**6, transcendentals=2 * tok * tok
        ),
        name="fold",
    )(info, key_base, *[q_parts[p] for p in parts], kv, *(() if first else state))


def diagonal():
    row = lax.broadcasted_iota(jnp.int32, (BLOCK, BLOCK), 0)
    return row == lax.broadcasted_iota(jnp.int32, (BLOCK, BLOCK), 1)


def pack(out_ref, out, log_sum):
    tok = out.shape[0]
    blocks = tok // BLOCK
    on = diagonal()
    rows = [
        jnp.sum(jnp.where(on, log_sum[i * BLOCK : (i + 1) * BLOCK, :], 0.0), axis=0, keepdims=True)
        for i in range(blocks)
    ]
    rest = jnp.concatenate(rows, axis=0)
    out_ref[:tok, :] = out.astype(jnp.bfloat16)
    for k in range(3):
        piece = rest.astype(jnp.bfloat16)
        rest = rest - piece.astype(jnp.float32)
        both = jnp.concatenate([piece.astype(jnp.float32), jnp.zeros((blocks, BLOCK), jnp.float32)])
        out_ref[tok + 2 * blocks * k : tok + 2 * blocks * (k + 1), :] = both.astype(jnp.bfloat16)


def unpack(ref, tok):
    blocks = tok // BLOCK
    on = diagonal()
    tail = ref[tok:, :].astype(jnp.float32)
    log_rows = sum(tail[2 * blocks * k : 2 * blocks * k + blocks, :] for k in range(3))
    columns = [
        jnp.sum(jnp.where(on, log_rows[i : i + 1, :], 0.0), axis=1, keepdims=True)
        for i in range(blocks)
    ]
    return ref[:tok, :].astype(jnp.float32), jnp.concatenate(columns, axis=0)


def packed_shape(tok):
    return jax.ShapeDtypeStruct((tok + 6 * (tok // BLOCK), HEAD_DIM), jnp.bfloat16)


def own_part(m_ref, a_ref, rows):
    return m_ref[rows, :], a_ref[rows, :HEAD_DIM], a_ref[rows, HEAD_DIM:]


def pack_state(out_ref, m, num, den):
    some = den > 0.0
    safe = jnp.where(some, den, 1.0)
    pack(out_ref, num / safe, jnp.where(some, m + jnp.log2(safe), START))


def mix(m, num, den, out, log_sum):
    top = jnp.maximum(m, log_sum)
    here = jnp.exp2(m - top)
    there = jnp.exp2(log_sum - top)
    return top, num * here + out * there, den * here + there * (log_sum > 0.5 * START)


def leave_kernel(tok, part, m_ref, a_ref, out_ref):
    pack_state(out_ref, *own_part(m_ref, a_ref, slice(part * tok, (part + 1) * tok)))


def pass_on_kernel(tok, part, m_ref, a_ref, other, out_ref):
    state = own_part(m_ref, a_ref, slice(part * tok, (part + 1) * tok))
    pack_state(out_ref, *mix(*state, *unpack(other, tok)))


def join_kernel(tok, m_ref, a_ref, other, back, out_ref):
    state = mix(*own_part(m_ref, a_ref, slice(0, tok)), *unpack(other, tok))
    _, num, den = mix(*state, *unpack(back, tok))
    out_ref[...] = (num / den).astype(jnp.bfloat16)


def small_call(kernel, name, out_shape, *args):
    return pl.pallas_call(
        kernel,
        out_shape=out_shape,
        in_specs=[vmem_spec()] * len(args),
        out_specs=vmem_spec(),
        compiler_params=pltpu.CompilerParams(vmem_limit_bytes=VMEM_LIMIT),
        name=name,
    )(*args)


def project_kernel(heads, own, left, right, far_a, far_b, weight, out_ref, lhs):
    step = pl.program_id(0)
    h = heads[0]
    count = weight.shape[0] // HEAD_DIM
    width = out_ref.shape[1]

    @pl.when(step == 0)
    def _():
        half = far_a.shape[0]
        for by, piece, rows in (
            (0, own, slice(0, 2 * half)),
            (count - 1, left, slice(0, 2 * half)),
            (1, right, slice(0, 2 * half)),
            (2, far_a, slice(0, half)),
            (2, far_b, slice(half, 2 * half)),
        ):
            column = pl.multiple_of(lax.rem(h + by, count) * HEAD_DIM, HEAD_DIM)
            lhs[rows, pl.ds(column, HEAD_DIM)] = piece[...]

    columns = pl.ds(pl.multiple_of(step * width, width), width)
    out_ref[...] = jnp.dot(
        lhs[...], weight[:, columns], preferred_element_type=jnp.float32
    ).astype(jnp.bfloat16)


def project(heads, pieces, weight):
    tok = pieces[0].shape[0]
    steps = 3
    width = weight.shape[1] // steps
    return pl.pallas_call(
        project_kernel,
        grid=(steps,),
        out_shape=jax.ShapeDtypeStruct((tok, weight.shape[1]), jnp.bfloat16),
        in_specs=[smem_spec()] + [vmem_spec()] * 6,
        out_specs=pl.BlockSpec((tok, width), lambda i: (0, i)),
        scratch_shapes=[pltpu.VMEM((tok, weight.shape[0]), jnp.bfloat16)],
        compiler_params=pltpu.CompilerParams(vmem_limit_bytes=VMEM_LIMIT),
        name="project",
    )(heads, *pieces, weight)


def shards(queries, key_states, value_states, clip_lengths, out_weight):
    tok = queries.shape[0]
    blocks = tok // BLOCK
    ctx_count = lax.axis_size("ctx")
    head_count = lax.axis_size("head")
    ring = 2 * RING_CHIPS
    me = lax.axis_index("ctx")
    core = me % 2
    first_of_ring = me // ring * ring
    place = (me % ring) // 2
    head = lax.axis_index("head")

    def send(value, target):
        return lax.ppermute(value, "ctx", [(i, target(i)) for i in range(ctx_count)])

    def sibling(i):
        return i ^ 1

    def along(i):
        at = i % ring
        by = 2 if i % 2 == 0 else -2
        return i - at + (at + by) % ring

    def after(value, state):
        value, m = lax.optimization_barrier((value, state[0]))
        return value, (m, state[1])

    def up(i):
        return (i + ring) % ctx_count

    def down(i):
        return (i - ring) % ctx_count

    def turn(value, by):
        pairs = [(i, (i + by) % head_count) for i in range(head_count)]
        return lax.ppermute(value, "head", pairs)

    upto = jnp.arange(clip_lengths.shape[0])
    ends = jnp.sum(jnp.where(upto[None, :] <= upto[:, None], clip_lengths[None, :], 0), axis=1)
    owners = jnp.stack([me, me ^ 1, (me + ring) % ctx_count, ((me + ring) % ctx_count) ^ 1])
    bases = owners * blocks
    q_blocks = bases[:, None] + jnp.arange(blocks, dtype=jnp.int32)[None, :]
    begin = jnp.max(
        jnp.where(ends[None, None, :] <= q_blocks[:, :, None], ends[None, None, :], 0), axis=-1
    )
    info = jnp.concatenate([bases, begin.reshape(-1)]).astype(jnp.int32)

    kv = jnp.stack([key_states, value_states])
    near = send(kv, along)
    kv, info = lax.optimization_barrier((kv, info))
    cross = send(kv, lambda i: along(sibling(i)))
    next_own = send(queries, down)
    q_sibling = send(queries, sibling)

    def base_of(step, of_core):
        chip = (place + jnp.where(core == 0, -step, step)) % RING_CHIPS
        return ((first_of_ring + 2 * chip + of_core) * blocks).reshape(1).astype(jnp.int32)

    order = []
    for step in range(1, RING_CHIPS // 2 + 1):
        order += [(step, core), (step, 1 - core)]
    order = order[:-1]
    arrived = [near, cross]
    everyone = (0, 1, 2, 3)
    own_base = base_of(0, core)
    state = fold(info, own_base, (queries,), (0,), kv, None, 4)
    state = fold(info, own_base, (queries, q_sibling), (1,), kv, state, 4)
    q_parts = (queries, q_sibling, next_own, send(queries, lambda i: sibling(down(i))))
    for n, (step, of_core) in enumerate(order):
        value = arrived[n]
        if n + 2 < len(order):
            value, state = after(value, state)
            arrived.append(send(value, along))
        if n == len(order) - 1:
            state = fold(info, own_base, q_parts, (2, 3), kv, state)
        state = fold(
            info, base_of(step, of_core), q_parts, everyone, value, state, 46 if n else 8
        )

    packed = packed_shape(tok)
    leave = functools.partial(leave_kernel, tok)
    next_there = send(small_call(functools.partial(leave, 3), "leave_next", packed, *state), sibling)
    own_there = send(small_call(functools.partial(leave, 1), "leave_own", packed, *state), sibling)
    passed = small_call(
        functools.partial(pass_on_kernel, tok, 2), "pass_on", packed, *state, next_there
    )
    back = send(passed, up)
    attended = small_call(
        functools.partial(join_kernel, tok),
        "join",
        jax.ShapeDtypeStruct((tok, HEAD_DIM), jnp.bfloat16),
        *state,
        own_there,
        back,
    )
    half = tok // 2
    pieces = (
        attended,
        turn(attended, 1),
        turn(attended, -1),
        turn(attended[:half], 2),
        turn(attended[half:], -2),
    )
    return project(head.reshape(1).astype(jnp.int32), pieces, out_weight)


def solution(mesh):
    placed = (P("ctx", "head"), P("ctx", "head"), P("ctx", "head"), P(), P(None, "head"))
    return jax.shard_map(
        shards, mesh=mesh, in_specs=placed, out_specs=P("ctx", "head"), check_vma=False
    )
```

```python
import functools
import math

import jax
import jax.numpy as jnp
from jax import lax
from jax.experimental import pallas as pl
from jax.experimental.pallas import tpu as pltpu
from jax.sharding import PartitionSpec as P

HEAD_DIM = 128
BLOCK = 128
FAR = -1e30
START = -1e25
TO_LOG2 = math.log2(math.e) * HEAD_DIM**-0.5
VMEM_LIMIT = 16 * 2**20
RING_CHIPS = 8


def vmem_spec():
    return pl.BlockSpec(memory_space=pltpu.VMEM)


def smem_spec():
    return pl.BlockSpec(memory_space=pltpu.SMEM)


def fold_kernel(first, parts, info, key_base, *refs):
    count = len(parts)
    q_refs, kv, refs = refs[:count], refs[count], refs[count + 1 :]
    if first:
        m_out, a_out, v_wide, q_all = refs
        m_in, a_in = m_out, a_out
        m_out[...] = jnp.full(m_out.shape, START, jnp.float32)
        a_out[...] = jnp.zeros(a_out.shape, jnp.float32)
    else:
        m_in, a_in, m_out, a_out, v_wide, q_all = refs
    tok = q_refs[0].shape[0]
    blocks = tok // BLOCK
    k_base = key_base[0]

    def wants(part):
        return (k_base + blocks > info[4 + part * blocks]) & (k_base < info[part] + blocks)

    any_wants = False
    for part, q_ref in zip(parts, q_refs):
        any_wants = any_wants | wants(part)

        @pl.when(wants(part))
        def _(part=part, q_ref=q_ref):
            q_all[part - parts[0]] = q_ref[...]

    @pl.when(any_wants)
    def _():
        v_wide[:, :HEAD_DIM] = kv[1]
        v_wide[:, HEAD_DIM:] = jnp.ones((tok, HEAD_DIM), jnp.bfloat16)

    @pl.loop(parts[0], parts[0] + count)
    def _(part):
        q_base = info[part]
        begin = [info[4 + part * blocks + i] for i in range(blocks)]

        @pl.when(wants(part))
        def _():
            half = tok // 2
            both = (slice(0, half), slice(half, tok))

            def score(rows_in):
                return lax.dot_general(
                    q_all[part - parts[0], rows_in, :],
                    kv[0],
                    (((1,), (1,)), ((), ())),
                    preferred_element_type=jnp.float32,
                )

            scores = [score(rows_in) for rows_in in both]
            for n, s in enumerate(scores):
                rows_here = pl.ds(pl.multiple_of(part * tok + n * half, half), half)
                columns = []
                for j in range(blocks):
                    column = []
                    for i in range(blocks // 2):
                        i_all = n * (blocks // 2) + i
                        seen = (k_base + j >= begin[i_all]) & (k_base + j <= q_base + i_all)
                        bias = jnp.where(seen, 0.0, FAR).astype(jnp.float32)
                        column.append(
                            s[i * BLOCK : (i + 1) * BLOCK, j * BLOCK : (j + 1) * BLOCK] + bias
                        )
                    columns.append(jnp.concatenate(column, axis=0))
                s = jnp.concatenate(columns, axis=1)
                m = m_in[rows_here, :]
                new_m = jnp.maximum(m, jnp.max(s, axis=1, keepdims=True) * TO_LOG2)
                factor = jnp.exp2(m - new_m)
                p = jnp.exp2(s * TO_LOG2 - jnp.concatenate([new_m] * blocks, axis=1))
                added = jnp.dot(
                    p.astype(jnp.bfloat16), v_wide[...], preferred_element_type=jnp.float32
                )
                a_out[rows_here, :] = (
                    a_in[rows_here, :] * jnp.concatenate([factor] * 2, axis=1) + added
                )
                m_out[rows_here, :] = new_m


def fold(info, key_base, q_parts, parts, kv, state, weight=46):
    tok = q_parts[0].shape[0]
    first = state is None
    count = len(parts)
    shapes = [
        pltpu.VMEM((4 * tok, HEAD_DIM), jnp.float32),
        pltpu.VMEM((4 * tok, 2 * HEAD_DIM), jnp.float32),
    ]
    return pl.pallas_call(
        functools.partial(fold_kernel, first, parts),
        out_shape=shapes,
        in_specs=[smem_spec()] * 2 + [vmem_spec()] * (count + (1 if first else 3)),
        out_specs=[vmem_spec()] * 2,
        scratch_shapes=[
            pltpu.VMEM((tok, 2 * HEAD_DIM), jnp.bfloat16),
            pltpu.VMEM((count, tok, HEAD_DIM), jnp.bfloat16),
        ],
        input_output_aliases={} if first else {count + 3: 0, count + 4: 1},
        compiler_params=pltpu.CompilerParams(vmem_limit_bytes=VMEM_LIMIT),
        cost_estimate=pl.CostEstimate(
            flops=weight * tok * tok * HEAD_DIM, bytes_accessed=10**6, transcendentals=2 * tok * tok
        ),
        name="fold",
    )(info, key_base, *[q_parts[p] for p in parts], kv, *(() if first else state))


def diagonal():
    row = lax.broadcasted_iota(jnp.int32, (BLOCK, BLOCK), 0)
    return row == lax.broadcasted_iota(jnp.int32, (BLOCK, BLOCK), 1)


def pack(out_ref, out, log_sum):
    tok = out.shape[0]
    blocks = tok // BLOCK
    on = diagonal()
    rows = [
        jnp.sum(jnp.where(on, log_sum[i * BLOCK : (i + 1) * BLOCK, :], 0.0), axis=0, keepdims=True)
        for i in range(blocks)
    ]
    rest = jnp.concatenate(rows, axis=0)
    out_ref[:tok, :] = out.astype(jnp.bfloat16)
    for k in range(3):
        piece = rest.astype(jnp.bfloat16)
        rest = rest - piece.astype(jnp.float32)
        both = jnp.concatenate([piece.astype(jnp.float32), jnp.zeros((blocks, BLOCK), jnp.float32)])
        out_ref[tok + 2 * blocks * k : tok + 2 * blocks * (k + 1), :] = both.astype(jnp.bfloat16)


def unpack(ref, tok):
    blocks = tok // BLOCK
    on = diagonal()
    tail = ref[tok:, :].astype(jnp.float32)
    log_rows = sum(tail[2 * blocks * k : 2 * blocks * k + blocks, :] for k in range(3))
    columns = [
        jnp.sum(jnp.where(on, log_rows[i : i + 1, :], 0.0), axis=1, keepdims=True)
        for i in range(blocks)
    ]
    return ref[:tok, :].astype(jnp.float32), jnp.concatenate(columns, axis=0)


def packed_shape(tok):
    return jax.ShapeDtypeStruct((tok + 6 * (tok // BLOCK), HEAD_DIM), jnp.bfloat16)


def own_part(m_ref, a_ref, rows):
    return m_ref[rows, :], a_ref[rows, :HEAD_DIM], a_ref[rows, HEAD_DIM:]


def pack_state(out_ref, m, num, den):
    some = den > 0.0
    safe = jnp.where(some, den, 1.0)
    pack(out_ref, num / safe, jnp.where(some, m + jnp.log2(safe), START))


def mix(m, num, den, out, log_sum):
    top = jnp.maximum(m, log_sum)
    here = jnp.exp2(m - top)
    there = jnp.exp2(log_sum - top)
    return top, num * here + out * there, den * here + there * (log_sum > 0.5 * START)


def leave_kernel(tok, part, m_ref, a_ref, out_ref):
    pack_state(out_ref, *own_part(m_ref, a_ref, slice(part * tok, (part + 1) * tok)))


def pass_on_kernel(tok, part, m_ref, a_ref, other, out_ref):
    state = own_part(m_ref, a_ref, slice(part * tok, (part + 1) * tok))
    pack_state(out_ref, *mix(*state, *unpack(other, tok)))


def join_kernel(tok, m_ref, a_ref, other, back, out_ref):
    state = mix(*own_part(m_ref, a_ref, slice(0, tok)), *unpack(other, tok))
    _, num, den = mix(*state, *unpack(back, tok))
    out_ref[...] = (num / den).astype(jnp.bfloat16)


def small_call(kernel, name, out_shape, *args):
    return pl.pallas_call(
        kernel,
        out_shape=out_shape,
        in_specs=[vmem_spec()] * len(args),
        out_specs=vmem_spec(),
        compiler_params=pltpu.CompilerParams(vmem_limit_bytes=VMEM_LIMIT),
        name=name,
    )(*args)


def project_kernel(heads, own, left, right, far_a, far_b, weight, out_ref, lhs):
    step = pl.program_id(0)
    h = heads[0]
    count = weight.shape[0] // HEAD_DIM
    width = out_ref.shape[1]

    @pl.when(step == 0)
    def _():
        half = far_a.shape[0]
        for by, piece, rows in (
            (0, own, slice(0, 2 * half)),
            (count - 1, left, slice(0, 2 * half)),
            (1, right, slice(0, 2 * half)),
            (2, far_a, slice(0, half)),
            (2, far_b, slice(half, 2 * half)),
        ):
            column = pl.multiple_of(lax.rem(h + by, count) * HEAD_DIM, HEAD_DIM)
            lhs[rows, pl.ds(column, HEAD_DIM)] = piece[...]

    columns = pl.ds(pl.multiple_of(step * width, width), width)
    out_ref[...] = jnp.dot(
        lhs[...], weight[:, columns], preferred_element_type=jnp.float32
    ).astype(jnp.bfloat16)


def project(heads, pieces, weight):
    tok = pieces[0].shape[0]
    steps = 3
    width = weight.shape[1] // steps
    return pl.pallas_call(
        project_kernel,
        grid=(steps,),
        out_shape=jax.ShapeDtypeStruct((tok, weight.shape[1]), jnp.bfloat16),
        in_specs=[smem_spec()] + [vmem_spec()] * 6,
        out_specs=pl.BlockSpec((tok, width), lambda i: (0, i)),
        scratch_shapes=[pltpu.VMEM((tok, weight.shape[0]), jnp.bfloat16)],
        compiler_params=pltpu.CompilerParams(vmem_limit_bytes=VMEM_LIMIT),
        name="project",
    )(heads, *pieces, weight)


def shards(queries, key_states, value_states, clip_lengths, out_weight):
    tok = queries.shape[0]
    blocks = tok // BLOCK
    ctx_count = lax.axis_size("ctx")
    head_count = lax.axis_size("head")
    ring = 2 * RING_CHIPS
    me = lax.axis_index("ctx")
    core = me % 2
    first_of_ring = me // ring * ring
    place = (me % ring) // 2
    head = lax.axis_index("head")

    def send(value, target):
        return lax.ppermute(value, "ctx", [(i, target(i)) for i in range(ctx_count)])

    def sibling(i):
        return i ^ 1

    def along(i):
        at = i % ring
        by = 2 if i % 2 == 0 else -2
        return i - at + (at + by) % ring

    def after(value, state):
        value, m = lax.optimization_barrier((value, state[0]))
        return value, (m, state[1])

    def up(i):
        return (i + ring) % ctx_count

    def down(i):
        return (i - ring) % ctx_count

    def turn(value, by):
        pairs = [(i, (i + by) % head_count) for i in range(head_count)]
        return lax.ppermute(value, "head", pairs)

    kv = jnp.stack([key_states, value_states])
    near = send(kv, along)
    next_own = send(queries, down)
    q_sibling = send(queries, sibling)
    kv, q_sibling = lax.optimization_barrier((kv, q_sibling))
    cross = send(kv, lambda i: along(sibling(i)))

    upto = jnp.arange(clip_lengths.shape[0])
    ends = jnp.sum(jnp.where(upto[None, :] <= upto[:, None], clip_lengths[None, :], 0), axis=1)
    owners = jnp.stack([me, me ^ 1, (me + ring) % ctx_count, ((me + ring) % ctx_count) ^ 1])
    bases = owners * blocks
    q_blocks = bases[:, None] + jnp.arange(blocks, dtype=jnp.int32)[None, :]
    begin = jnp.max(
        jnp.where(ends[None, None, :] <= q_blocks[:, :, None], ends[None, None, :], 0), axis=-1
    )
    info = jnp.concatenate([bases, begin.reshape(-1)]).astype(jnp.int32)

    def base_of(step, of_core):
        chip = (place + jnp.where(core == 0, -step, step)) % RING_CHIPS
        return ((first_of_ring + 2 * chip + of_core) * blocks).reshape(1).astype(jnp.int32)

    order = []
    for step in range(1, RING_CHIPS // 2 + 1):
        order += [(step, core), (step, 1 - core)]
    order = order[:-1]
    arrived = [near, cross]
    everyone = (0, 1, 2, 3)
    own_base = base_of(0, core)
    state = fold(info, own_base, (queries,), (0,), kv, None, 4)
    state = fold(info, own_base, (queries, q_sibling), (1,), kv, state, 4)
    q_parts = (queries, q_sibling, next_own, send(queries, lambda i: sibling(down(i))))
    for n, (step, of_core) in enumerate(order):
        value = arrived[n]
        if n + 2 < len(order):
            value, state = after(value, state)
            arrived.append(send(value, along))
        if n == len(order) - 1:
            state = fold(info, own_base, q_parts, (2, 3), kv, state)
        state = fold(
            info, base_of(step, of_core), q_parts, everyone, value, state, 46 if n else 8
        )

    packed = packed_shape(tok)
    leave = functools.partial(leave_kernel, tok)
    next_there = send(small_call(functools.partial(leave, 3), "leave_next", packed, *state), sibling)
    own_there = send(small_call(functools.partial(leave, 1), "leave_own", packed, *state), sibling)
    passed = small_call(
        functools.partial(pass_on_kernel, tok, 2), "pass_on", packed, *state, next_there
    )
    back = send(passed, up)
    attended = small_call(
        functools.partial(join_kernel, tok),
        "join",
        jax.ShapeDtypeStruct((tok, HEAD_DIM), jnp.bfloat16),
        *state,
        own_there,
        back,
    )
    half = tok // 2
    pieces = (
        attended,
        turn(attended, 1),
        turn(attended, -1),
        turn(attended[:half], 2),
        turn(attended[half:], -2),
    )
    return project(head.reshape(1).astype(jnp.int32), pieces, out_weight)


def solution(mesh):
    placed = (P("ctx", "head"), P("ctx", "head"), P("ctx", "head"), P(), P(None, "head"))
    return jax.shard_map(
        shards, mesh=mesh, in_specs=placed, out_specs=P("ctx", "head"), check_vma=False
    )
```

```python
import functools
import math

import jax
import jax.numpy as jnp
from jax import lax
from jax.experimental import pallas as pl
from jax.experimental.pallas import tpu as pltpu
from jax.sharding import PartitionSpec as P

HEAD_DIM = 128
BLOCK = 128
FAR = -1e30
START = -1e25
TO_LOG2 = math.log2(math.e) * HEAD_DIM**-0.5
VMEM_LIMIT = 16 * 2**20
RING_CHIPS = 8


def vmem_spec():
    return pl.BlockSpec(memory_space=pltpu.VMEM)


def smem_spec():
    return pl.BlockSpec(memory_space=pltpu.SMEM)


def fold_kernel(first, parts, info, key_base, *refs):
    count = len(parts)
    q_refs, kv, refs = refs[:count], refs[count], refs[count + 1 :]
    if first:
        m_out, a_out, v_wide, q_all = refs
        m_in, a_in = m_out, a_out
        m_out[...] = jnp.full(m_out.shape, START, jnp.float32)
        a_out[...] = jnp.zeros(a_out.shape, jnp.float32)
    else:
        m_in, a_in, m_out, a_out, v_wide, q_all = refs
    tok = q_refs[0].shape[0]
    blocks = tok // BLOCK
    k_base = key_base[0]

    def wants(part):
        return (k_base + blocks > info[4 + part * blocks]) & (k_base < info[part] + blocks)

    any_wants = False
    for part, q_ref in zip(parts, q_refs):
        any_wants = any_wants | wants(part)

        @pl.when(wants(part))
        def _(part=part, q_ref=q_ref):
            q_all[part - parts[0]] = q_ref[...]

    @pl.when(any_wants)
    def _():
        v_wide[:, :HEAD_DIM] = kv[1]
        v_wide[:, HEAD_DIM:] = jnp.ones((tok, HEAD_DIM), jnp.bfloat16)

    @pl.loop(parts[0], parts[0] + count)
    def _(part):
        q_base = info[part]
        begin = [info[4 + part * blocks + i] for i in range(blocks)]

        @pl.when(wants(part))
        def _():
            half = tok // 2
            both = (slice(0, half), slice(half, tok))

            def score(rows_in):
                return lax.dot_general(
                    q_all[part - parts[0], rows_in, :],
                    kv[0],
                    (((1,), (1,)), ((), ())),
                    preferred_element_type=jnp.float32,
                )

            scores = [score(rows_in) for rows_in in both]
            for n, s in enumerate(scores):
                rows_here = pl.ds(pl.multiple_of(part * tok + n * half, half), half)
                columns = []
                for j in range(blocks):
                    column = []
                    for i in range(blocks // 2):
                        i_all = n * (blocks // 2) + i
                        seen = (k_base + j >= begin[i_all]) & (k_base + j <= q_base + i_all)
                        bias = jnp.where(seen, 0.0, FAR).astype(jnp.float32)
                        column.append(
                            s[i * BLOCK : (i + 1) * BLOCK, j * BLOCK : (j + 1) * BLOCK] + bias
                        )
                    columns.append(jnp.concatenate(column, axis=0))
                s = jnp.concatenate(columns, axis=1)
                m = m_in[rows_here, :]
                new_m = jnp.maximum(m, jnp.max(s, axis=1, keepdims=True) * TO_LOG2)
                factor = jnp.exp2(m - new_m)
                p = jnp.exp2(s * TO_LOG2 - jnp.concatenate([new_m] * blocks, axis=1))
                added = jnp.dot(
                    p.astype(jnp.bfloat16), v_wide[...], preferred_element_type=jnp.float32
                )
                a_out[rows_here, :] = (
                    a_in[rows_here, :] * jnp.concatenate([factor] * 2, axis=1) + added
                )
                m_out[rows_here, :] = new_m


def fold(info, key_base, q_parts, parts, kv, state, weight=46):
    tok = q_parts[0].shape[0]
    first = state is None
    count = len(parts)
    shapes = [
        pltpu.VMEM((4 * tok, HEAD_DIM), jnp.float32),
        pltpu.VMEM((4 * tok, 2 * HEAD_DIM), jnp.float32),
    ]
    return pl.pallas_call(
        functools.partial(fold_kernel, first, parts),
        out_shape=shapes,
        in_specs=[smem_spec()] * 2 + [vmem_spec()] * (count + (1 if first else 3)),
        out_specs=[vmem_spec()] * 2,
        scratch_shapes=[
            pltpu.VMEM((tok, 2 * HEAD_DIM), jnp.bfloat16),
            pltpu.VMEM((count, tok, HEAD_DIM), jnp.bfloat16),
        ],
        input_output_aliases={} if first else {count + 3: 0, count + 4: 1},
        compiler_params=pltpu.CompilerParams(vmem_limit_bytes=VMEM_LIMIT),
        cost_estimate=pl.CostEstimate(
            flops=weight * tok * tok * HEAD_DIM, bytes_accessed=10**6, transcendentals=2 * tok * tok
        ),
        name="fold",
    )(info, key_base, *[q_parts[p] for p in parts], kv, *(() if first else state))


def diagonal():
    row = lax.broadcasted_iota(jnp.int32, (BLOCK, BLOCK), 0)
    return row == lax.broadcasted_iota(jnp.int32, (BLOCK, BLOCK), 1)


PIECE_ROWS = 16


def pack(out_ref, out, log_sum):
    tok = out.shape[0]
    blocks = tok // BLOCK
    on = diagonal()
    rows = [
        jnp.sum(jnp.where(on, log_sum[i * BLOCK : (i + 1) * BLOCK, :], 0.0), axis=0, keepdims=True)
        for i in range(blocks)
    ]
    rows.append(jnp.zeros((PIECE_ROWS - blocks, BLOCK), jnp.float32))
    rest = jnp.concatenate(rows, axis=0)
    out_ref[:tok, :] = out.astype(jnp.bfloat16)
    for k in range(3):
        piece = rest.astype(jnp.bfloat16)
        rest = rest - piece.astype(jnp.float32)
        out_ref[tok + PIECE_ROWS * k : tok + PIECE_ROWS * (k + 1), :] = piece


def unpack(ref, rows):
    on = diagonal()
    tok = ref.shape[0] - 3 * PIECE_ROWS
    tail = ref[tok:, :].astype(jnp.float32)
    log_rows = sum(tail[PIECE_ROWS * k : PIECE_ROWS * (k + 1), :] for k in range(3))
    columns = [
        jnp.sum(jnp.where(on, log_rows[i : i + 1, :], 0.0), axis=1, keepdims=True)
        for i in range(rows.start // BLOCK, rows.stop // BLOCK)
    ]
    return ref[rows, :].astype(jnp.float32), jnp.concatenate(columns, axis=0)


def packed_shape(tok):
    return jax.ShapeDtypeStruct((tok + 3 * PIECE_ROWS, HEAD_DIM), jnp.bfloat16)


def own_part(m_ref, a_ref, rows):
    return m_ref[rows, :], a_ref[rows, :HEAD_DIM], a_ref[rows, HEAD_DIM:]


def pack_state(out_ref, m, num, den):
    some = den > 0.0
    safe = jnp.where(some, den, 1.0)
    pack(out_ref, num / safe, jnp.where(some, m + jnp.log2(safe), START))


def mix(m, num, den, out, log_sum):
    top = jnp.maximum(m, log_sum)
    here = jnp.exp2(m - top)
    there = jnp.exp2(log_sum - top)
    return top, num * here + out * there, den * here + there * (log_sum > 0.5 * START)


def leave_kernel(tok, part, m_ref, a_ref, out_ref):
    pack_state(out_ref, *own_part(m_ref, a_ref, slice(part * tok, (part + 1) * tok)))


def pass_on_kernel(tok, part, rows, m_ref, a_ref, other, out_ref):
    state = own_part(m_ref, a_ref, slice(part * tok + rows.start, part * tok + rows.stop))
    pack_state(out_ref, *mix(*state, *unpack(other, rows)))


def join_kernel(rows, m_ref, a_ref, other, back, out_ref):
    state = mix(*own_part(m_ref, a_ref, rows), *unpack(other, rows))
    _, num, den = mix(*state, *unpack(back, slice(0, rows.stop - rows.start)))
    out_ref[...] = (num / den).astype(jnp.bfloat16)


def small_call(kernel, name, out_shape, *args):
    return pl.pallas_call(
        kernel,
        out_shape=out_shape,
        in_specs=[vmem_spec()] * len(args),
        out_specs=vmem_spec(),
        compiler_params=pltpu.CompilerParams(vmem_limit_bytes=VMEM_LIMIT),
        name=name,
    )(*args)


def project_kernel(heads, own, left, right, far, weight, *refs):
    out_ref, lhs = refs[-2:]
    step = pl.program_id(0)
    h = heads[0]
    count = weight.shape[0] // HEAD_DIM
    width = out_ref.shape[1]

    @pl.when(step == 0)
    def _():
        for by, piece in ((0, own), (count - 1, left), (1, right), (2, far)):
            column = pl.multiple_of(lax.rem(h + by, count) * HEAD_DIM, HEAD_DIM)
            lhs[:, pl.ds(column, HEAD_DIM)] = piece[...]

    columns = pl.ds(pl.multiple_of(step * width, width), width)
    out_ref[...] = jnp.dot(
        lhs[...], weight[:, columns], preferred_element_type=jnp.float32
    ).astype(jnp.bfloat16)


def project(heads, pieces, weight, tok, before):
    rows = pieces[0].shape[0]
    steps = 3
    width = weight.shape[1] // steps
    row_block = 0 if before is None else 1
    return pl.pallas_call(
        project_kernel,
        grid=(steps,),
        out_shape=jax.ShapeDtypeStruct((tok, weight.shape[1]), jnp.bfloat16),
        in_specs=[smem_spec()]
        + [vmem_spec()] * 5
        + ([] if before is None else [pl.BlockSpec(memory_space=pl.ANY)]),
        out_specs=pl.BlockSpec((rows, width), lambda i: (row_block, i)),
        scratch_shapes=[pltpu.VMEM((rows, weight.shape[0]), jnp.bfloat16)],
        input_output_aliases={} if before is None else {6: 0},
        compiler_params=pltpu.CompilerParams(vmem_limit_bytes=VMEM_LIMIT),
        cost_estimate=pl.CostEstimate(
            flops=2 * rows * weight.shape[0] * weight.shape[1],
            bytes_accessed=2 * rows * weight.shape[1],
            transcendentals=0,
        ),
        name="project",
    )(heads, *pieces, weight, *([] if before is None else [before]))


def shards(queries, key_states, value_states, clip_lengths, out_weight):
    tok = queries.shape[0]
    blocks = tok // BLOCK
    ctx_count = lax.axis_size("ctx")
    head_count = lax.axis_size("head")
    ring = 2 * RING_CHIPS
    me = lax.axis_index("ctx")
    core = me % 2
    first_of_ring = me // ring * ring
    place = (me % ring) // 2
    head = lax.axis_index("head")

    def send(value, target):
        return lax.ppermute(value, "ctx", [(i, target(i)) for i in range(ctx_count)])

    def sibling(i):
        return i ^ 1

    def along(i):
        at = i % ring
        by = 2 if i % 2 == 0 else -2
        return i - at + (at + by) % ring

    def after(value, state):
        value, m = lax.optimization_barrier((value, state[0]))
        return value, (m, state[1])

    def up(i):
        return (i + ring) % ctx_count

    def down(i):
        return (i - ring) % ctx_count

    def turn(value, by):
        pairs = [(i, (i + by) % head_count) for i in range(head_count)]
        return lax.ppermute(value, "head", pairs)

    upto = jnp.arange(clip_lengths.shape[0])
    ends = jnp.sum(jnp.where(upto[None, :] <= upto[:, None], clip_lengths[None, :], 0), axis=1)
    owners = jnp.stack([me, me ^ 1, (me + ring) % ctx_count, ((me + ring) % ctx_count) ^ 1])
    bases = owners * blocks
    q_blocks = bases[:, None] + jnp.arange(blocks, dtype=jnp.int32)[None, :]
    begin = jnp.max(
        jnp.where(ends[None, None, :] <= q_blocks[:, :, None], ends[None, None, :], 0), axis=-1
    )
    info = jnp.concatenate([bases, begin.reshape(-1)]).astype(jnp.int32)

    kv = jnp.stack([key_states, value_states])
    near = send(kv, along)
    kv, info = lax.optimization_barrier((kv, info))
    cross = send(kv, lambda i: along(sibling(i)))
    next_own = send(queries, down)
    q_sibling = send(queries, sibling)

    def base_of(step, of_core):
        chip = (place + jnp.where(core == 0, -step, step)) % RING_CHIPS
        return ((first_of_ring + 2 * chip + of_core) * blocks).reshape(1).astype(jnp.int32)

    order = []
    for step in range(1, RING_CHIPS // 2 + 1):
        order += [(step, core), (step, 1 - core)]
    order = order[:-1]
    arrived = [near, cross]
    everyone = (0, 1, 2, 3)
    own_base = base_of(0, core)
    state = fold(info, own_base, (queries,), (0,), kv, None, 4)
    state = fold(info, own_base, (queries, q_sibling), (1,), kv, state, 4)
    q_parts = (queries, q_sibling, next_own, send(queries, lambda i: sibling(down(i))))
    for n, (step, of_core) in enumerate(order):
        value = arrived[n]
        if n + 2 < len(order):
            value, state = after(value, state)
            arrived.append(send(value, along))
        if n == len(order) - 1:
            state = fold(info, own_base, q_parts, (2, 3), kv, state)
        state = fold(
            info, base_of(step, of_core), q_parts, everyone, value, state, 46 if n else 8
        )

    packed = packed_shape(tok)
    half = tok // 2
    halves = (slice(0, half), slice(half, tok))
    leave = functools.partial(leave_kernel, tok)
    next_there = send(small_call(functools.partial(leave, 3), "leave_next", packed, *state), sibling)
    own_there = send(small_call(functools.partial(leave, 1), "leave_own", packed, *state), sibling)
    back = [
        send(
            small_call(
                functools.partial(pass_on_kernel, tok, 2, rows),
                "pass_on",
                packed_shape(half),
                *state,
                next_there,
            ),
            up,
        )
        for rows in halves
    ]
    pieces = []
    for rows, returned in zip(halves, back):
        attended = small_call(
            functools.partial(join_kernel, rows),
            "join",
            jax.ShapeDtypeStruct((half, HEAD_DIM), jnp.bfloat16),
            *state,
            own_there,
            returned,
        )
        pieces.append(
            (
                attended,
                turn(attended, 1),
                turn(attended, -1),
                turn(attended, 2),
            )
        )
    heads = head.reshape(1).astype(jnp.int32)
    first = project(heads, pieces[0], out_weight, tok, None)
    return project(heads, pieces[1], out_weight, tok, first)


def solution(mesh):
    placed = (P("ctx", "head"), P("ctx", "head"), P("ctx", "head"), P(), P(None, "head"))
    return jax.shard_map(
        shards, mesh=mesh, in_specs=placed, out_specs=P("ctx", "head"), check_vma=False
    )
```

```python
import functools
import math

import jax
import jax.numpy as jnp
from jax import lax
from jax.experimental import pallas as pl
from jax.experimental.pallas import tpu as pltpu
from jax.sharding import PartitionSpec as P

HEAD_DIM = 128
BLOCK = 128
FAR = -1e30
START = -1e25
TO_LOG2 = math.log2(math.e) * HEAD_DIM**-0.5
VMEM_LIMIT = 16 * 2**20
RING_CHIPS = 8


def vmem_spec():
    return pl.BlockSpec(memory_space=pltpu.VMEM)


def smem_spec():
    return pl.BlockSpec(memory_space=pltpu.SMEM)


def fold_kernel(first, parts, info, key_base, *refs):
    count = len(parts)
    q_refs, kv, refs = refs[:count], refs[count], refs[count + 1 :]
    if first:
        m_out, a_out, v_wide, q_all = refs
        m_in, a_in = m_out, a_out
        m_out[...] = jnp.full(m_out.shape, START, jnp.float32)
        a_out[...] = jnp.zeros(a_out.shape, jnp.float32)
    else:
        m_in, a_in, m_out, a_out, v_wide, q_all = refs
    tok = q_refs[0].shape[0]
    blocks = tok // BLOCK
    k_base = key_base[0]

    def wants(part):
        return (k_base + blocks > info[4 + part * blocks]) & (k_base < info[part] + blocks)

    any_wants = False
    for part, q_ref in zip(parts, q_refs):
        any_wants = any_wants | wants(part)

        @pl.when(wants(part))
        def _(part=part, q_ref=q_ref):
            q_all[part - parts[0]] = q_ref[...]

    @pl.when(any_wants)
    def _():
        v_wide[:, :HEAD_DIM] = kv[1]
        v_wide[:, HEAD_DIM:] = jnp.ones((tok, HEAD_DIM), jnp.bfloat16)

    @pl.loop(parts[0], parts[0] + count)
    def _(part):
        q_base = info[part]
        begin = [info[4 + part * blocks + i] for i in range(blocks)]

        @pl.when(wants(part))
        def _():
            half = tok // 2
            both = (slice(0, half), slice(half, tok))

            def score(rows_in):
                return lax.dot_general(
                    q_all[part - parts[0], rows_in, :],
                    kv[0],
                    (((1,), (1,)), ((), ())),
                    preferred_element_type=jnp.float32,
                )

            scores = [score(rows_in) for rows_in in both]
            for n, s in enumerate(scores):
                rows_here = pl.ds(pl.multiple_of(part * tok + n * half, half), half)
                columns = []
                for j in range(blocks):
                    column = []
                    for i in range(blocks // 2):
                        i_all = n * (blocks // 2) + i
                        seen = (k_base + j >= begin[i_all]) & (k_base + j <= q_base + i_all)
                        bias = jnp.where(seen, 0.0, FAR).astype(jnp.float32)
                        column.append(
                            s[i * BLOCK : (i + 1) * BLOCK, j * BLOCK : (j + 1) * BLOCK] + bias
                        )
                    columns.append(jnp.concatenate(column, axis=0))
                s = jnp.concatenate(columns, axis=1)
                m = m_in[rows_here, :]
                new_m = jnp.maximum(m, jnp.max(s, axis=1, keepdims=True) * TO_LOG2)
                factor = jnp.exp2(m - new_m)
                p = jnp.exp2(s * TO_LOG2 - jnp.concatenate([new_m] * blocks, axis=1))
                added = jnp.dot(
                    p.astype(jnp.bfloat16), v_wide[...], preferred_element_type=jnp.float32
                )
                a_out[rows_here, :] = (
                    a_in[rows_here, :] * jnp.concatenate([factor] * 2, axis=1) + added
                )
                m_out[rows_here, :] = new_m


def fold(info, key_base, q_parts, parts, kv, state, weight=46):
    tok = q_parts[0].shape[0]
    first = state is None
    count = len(parts)
    shapes = [
        pltpu.VMEM((4 * tok, HEAD_DIM), jnp.float32),
        pltpu.VMEM((4 * tok, 2 * HEAD_DIM), jnp.float32),
    ]
    return pl.pallas_call(
        functools.partial(fold_kernel, first, parts),
        out_shape=shapes,
        in_specs=[smem_spec()] * 2 + [vmem_spec()] * (count + (1 if first else 3)),
        out_specs=[vmem_spec()] * 2,
        scratch_shapes=[
            pltpu.VMEM((tok, 2 * HEAD_DIM), jnp.bfloat16),
            pltpu.VMEM((count, tok, HEAD_DIM), jnp.bfloat16),
        ],
        input_output_aliases={} if first else {count + 3: 0, count + 4: 1},
        compiler_params=pltpu.CompilerParams(vmem_limit_bytes=VMEM_LIMIT),
        cost_estimate=pl.CostEstimate(
            flops=weight * tok * tok * HEAD_DIM, bytes_accessed=10**6, transcendentals=2 * tok * tok
        ),
        name="fold",
    )(info, key_base, *[q_parts[p] for p in parts], kv, *(() if first else state))


def diagonal():
    row = lax.broadcasted_iota(jnp.int32, (BLOCK, BLOCK), 0)
    return row == lax.broadcasted_iota(jnp.int32, (BLOCK, BLOCK), 1)


PIECE_ROWS = 16


def pack(out_ref, out, log_sum):
    tok = out.shape[0]
    blocks = tok // BLOCK
    on = diagonal()
    rows = [
        jnp.sum(jnp.where(on, log_sum[i * BLOCK : (i + 1) * BLOCK, :], 0.0), axis=0, keepdims=True)
        for i in range(blocks)
    ]
    rows.append(jnp.zeros((PIECE_ROWS - blocks, BLOCK), jnp.float32))
    rest = jnp.concatenate(rows, axis=0)
    out_ref[:tok, :] = out.astype(jnp.bfloat16)
    for k in range(3):
        piece = rest.astype(jnp.bfloat16)
        rest = rest - piece.astype(jnp.float32)
        out_ref[tok + PIECE_ROWS * k : tok + PIECE_ROWS * (k + 1), :] = piece


def unpack(ref, rows):
    on = diagonal()
    tok = ref.shape[0] - 3 * PIECE_ROWS
    tail = ref[tok:, :].astype(jnp.float32)
    log_rows = sum(tail[PIECE_ROWS * k : PIECE_ROWS * (k + 1), :] for k in range(3))
    columns = [
        jnp.sum(jnp.where(on, log_rows[i : i + 1, :], 0.0), axis=1, keepdims=True)
        for i in range(rows.start // BLOCK, rows.stop // BLOCK)
    ]
    return ref[rows, :].astype(jnp.float32), jnp.concatenate(columns, axis=0)


def packed_shape(tok):
    return jax.ShapeDtypeStruct((tok + 3 * PIECE_ROWS, HEAD_DIM), jnp.bfloat16)


def own_part(m_ref, a_ref, rows):
    return m_ref[rows, :], a_ref[rows, :HEAD_DIM], a_ref[rows, HEAD_DIM:]


def pack_state(out_ref, m, num, den):
    some = den > 0.0
    safe = jnp.where(some, den, 1.0)
    pack(out_ref, num / safe, jnp.where(some, m + jnp.log2(safe), START))


def mix(m, num, den, out, log_sum):
    top = jnp.maximum(m, log_sum)
    here = jnp.exp2(m - top)
    there = jnp.exp2(log_sum - top)
    return top, num * here + out * there, den * here + there * (log_sum > 0.5 * START)


def leave_kernel(tok, part, m_ref, a_ref, out_ref):
    pack_state(out_ref, *own_part(m_ref, a_ref, slice(part * tok, (part + 1) * tok)))


def pass_on_kernel(tok, part, rows, m_ref, a_ref, other, out_ref):
    state = own_part(m_ref, a_ref, slice(part * tok + rows.start, part * tok + rows.stop))
    pack_state(out_ref, *mix(*state, *unpack(other, rows)))


def join_kernel(rows, m_ref, a_ref, other, back, out_ref):
    state = mix(*own_part(m_ref, a_ref, rows), *unpack(other, rows))
    _, num, den = mix(*state, *unpack(back, slice(0, rows.stop - rows.start)))
    out_ref[...] = (num / den).astype(jnp.bfloat16)


def small_call(kernel, name, out_shape, *args):
    return pl.pallas_call(
        kernel,
        out_shape=out_shape,
        in_specs=[vmem_spec()] * len(args),
        out_specs=vmem_spec(),
        compiler_params=pltpu.CompilerParams(vmem_limit_bytes=VMEM_LIMIT),
        name=name,
    )(*args)


PROJECT_STEPS = 3


def project_kernel(row_block, heads, own, left, right, far, weight, *refs):
    out_ref, lhs, result, done = refs[-4:]
    h = heads[0]
    count = weight.shape[0] // HEAD_DIM
    rows, width = result.shape[0], result.shape[1] // PROJECT_STEPS
    for by, piece in ((0, own), (count - 1, left), (1, right), (2, far)):
        column = pl.multiple_of(lax.rem(h + by, count) * HEAD_DIM, HEAD_DIM)
        lhs[:, pl.ds(column, HEAD_DIM)] = piece[...]
    copies = []
    for step in range(PROJECT_STEPS):
        columns = pl.ds(step * width, width)
        result[:, columns] = jnp.dot(
            lhs[...], weight[:, columns], preferred_element_type=jnp.float32
        ).astype(jnp.bfloat16)
        copies.append(
            pltpu.make_async_copy(
                result.at[:, columns],
                out_ref.at[pl.ds(row_block * rows, rows), columns],
                done.at[step],
            )
        )
        copies[-1].start()
    for copy in copies:
        copy.wait()


def project(heads, pieces, weight, tok, before):
    rows = pieces[0].shape[0]
    return pl.pallas_call(
        functools.partial(project_kernel, 0 if before is None else 1),
        out_shape=jax.ShapeDtypeStruct((tok, weight.shape[1]), jnp.bfloat16),
        in_specs=[smem_spec()]
        + [vmem_spec()] * 5
        + ([] if before is None else [pl.BlockSpec(memory_space=pl.ANY)]),
        out_specs=pl.BlockSpec(memory_space=pl.ANY),
        scratch_shapes=[
            pltpu.VMEM((rows, weight.shape[0]), jnp.bfloat16),
            pltpu.VMEM((rows, weight.shape[1]), jnp.bfloat16),
            pltpu.SemaphoreType.DMA((PROJECT_STEPS,)),
        ],
        input_output_aliases={} if before is None else {6: 0},
        compiler_params=pltpu.CompilerParams(vmem_limit_bytes=VMEM_LIMIT),
        cost_estimate=pl.CostEstimate(
            flops=2 * rows * weight.shape[0] * weight.shape[1],
            bytes_accessed=2 * rows * weight.shape[1],
            transcendentals=0,
        ),
        name="project",
    )(heads, *pieces, weight, *([] if before is None else [before]))


def shards(queries, key_states, value_states, clip_lengths, out_weight):
    tok = queries.shape[0]
    blocks = tok // BLOCK
    ctx_count = lax.axis_size("ctx")
    head_count = lax.axis_size("head")
    ring = 2 * RING_CHIPS
    me = lax.axis_index("ctx")
    core = me % 2
    first_of_ring = me // ring * ring
    place = (me % ring) // 2
    head = lax.axis_index("head")

    def send(value, target):
        return lax.ppermute(value, "ctx", [(i, target(i)) for i in range(ctx_count)])

    def sibling(i):
        return i ^ 1

    def along(i):
        at = i % ring
        by = 2 if i % 2 == 0 else -2
        return i - at + (at + by) % ring

    def after(value, state):
        value, m = lax.optimization_barrier((value, state[0]))
        return value, (m, state[1])

    def up(i):
        return (i + ring) % ctx_count

    def down(i):
        return (i - ring) % ctx_count

    def turn(value, by):
        pairs = [(i, (i + by) % head_count) for i in range(head_count)]
        return lax.ppermute(value, "head", pairs)

    upto = jnp.arange(clip_lengths.shape[0])
    ends = jnp.sum(jnp.where(upto[None, :] <= upto[:, None], clip_lengths[None, :], 0), axis=1)
    owners = jnp.stack([me, me ^ 1, (me + ring) % ctx_count, ((me + ring) % ctx_count) ^ 1])
    bases = owners * blocks
    q_blocks = bases[:, None] + jnp.arange(blocks, dtype=jnp.int32)[None, :]
    begin = jnp.max(
        jnp.where(ends[None, None, :] <= q_blocks[:, :, None], ends[None, None, :], 0), axis=-1
    )
    info = jnp.concatenate([bases, begin.reshape(-1)]).astype(jnp.int32)

    kv = jnp.stack([key_states, value_states])
    near = send(kv, along)
    kv, info = lax.optimization_barrier((kv, info))
    cross = send(kv, lambda i: along(sibling(i)))
    next_own = send(queries, down)
    q_sibling = send(queries, sibling)

    def base_of(step, of_core):
        chip = (place + jnp.where(core == 0, -step, step)) % RING_CHIPS
        return ((first_of_ring + 2 * chip + of_core) * blocks).reshape(1).astype(jnp.int32)

    order = []
    for step in range(1, RING_CHIPS // 2 + 1):
        order += [(step, core), (step, 1 - core)]
    order = order[:-1]
    arrived = [near, cross]
    everyone = (0, 1, 2, 3)
    own_base = base_of(0, core)
    state = fold(info, own_base, (queries,), (0,), kv, None, 4)
    state = fold(info, own_base, (queries, q_sibling), (1,), kv, state, 4)
    q_parts = (queries, q_sibling, next_own, send(queries, lambda i: sibling(down(i))))
    for n, (step, of_core) in enumerate(order):
        value = arrived[n]
        if n + 2 < len(order):
            value, state = after(value, state)
            arrived.append(send(value, along))
        if n == len(order) - 1:
            state = fold(info, own_base, q_parts, (2, 3), kv, state)
        state = fold(
            info, base_of(step, of_core), q_parts, everyone, value, state, 46 if n else 8
        )

    packed = packed_shape(tok)
    half = tok // 2
    halves = (slice(0, half), slice(half, tok))
    leave = functools.partial(leave_kernel, tok)
    next_there = send(small_call(functools.partial(leave, 3), "leave_next", packed, *state), sibling)
    own_there = send(small_call(functools.partial(leave, 1), "leave_own", packed, *state), sibling)
    back = [
        send(
            small_call(
                functools.partial(pass_on_kernel, tok, 2, rows),
                "pass_on",
                packed_shape(half),
                *state,
                next_there,
            ),
            up,
        )
        for rows in halves
    ]
    pieces = []
    for rows, returned in zip(halves, back):
        attended = small_call(
            functools.partial(join_kernel, rows),
            "join",
            jax.ShapeDtypeStruct((half, HEAD_DIM), jnp.bfloat16),
            *state,
            own_there,
            returned,
        )
        pieces.append(
            (
                attended,
                turn(attended, 1),
                turn(attended, -1),
                turn(attended, 2),
            )
        )
    heads = head.reshape(1).astype(jnp.int32)
    first = project(heads, pieces[0], out_weight, tok, None)
    return project(heads, pieces[1], out_weight, tok, first)


def solution(mesh):
    placed = (P("ctx", "head"), P("ctx", "head"), P("ctx", "head"), P(), P(None, "head"))
    return jax.shard_map(
        shards, mesh=mesh, in_specs=placed, out_specs=P("ctx", "head"), check_vma=False
    )
```

```python
import functools
import math

import jax
import jax.numpy as jnp
from jax import lax
from jax.experimental import pallas as pl
from jax.experimental.pallas import tpu as pltpu
from jax.sharding import PartitionSpec as P

HEAD_DIM = 128
BLOCK = 128
FAR = -1e30
START = -1e25
TO_LOG2 = math.log2(math.e) * HEAD_DIM**-0.5
VMEM_LIMIT = 16 * 2**20
RING_CHIPS = 8


def vmem_spec():
    return pl.BlockSpec(memory_space=pltpu.VMEM)


def smem_spec():
    return pl.BlockSpec(memory_space=pltpu.SMEM)


def fold_kernel(first, parts, info, key_base, *refs):
    count = len(parts)
    q_refs, kv, refs = refs[:count], refs[count], refs[count + 1 :]
    if first:
        m_out, a_out, v_wide, q_all = refs
        m_in, a_in = m_out, a_out
        m_out[...] = jnp.full(m_out.shape, START, jnp.float32)
        a_out[...] = jnp.zeros(a_out.shape, jnp.float32)
    else:
        m_in, a_in, m_out, a_out, v_wide, q_all = refs
    tok = q_refs[0].shape[0]
    blocks = tok // BLOCK
    k_base = key_base[0]

    def wants(part):
        return (k_base + blocks > info[4 + part * blocks]) & (k_base < info[part] + blocks)

    any_wants = False
    for part, q_ref in zip(parts, q_refs):
        any_wants = any_wants | wants(part)

        @pl.when(wants(part))
        def _(part=part, q_ref=q_ref):
            q_all[part - parts[0]] = q_ref[...]

    @pl.when(any_wants)
    def _():
        v_wide[:, :HEAD_DIM] = kv[1]
        v_wide[:, HEAD_DIM:] = jnp.ones((tok, HEAD_DIM), jnp.bfloat16)

    @pl.loop(parts[0], parts[0] + count)
    def _(part):
        q_base = info[part]
        begin = [info[4 + part * blocks + i] for i in range(blocks)]

        @pl.when(wants(part))
        def _():
            half = tok // 2
            both = (slice(0, half), slice(half, tok))

            def score(rows_in):
                return lax.dot_general(
                    q_all[part - parts[0], rows_in, :],
                    kv[0],
                    (((1,), (1,)), ((), ())),
                    preferred_element_type=jnp.float32,
                )

            scores = [score(rows_in) for rows_in in both]
            for n, s in enumerate(scores):
                rows_here = pl.ds(pl.multiple_of(part * tok + n * half, half), half)
                columns = []
                for j in range(blocks):
                    column = []
                    for i in range(blocks // 2):
                        i_all = n * (blocks // 2) + i
                        seen = (k_base + j >= begin[i_all]) & (k_base + j <= q_base + i_all)
                        bias = jnp.where(seen, 0.0, FAR).astype(jnp.float32)
                        column.append(
                            s[i * BLOCK : (i + 1) * BLOCK, j * BLOCK : (j + 1) * BLOCK] + bias
                        )
                    columns.append(jnp.concatenate(column, axis=0))
                s = jnp.concatenate(columns, axis=1)
                m = m_in[rows_here, :]
                new_m = jnp.maximum(m, jnp.max(s, axis=1, keepdims=True) * TO_LOG2)
                factor = jnp.exp2(m - new_m)
                p = jnp.exp2(s * TO_LOG2 - jnp.concatenate([new_m] * blocks, axis=1))
                added = jnp.dot(
                    p.astype(jnp.bfloat16), v_wide[...], preferred_element_type=jnp.float32
                )
                a_out[rows_here, :] = (
                    a_in[rows_here, :] * jnp.concatenate([factor] * 2, axis=1) + added
                )
                m_out[rows_here, :] = new_m


def fold(info, key_base, q_parts, parts, kv, state, weight=46):
    tok = q_parts[0].shape[0]
    first = state is None
    count = len(parts)
    shapes = [
        pltpu.VMEM((4 * tok, HEAD_DIM), jnp.float32),
        pltpu.VMEM((4 * tok, 2 * HEAD_DIM), jnp.float32),
    ]
    return pl.pallas_call(
        functools.partial(fold_kernel, first, parts),
        out_shape=shapes,
        in_specs=[smem_spec()] * 2 + [vmem_spec()] * (count + (1 if first else 3)),
        out_specs=[vmem_spec()] * 2,
        scratch_shapes=[
            pltpu.VMEM((tok, 2 * HEAD_DIM), jnp.bfloat16),
            pltpu.VMEM((count, tok, HEAD_DIM), jnp.bfloat16),
        ],
        input_output_aliases={} if first else {count + 3: 0, count + 4: 1},
        compiler_params=pltpu.CompilerParams(vmem_limit_bytes=VMEM_LIMIT),
        cost_estimate=pl.CostEstimate(
            flops=weight * tok * tok * HEAD_DIM, bytes_accessed=10**6, transcendentals=2 * tok * tok
        ),
        name="fold",
    )(info, key_base, *[q_parts[p] for p in parts], kv, *(() if first else state))


def diagonal():
    row = lax.broadcasted_iota(jnp.int32, (BLOCK, BLOCK), 0)
    return row == lax.broadcasted_iota(jnp.int32, (BLOCK, BLOCK), 1)


PIECE_ROWS = 16


def pack(out_ref, out, log_sum):
    tok = out.shape[0]
    blocks = tok // BLOCK
    on = diagonal()
    rows = [
        jnp.sum(jnp.where(on, log_sum[i * BLOCK : (i + 1) * BLOCK, :], 0.0), axis=0, keepdims=True)
        for i in range(blocks)
    ]
    rows.append(jnp.zeros((PIECE_ROWS - blocks, BLOCK), jnp.float32))
    rest = jnp.concatenate(rows, axis=0)
    out_ref[:tok, :] = out.astype(jnp.bfloat16)
    for k in range(3):
        piece = rest.astype(jnp.bfloat16)
        rest = rest - piece.astype(jnp.float32)
        out_ref[tok + PIECE_ROWS * k : tok + PIECE_ROWS * (k + 1), :] = piece


def unpack(ref, rows):
    on = diagonal()
    tok = ref.shape[0] - 3 * PIECE_ROWS
    tail = ref[tok:, :].astype(jnp.float32)
    log_rows = sum(tail[PIECE_ROWS * k : PIECE_ROWS * (k + 1), :] for k in range(3))
    columns = [
        jnp.sum(jnp.where(on, log_rows[i : i + 1, :], 0.0), axis=1, keepdims=True)
        for i in range(rows.start // BLOCK, rows.stop // BLOCK)
    ]
    return ref[rows, :].astype(jnp.float32), jnp.concatenate(columns, axis=0)


def packed_shape(tok):
    return jax.ShapeDtypeStruct((tok + 3 * PIECE_ROWS, HEAD_DIM), jnp.bfloat16)


def own_part(m_ref, a_ref, rows):
    return m_ref[rows, :], a_ref[rows, :HEAD_DIM], a_ref[rows, HEAD_DIM:]


def pack_state(out_ref, m, num, den):
    some = den > 0.0
    safe = jnp.where(some, den, 1.0)
    pack(out_ref, num / safe, jnp.where(some, m + jnp.log2(safe), START))


def mix(m, num, den, out, log_sum):
    top = jnp.maximum(m, log_sum)
    here = jnp.exp2(m - top)
    there = jnp.exp2(log_sum - top)
    return top, num * here + out * there, den * here + there * (log_sum > 0.5 * START)


def leave_kernel(tok, part, m_ref, a_ref, out_ref):
    pack_state(out_ref, *own_part(m_ref, a_ref, slice(part * tok, (part + 1) * tok)))


def pass_on_kernel(tok, part, rows, m_ref, a_ref, other, out_ref):
    state = own_part(m_ref, a_ref, slice(part * tok + rows.start, part * tok + rows.stop))
    pack_state(out_ref, *mix(*state, *unpack(other, rows)))


def join_kernel(rows, m_ref, a_ref, other, back, out_ref):
    state = mix(*own_part(m_ref, a_ref, rows), *unpack(other, rows))
    _, num, den = mix(*state, *unpack(back, slice(0, rows.stop - rows.start)))
    out_ref[...] = (num / den).astype(jnp.bfloat16)


def small_call(kernel, name, out_shape, *args):
    return pl.pallas_call(
        kernel,
        out_shape=out_shape,
        in_specs=[vmem_spec()] * len(args),
        out_specs=vmem_spec(),
        compiler_params=pltpu.CompilerParams(vmem_limit_bytes=VMEM_LIMIT),
        name=name,
    )(*args)


PROJECT_STEPS = 3


def project_kernel(row_block, heads, own, left, right, far, weight, *refs):
    out_ref, lhs, result, done = refs[-4:]
    h = heads[0]
    count = weight.shape[0] // HEAD_DIM
    rows, width = result.shape[0], result.shape[1] // PROJECT_STEPS
    for by, piece in ((0, own), (count - 1, left), (1, right), (2, far)):
        column = pl.multiple_of(lax.rem(h + by, count) * HEAD_DIM, HEAD_DIM)
        lhs[:, pl.ds(column, HEAD_DIM)] = piece[...]
    copies = []
    for step in range(PROJECT_STEPS):
        columns = pl.ds(step * width, width)
        result[:, columns] = jnp.dot(
            lhs[...], weight[:, columns], preferred_element_type=jnp.float32
        ).astype(jnp.bfloat16)
        copies.append(
            pltpu.make_async_copy(
                result.at[:, columns],
                out_ref.at[pl.ds(row_block * rows, rows), columns],
                done.at[step],
            )
        )
        copies[-1].start()
    for copy in copies:
        copy.wait()


def project(heads, pieces, weight, tok, before):
    rows = pieces[0].shape[0]
    return pl.pallas_call(
        functools.partial(project_kernel, 0 if before is None else 1),
        out_shape=jax.ShapeDtypeStruct((tok, weight.shape[1]), jnp.bfloat16),
        in_specs=[smem_spec()]
        + [vmem_spec()] * 5
        + ([] if before is None else [pl.BlockSpec(memory_space=pl.ANY)]),
        out_specs=pl.BlockSpec(memory_space=pl.ANY),
        scratch_shapes=[
            pltpu.VMEM((rows, weight.shape[0]), jnp.bfloat16),
            pltpu.VMEM((rows, weight.shape[1]), jnp.bfloat16),
            pltpu.SemaphoreType.DMA((PROJECT_STEPS,)),
        ],
        input_output_aliases={} if before is None else {6: 0},
        compiler_params=pltpu.CompilerParams(vmem_limit_bytes=VMEM_LIMIT),
        cost_estimate=pl.CostEstimate(
            flops=2 * rows * weight.shape[0] * weight.shape[1],
            bytes_accessed=2 * rows * weight.shape[1],
            transcendentals=0,
        ),
        name="project",
    )(heads, *pieces, weight, *([] if before is None else [before]))


def shards(queries, key_states, value_states, clip_lengths, out_weight):
    tok = queries.shape[0]
    blocks = tok // BLOCK
    ctx_count = lax.axis_size("ctx")
    head_count = lax.axis_size("head")
    ring = 2 * RING_CHIPS
    me = lax.axis_index("ctx")
    core = me % 2
    first_of_ring = me // ring * ring
    place = (me % ring) // 2
    head = lax.axis_index("head")

    def send(value, target):
        return lax.ppermute(value, "ctx", [(i, target(i)) for i in range(ctx_count)])

    def sibling(i):
        return i ^ 1

    def along(i):
        at = i % ring
        by = 2 if i % 2 == 0 else -2
        return i - at + (at + by) % ring

    def after(value, state):
        value, m = lax.optimization_barrier((value, state[0]))
        return value, (m, state[1])

    def up(i):
        return (i + ring) % ctx_count

    def down(i):
        return (i - ring) % ctx_count

    def turn(value, by):
        pairs = [(i, (i + by) % head_count) for i in range(head_count)]
        return lax.ppermute(value, "head", pairs)

    upto = jnp.arange(clip_lengths.shape[0])
    ends = jnp.sum(jnp.where(upto[None, :] <= upto[:, None], clip_lengths[None, :], 0), axis=1)
    owners = jnp.stack([me, me ^ 1, (me + ring) % ctx_count, ((me + ring) % ctx_count) ^ 1])
    bases = owners * blocks
    q_blocks = bases[:, None] + jnp.arange(blocks, dtype=jnp.int32)[None, :]
    begin = jnp.max(
        jnp.where(ends[None, None, :] <= q_blocks[:, :, None], ends[None, None, :], 0), axis=-1
    )
    info = jnp.concatenate([bases, begin.reshape(-1)]).astype(jnp.int32)

    kv = jnp.stack([key_states, value_states])
    near = send(kv, along)
    kv, info = lax.optimization_barrier((kv, info))
    cross = send(kv, lambda i: along(sibling(i)))
    next_own = send(queries, down)
    q_sibling = send(queries, sibling)

    def base_of(step, of_core):
        chip = (place + jnp.where(core == 0, -step, step)) % RING_CHIPS
        return ((first_of_ring + 2 * chip + of_core) * blocks).reshape(1).astype(jnp.int32)

    order = []
    for step in range(1, RING_CHIPS // 2 + 1):
        order += [(step, core), (step, 1 - core)]
    order = order[:-1]
    arrived = [near, cross]
    everyone = (0, 1, 2, 3)
    own_base = base_of(0, core)
    state = fold(info, own_base, (queries,), (0,), kv, None, 4)
    state = fold(info, own_base, (queries, q_sibling), (1,), kv, state, 4)
    q_parts = (queries, q_sibling, next_own, send(queries, lambda i: sibling(down(i))))
    for n, (step, of_core) in enumerate(order):
        value = arrived[n]
        if n + 2 < len(order):
            if n != 1:
                value, state = after(value, state)
            arrived.append(send(value, along))
        if n == len(order) - 1:
            state = fold(info, own_base, q_parts, (2, 3), kv, state)
        state = fold(
            info, base_of(step, of_core), q_parts, everyone, value, state, 46 if n else 8
        )

    packed = packed_shape(tok)
    half = tok // 2
    halves = (slice(0, half), slice(half, tok))
    leave = functools.partial(leave_kernel, tok)
    next_there = send(small_call(functools.partial(leave, 3), "leave_next", packed, *state), sibling)
    own_there = send(small_call(functools.partial(leave, 1), "leave_own", packed, *state), sibling)
    back = [
        send(
            small_call(
                functools.partial(pass_on_kernel, tok, 2, rows),
                "pass_on",
                packed_shape(half),
                *state,
                next_there,
            ),
            up,
        )
        for rows in halves
    ]
    pieces = []
    for rows, returned in zip(halves, back):
        attended = small_call(
            functools.partial(join_kernel, rows),
            "join",
            jax.ShapeDtypeStruct((half, HEAD_DIM), jnp.bfloat16),
            *state,
            own_there,
            returned,
        )
        pieces.append(
            (
                attended,
                turn(attended, 1),
                turn(attended, -1),
                turn(attended, 2),
            )
        )
    heads = head.reshape(1).astype(jnp.int32)
    first = project(heads, pieces[0], out_weight, tok, None)
    return project(heads, pieces[1], out_weight, tok, first)


def solution(mesh):
    placed = (P("ctx", "head"), P("ctx", "head"), P("ctx", "head"), P(), P(None, "head"))
    return jax.shard_map(
        shards, mesh=mesh, in_specs=placed, out_specs=P("ctx", "head"), check_vma=False
    )
```

```python
import functools
import math

import jax
import jax.numpy as jnp
from jax import lax
from jax.experimental import pallas as pl
from jax.experimental.pallas import tpu as pltpu
from jax.sharding import PartitionSpec as P

HEAD_DIM = 128
BLOCK = 128
FAR = -1e30
START = -1e25
TO_LOG2 = math.log2(math.e) * HEAD_DIM**-0.5
VMEM_LIMIT = 16 * 2**20
RING_CHIPS = 8


def vmem_spec():
    return pl.BlockSpec(memory_space=pltpu.VMEM)


def smem_spec():
    return pl.BlockSpec(memory_space=pltpu.SMEM)


def fold_kernel(first, parts, info, key_base, *refs):
    count = len(parts)
    q_refs, kv, refs = refs[:count], refs[count], refs[count + 1 :]
    if first:
        m_out, a_out, v_wide, q_all = refs
        m_in, a_in = m_out, a_out
        m_out[...] = jnp.full(m_out.shape, START, jnp.float32)
        a_out[...] = jnp.zeros(a_out.shape, jnp.float32)
    else:
        m_in, a_in, m_out, a_out, v_wide, q_all = refs
    tok = q_refs[0].shape[0]
    blocks = tok // BLOCK
    k_base = key_base[0]

    def wants(part):
        return (k_base + blocks > info[4 + part * blocks]) & (k_base < info[part] + blocks)

    any_wants = False
    for part, q_ref in zip(parts, q_refs):
        any_wants = any_wants | wants(part)

        @pl.when(wants(part))
        def _(part=part, q_ref=q_ref):
            q_all[part - parts[0]] = q_ref[...]

    @pl.when(any_wants)
    def _():
        v_wide[:, :HEAD_DIM] = kv[1]
        v_wide[:, HEAD_DIM:] = jnp.ones((tok, HEAD_DIM), jnp.bfloat16)

    @pl.loop(parts[0], parts[0] + count)
    def _(part):
        q_base = info[part]
        begin = [info[4 + part * blocks + i] for i in range(blocks)]

        whole = (k_base >= begin[blocks - 1]) & (k_base + blocks - 1 <= q_base)

        def run(masked):
            half = tok // 2
            both = (slice(0, half), slice(half, tok))

            def score(rows_in):
                return lax.dot_general(
                    q_all[part - parts[0], rows_in, :],
                    kv[0],
                    (((1,), (1,)), ((), ())),
                    preferred_element_type=jnp.float32,
                )

            scores = [score(rows_in) for rows_in in both]
            for n, s in enumerate(scores):
                rows_here = pl.ds(pl.multiple_of(part * tok + n * half, half), half)
                if masked:
                    columns = []
                    for j in range(blocks):
                        column = []
                        for i in range(blocks // 2):
                            i_all = n * (blocks // 2) + i
                            seen = (k_base + j >= begin[i_all]) & (k_base + j <= q_base + i_all)
                            bias = jnp.where(seen, 0.0, FAR).astype(jnp.float32)
                            column.append(
                                s[i * BLOCK : (i + 1) * BLOCK, j * BLOCK : (j + 1) * BLOCK] + bias
                            )
                        columns.append(jnp.concatenate(column, axis=0))
                    s = jnp.concatenate(columns, axis=1)
                m = m_in[rows_here, :]
                new_m = jnp.maximum(m, jnp.max(s, axis=1, keepdims=True) * TO_LOG2)
                factor = jnp.exp2(m - new_m)
                p = jnp.exp2(s * TO_LOG2 - jnp.concatenate([new_m] * blocks, axis=1))
                added = jnp.dot(
                    p.astype(jnp.bfloat16), v_wide[...], preferred_element_type=jnp.float32
                )
                a_out[rows_here, :] = (
                    a_in[rows_here, :] * jnp.concatenate([factor] * 2, axis=1) + added
                )
                m_out[rows_here, :] = new_m

        pl.when(wants(part) & whole)(functools.partial(run, False))
        pl.when(wants(part) & jnp.logical_not(whole))(functools.partial(run, True))


def fold(info, key_base, q_parts, parts, kv, state, weight=46):
    tok = q_parts[0].shape[0]
    first = state is None
    count = len(parts)
    shapes = [
        pltpu.VMEM((4 * tok, HEAD_DIM), jnp.float32),
        pltpu.VMEM((4 * tok, 2 * HEAD_DIM), jnp.float32),
    ]
    return pl.pallas_call(
        functools.partial(fold_kernel, first, parts),
        out_shape=shapes,
        in_specs=[smem_spec()] * 2 + [vmem_spec()] * (count + (1 if first else 3)),
        out_specs=[vmem_spec()] * 2,
        scratch_shapes=[
            pltpu.VMEM((tok, 2 * HEAD_DIM), jnp.bfloat16),
            pltpu.VMEM((count, tok, HEAD_DIM), jnp.bfloat16),
        ],
        input_output_aliases={} if first else {count + 3: 0, count + 4: 1},
        compiler_params=pltpu.CompilerParams(vmem_limit_bytes=VMEM_LIMIT),
        cost_estimate=pl.CostEstimate(
            flops=weight * tok * tok * HEAD_DIM, bytes_accessed=10**6, transcendentals=2 * tok * tok
        ),
        name="fold",
    )(info, key_base, *[q_parts[p] for p in parts], kv, *(() if first else state))


def diagonal():
    row = lax.broadcasted_iota(jnp.int32, (BLOCK, BLOCK), 0)
    return row == lax.broadcasted_iota(jnp.int32, (BLOCK, BLOCK), 1)


PIECE_ROWS = 16


def pack(out_ref, out, log_sum):
    tok = out.shape[0]
    blocks = tok // BLOCK
    on = diagonal()
    rows = [
        jnp.sum(jnp.where(on, log_sum[i * BLOCK : (i + 1) * BLOCK, :], 0.0), axis=0, keepdims=True)
        for i in range(blocks)
    ]
    rows.append(jnp.zeros((PIECE_ROWS - blocks, BLOCK), jnp.float32))
    rest = jnp.concatenate(rows, axis=0)
    out_ref[:tok, :] = out.astype(jnp.bfloat16)
    for k in range(3):
        piece = rest.astype(jnp.bfloat16)
        rest = rest - piece.astype(jnp.float32)
        out_ref[tok + PIECE_ROWS * k : tok + PIECE_ROWS * (k + 1), :] = piece


def unpack(ref, rows):
    on = diagonal()
    tok = ref.shape[0] - 3 * PIECE_ROWS
    tail = ref[tok:, :].astype(jnp.float32)
    log_rows = sum(tail[PIECE_ROWS * k : PIECE_ROWS * (k + 1), :] for k in range(3))
    columns = [
        jnp.sum(jnp.where(on, log_rows[i : i + 1, :], 0.0), axis=1, keepdims=True)
        for i in range(rows.start // BLOCK, rows.stop // BLOCK)
    ]
    return ref[rows, :].astype(jnp.float32), jnp.concatenate(columns, axis=0)


def packed_shape(tok):
    return jax.ShapeDtypeStruct((tok + 3 * PIECE_ROWS, HEAD_DIM), jnp.bfloat16)


def own_part(m_ref, a_ref, rows):
    return m_ref[rows, :], a_ref[rows, :HEAD_DIM], a_ref[rows, HEAD_DIM:]


def pack_state(out_ref, m, num, den):
    some = den > 0.0
    safe = jnp.where(some, den, 1.0)
    pack(out_ref, num / safe, jnp.where(some, m + jnp.log2(safe), START))


def mix(m, num, den, out, log_sum):
    top = jnp.maximum(m, log_sum)
    here = jnp.exp2(m - top)
    there = jnp.exp2(log_sum - top)
    return top, num * here + out * there, den * here + there * (log_sum > 0.5 * START)


def leave_kernel(tok, part, m_ref, a_ref, out_ref):
    pack_state(out_ref, *own_part(m_ref, a_ref, slice(part * tok, (part + 1) * tok)))


def pass_on_kernel(tok, part, rows, m_ref, a_ref, other, out_ref):
    state = own_part(m_ref, a_ref, slice(part * tok + rows.start, part * tok + rows.stop))
    pack_state(out_ref, *mix(*state, *unpack(other, rows)))


def join_kernel(rows, m_ref, a_ref, other, back, out_ref):
    state = mix(*own_part(m_ref, a_ref, rows), *unpack(other, rows))
    _, num, den = mix(*state, *unpack(back, slice(0, rows.stop - rows.start)))
    out_ref[...] = (num / den).astype(jnp.bfloat16)


def small_call(kernel, name, out_shape, *args):
    return pl.pallas_call(
        kernel,
        out_shape=out_shape,
        in_specs=[vmem_spec()] * len(args),
        out_specs=vmem_spec(),
        compiler_params=pltpu.CompilerParams(vmem_limit_bytes=VMEM_LIMIT),
        name=name,
    )(*args)


PROJECT_STEPS = 3


def project_kernel(row_block, heads, own, left, right, far, weight, *refs):
    out_ref, lhs, result, done = refs[-4:]
    h = heads[0]
    count = weight.shape[0] // HEAD_DIM
    rows, width = result.shape[0], result.shape[1] // PROJECT_STEPS
    for by, piece in ((0, own), (count - 1, left), (1, right), (2, far)):
        column = pl.multiple_of(lax.rem(h + by, count) * HEAD_DIM, HEAD_DIM)
        lhs[:, pl.ds(column, HEAD_DIM)] = piece[...]
    copies = []
    for step in range(PROJECT_STEPS):
        columns = pl.ds(step * width, width)
        result[:, columns] = jnp.dot(
            lhs[...], weight[:, columns], preferred_element_type=jnp.float32
        ).astype(jnp.bfloat16)
        copies.append(
            pltpu.make_async_copy(
                result.at[:, columns],
                out_ref.at[pl.ds(row_block * rows, rows), columns],
                done.at[step],
            )
        )
        copies[-1].start()
    for copy in copies:
        copy.wait()


def project(heads, pieces, weight, tok, before):
    rows = pieces[0].shape[0]
    return pl.pallas_call(
        functools.partial(project_kernel, 0 if before is None else 1),
        out_shape=jax.ShapeDtypeStruct((tok, weight.shape[1]), jnp.bfloat16),
        in_specs=[smem_spec()]
        + [vmem_spec()] * 5
        + ([] if before is None else [pl.BlockSpec(memory_space=pl.ANY)]),
        out_specs=pl.BlockSpec(memory_space=pl.ANY),
        scratch_shapes=[
            pltpu.VMEM((rows, weight.shape[0]), jnp.bfloat16),
            pltpu.VMEM((rows, weight.shape[1]), jnp.bfloat16),
            pltpu.SemaphoreType.DMA((PROJECT_STEPS,)),
        ],
        input_output_aliases={} if before is None else {6: 0},
        compiler_params=pltpu.CompilerParams(vmem_limit_bytes=VMEM_LIMIT),
        cost_estimate=pl.CostEstimate(
            flops=2 * rows * weight.shape[0] * weight.shape[1],
            bytes_accessed=2 * rows * weight.shape[1],
            transcendentals=0,
        ),
        name="project",
    )(heads, *pieces, weight, *([] if before is None else [before]))


def shards(queries, key_states, value_states, clip_lengths, out_weight):
    tok = queries.shape[0]
    blocks = tok // BLOCK
    ctx_count = lax.axis_size("ctx")
    head_count = lax.axis_size("head")
    ring = 2 * RING_CHIPS
    me = lax.axis_index("ctx")
    core = me % 2
    first_of_ring = me // ring * ring
    place = (me % ring) // 2
    head = lax.axis_index("head")

    def send(value, target):
        return lax.ppermute(value, "ctx", [(i, target(i)) for i in range(ctx_count)])

    def sibling(i):
        return i ^ 1

    def along(i):
        at = i % ring
        by = 2 if i % 2 == 0 else -2
        return i - at + (at + by) % ring

    def after(value, state):
        value, m = lax.optimization_barrier((value, state[0]))
        return value, (m, state[1])

    def up(i):
        return (i + ring) % ctx_count

    def down(i):
        return (i - ring) % ctx_count

    def turn(value, by):
        pairs = [(i, (i + by) % head_count) for i in range(head_count)]
        return lax.ppermute(value, "head", pairs)

    upto = jnp.arange(clip_lengths.shape[0])
    ends = jnp.sum(jnp.where(upto[None, :] <= upto[:, None], clip_lengths[None, :], 0), axis=1)
    owners = jnp.stack([me, me ^ 1, (me + ring) % ctx_count, ((me + ring) % ctx_count) ^ 1])
    bases = owners * blocks
    q_blocks = bases[:, None] + jnp.arange(blocks, dtype=jnp.int32)[None, :]
    begin = jnp.max(
        jnp.where(ends[None, None, :] <= q_blocks[:, :, None], ends[None, None, :], 0), axis=-1
    )
    info = jnp.concatenate([bases, begin.reshape(-1)]).astype(jnp.int32)

    kv = jnp.stack([key_states, value_states])
    near = send(kv, along)
    kv, info = lax.optimization_barrier((kv, info))
    cross = send(kv, lambda i: along(sibling(i)))
    next_own = send(queries, down)
    q_sibling = send(queries, sibling)

    def base_of(step, of_core):
        chip = (place + jnp.where(core == 0, -step, step)) % RING_CHIPS
        return ((first_of_ring + 2 * chip + of_core) * blocks).reshape(1).astype(jnp.int32)

    order = []
    for step in range(1, RING_CHIPS // 2 + 1):
        order += [(step, core), (step, 1 - core)]
    order = order[:-1]
    arrived = [near, cross]
    everyone = (0, 1, 2, 3)
    own_base = base_of(0, core)
    state = fold(info, own_base, (queries,), (0,), kv, None, 4)
    state = fold(info, own_base, (queries, q_sibling), (1,), kv, state, 4)
    q_parts = (queries, q_sibling, next_own, send(queries, lambda i: sibling(down(i))))
    for n, (step, of_core) in enumerate(order):
        value = arrived[n]
        if n + 2 < len(order):
            if n != 1:
                value, state = after(value, state)
            arrived.append(send(value, along))
        if n == len(order) - 1:
            state = fold(info, own_base, q_parts, (2, 3), kv, state)
        state = fold(
            info, base_of(step, of_core), q_parts, everyone, value, state, 46 if n else 8
        )

    packed = packed_shape(tok)
    half = tok // 2
    halves = (slice(0, half), slice(half, tok))
    leave = functools.partial(leave_kernel, tok)
    next_there = send(small_call(functools.partial(leave, 3), "leave_next", packed, *state), sibling)
    own_there = send(small_call(functools.partial(leave, 1), "leave_own", packed, *state), sibling)
    back = [
        send(
            small_call(
                functools.partial(pass_on_kernel, tok, 2, rows),
                "pass_on",
                packed_shape(half),
                *state,
                next_there,
            ),
            up,
        )
        for rows in halves
    ]
    pieces = []
    for rows, returned in zip(halves, back):
        attended = small_call(
            functools.partial(join_kernel, rows),
            "join",
            jax.ShapeDtypeStruct((half, HEAD_DIM), jnp.bfloat16),
            *state,
            own_there,
            returned,
        )
        pieces.append(
            (
                attended,
                turn(attended, 1),
                turn(attended, -1),
                turn(attended, 2),
            )
        )
    heads = head.reshape(1).astype(jnp.int32)
    first = project(heads, pieces[0], out_weight, tok, None)
    return project(heads, pieces[1], out_weight, tok, first)


def solution(mesh):
    placed = (P("ctx", "head"), P("ctx", "head"), P("ctx", "head"), P(), P(None, "head"))
    return jax.shard_map(
        shards, mesh=mesh, in_specs=placed, out_specs=P("ctx", "head"), check_vma=False
    )
```
